32 devices in a mesh: fsdp: 4 (over y, x), dp: 8 (over z, core).
Axes of the slice: x: 2, y: 2, z: 4, core: 2. Of those that a mesh axis runs over, the one named last changes fastest.
Arguments:
- tokens: bfloat16 [32768, 1024], P(('fsdp', 'dp')), may hold values from -6 to 6
- clip_frames: int32 [32, 4], P(('fsdp', 'dp')), may hold values from 0 to 3, as said below
- clip_patches: int32 [32, 4], P(('fsdp', 'dp')), may hold values from 256 to 576, as said below
- qkv_weight: bfloat16 [1024, 3072], P(('fsdp', 'dp')), may hold values from -0.1875 to 0.1875
- qkv_bias: bfloat16 [3072], P(('fsdp', 'dp')), may hold values from -3 to 3
- out_weight: bfloat16 [1024, 1024], P(('fsdp', 'dp')), may hold values from -1.5 to 1.5
- out_bias: bfloat16 [1024], P(('fsdp', 'dp')), may hold values from -2 to 2
- up_weight: bfloat16 [1024, 4096], P(('fsdp', 'dp')), may hold values from -0.1875 to 0.1875
- up_bias: bfloat16 [4096], P(('fsdp', 'dp')), may hold values from -3 to 3
- down_weight: bfloat16 [4096, 1024], P(('fsdp', 'dp')), may hold values from -0.09375 to 0.09375
- down_bias: bfloat16 [1024], P(('fsdp', 'dp')), may hold values from -2 to 2
- norm1_gain: bfloat16 [1024], P(('fsdp', 'dp')), may hold values from 0.099609375 to 1.8984375
- norm1_shift: bfloat16 [1024], P(('fsdp', 'dp')), may hold values from -2 to 2
- norm2_gain: bfloat16 [1024], P(('fsdp', 'dp')), may hold values from 0.099609375 to 1.8984375
- norm2_shift: bfloat16 [1024], P(('fsdp', 'dp')), may hold values from -2 to 2
- cotangent: bfloat16 [32768, 1024], P(('fsdp', 'dp')), may hold values from -6 to 6
Outputs:
- output: bfloat16 [32768, 1024], P(('fsdp', 'dp'))
- grad_tokens: bfloat16 [32768, 1024], P(('fsdp', 'dp'))
- grad_qkv_weight: float32 [1024, 3072], P(('fsdp', 'dp'))
- grad_qkv_bias: float32 [3072], P(('fsdp', 'dp'))
- grad_out_weight: float32 [1024, 1024], P(('fsdp', 'dp'))
- grad_out_bias: float32 [1024], P(('fsdp', 'dp'))
- grad_up_weight: float32 [1024, 4096], P(('fsdp', 'dp'))
- grad_up_bias: float32 [4096], P(('fsdp', 'dp'))
- grad_down_weight: float32 [4096, 1024], P(('fsdp', 'dp'))
- grad_down_bias: float32 [1024], P(('fsdp', 'dp'))
- grad_norm1_gain: float32 [1024], P(('fsdp', 'dp'))
- grad_norm1_shift: float32 [1024], P(('fsdp', 'dp'))
- grad_norm2_gain: float32 [1024], P(('fsdp', 'dp'))
- grad_norm2_shift: float32 [1024], P(('fsdp', 'dp'))
The draws below stay inside these ranges and needn't reach their ends.
Inputs may be any that keep to these rules, and one draw needn't show every extreme that they name: `clip_frames`: per device, the slots' frames times (patches + 2) add up to at most 1024; 0 marks an empty slot, every device has a clip in slot 0. `clip_patches`: each entry is 256 or 576.
All inputs are finite; a program needn't handle non-finite values.
Results may differ from the reference program's by a relative error of at most 0.0077.
Values may be sent and summed in bfloat16 or wider, within the bound.
No kernel may reach another device: no remote copies, remote signals or barrier semaphores. Data moves between devices by JAX's collectives and lax.ppermute only.
A program may use at most 256 MiB of HBM per device.

```python
import jax
import jax.numpy as jnp
import numpy as np
from jax import lax

D = 1024
HEADS = 16
HEAD = 64
FF = 4096
SIDE_SMALL = 16
SIDE_LARGE = 24
CLIPS_DEV = 4
TOK_DEV = 1024
TOKENS = 32768
DEVICES = 32


def clip_plan(base_key):
    small_tokens = SIDE_SMALL * SIDE_SMALL + 2
    large_tokens = SIDE_LARGE * SIDE_LARGE + 2
    most_frames = TOK_DEV // small_tokens
    kind_key, long_key, pick_key, other_key = jax.random.split(base_key, 4)
    kinds = jax.random.randint(kind_key, (DEVICES, CLIPS_DEV), 0, 2)
    lengths = jax.random.randint(long_key, (DEVICES, CLIPS_DEV), 0, 4)
    first_dev = jax.random.randint(pick_key, (), 0, DEVICES)
    second_dev = (first_dev + 1 + jax.random.randint(other_key, (), 0, DEVICES - 1)) % DEVICES
    device_ids = jnp.arange(DEVICES)
    kinds = kinds.at[:, 0].set(jnp.where(device_ids == first_dev, 0, jnp.where(device_ids == second_dev, 1, kinds[:, 0])))
    lengths = lengths.at[:, 0].set(jnp.where(device_ids == first_dev, 0, jnp.where(device_ids == second_dev, 1, lengths[:, 0])))
    wanted = jnp.where(lengths == 0, most_frames, 1 + lengths // 3)
    used = jnp.zeros((DEVICES,), jnp.int32)
    columns = []
    for slot in range(CLIPS_DEV):
        per_frame = jnp.where(kinds[:, slot] == 0, small_tokens, large_tokens)
        room = (TOK_DEV - used) // per_frame
        placed = jnp.minimum(wanted[:, slot], room)
        used = used + placed * per_frame
        columns.append(placed)
    frames = jnp.stack(columns, axis=1).astype(jnp.int32)
    patches = jnp.where(kinds == 0, SIDE_SMALL * SIDE_SMALL, SIDE_LARGE * SIDE_LARGE).astype(jnp.int32)
    return (frames, patches)


def draw_clip_frames(key, part):
    frames, patches = clip_plan(key)
    return frames


def draw_clip_patches(key, part):
    frames, patches = clip_plan(key)
    return patches


def with_spikes(entries, key, source, target, parts, factor):
    def block_of(axis_at):
        return (jnp.arange(entries.shape[axis_at]) // (entries.shape[axis_at] // parts)).reshape((-1,) + (1,) * (entries.ndim - 1 - axis_at))

    first = jax.random.permutation(key, parts)[block_of(target)]
    second = (block_of(target) + parts // 2) % parts
    return jnp.where((block_of(source) == first) | (block_of(source) == second), factor * entries, entries)


def level_of(rng, shape, cuts, low, largest):
    factor_of, own = 1.0, jax.random.fold_in(rng, 6)
    for axis_at, blocks in cuts:
        draws = jnp.exp(jax.random.uniform(jax.random.fold_in(own, axis_at), (blocks,), jnp.float32, low / len(cuts), largest / len(cuts)))
        factor_of = factor_of * jnp.repeat(draws, shape[axis_at] // blocks).reshape([-1 if axis == axis_at else 1 for axis in range(len(shape))])
    return factor_of


def scatter_about(stream_key, dims, spread, most, cuts=(), kind=jnp.bfloat16):
    level = level_of(stream_key, dims, cuts, -0.22, 0.18) if cuts else 1.0
    values = jax.random.normal(stream_key, dims, jnp.float32) * spread * level
    return jnp.minimum(jnp.maximum(values, -most), most).astype(kind)


def gaussian_with(own_key, shape, scale, most, cuts, heavy, kind=jnp.bfloat16):
    values = scale * jax.random.normal(own_key, shape, jnp.float32)
    if cuts:
        values = values * level_of(own_key, shape, cuts, -0.22, 0.18)
    return jnp.clip(with_spikes(values, jax.random.fold_in(own_key, 3), *heavy), -most, most).astype(kind)


def setup_inputs(seed: int = 0) -> dict:
    streams_of = jax.random.split(jax.random.key(seed), 17)
    tokens = scatter_about(streams_of[0], (TOKENS, D), 1.0, 6.0, ((0, 32),))
    clip_frames = draw_clip_frames(jax.random.fold_in(streams_of[16], 71), 0)
    clip_patches = draw_clip_patches(jax.random.fold_in(streams_of[16], 71), 0)
    qkv_weight = scatter_about(streams_of[3], (D, 3 * D), D ** -0.5, 0.1875, ((0, 32),))
    qkv_bias = scatter_about(streams_of[4], (3 * D,), 0.5, 3.0, ((0, 32),))
    out_weight = scatter_about(streams_of[5], (D, D), (D // 64) ** -0.5, 1.5, ((0, 32),))
    out_bias = scatter_about(streams_of[6], (D,), 0.3, 2.0, ((0, 32),))
    up_weight = scatter_about(streams_of[7], (D, FF), D ** -0.5, 0.1875, ((0, 32),))
    up_bias = scatter_about(streams_of[8], (FF,), 0.5, 3.0, ((0, 32),))
    down_weight = scatter_about(streams_of[9], (FF, D), FF ** -0.5, 0.09375, ((0, 32),))
    down_bias = scatter_about(streams_of[10], (D,), 0.3, 2.0, ((0, 32),))
    norm1_gain = jnp.clip(1.0 + 0.18 * jax.random.normal(streams_of[11], (D,), jnp.float32), 0.099609375, 1.8984375).astype(jnp.bfloat16)
    norm1_shift = scatter_about(streams_of[12], (D,), 0.3, 2.0, ((0, 32),))
    norm2_gain = jnp.clip(1.0 + 0.18 * jax.random.normal(streams_of[13], (D,), jnp.float32), 0.099609375, 1.8984375).astype(jnp.bfloat16)
    norm2_shift = scatter_about(streams_of[14], (D,), 0.3, 2.0, ((0, 32),))
    cotangent = gaussian_with(streams_of[15], (TOKENS, D), 1.0, 6.0, ((0, 32),), (0, 1, 32, 2.75))
    return {"tokens": tokens, "clip_frames": clip_frames, "clip_patches": clip_patches, "qkv_weight": qkv_weight, "qkv_bias": qkv_bias, "out_weight": out_weight, "out_bias": out_bias, "up_weight": up_weight, "up_bias": up_bias, "down_weight": down_weight, "down_bias": down_bias, "norm1_gain": norm1_gain, "norm1_shift": norm1_shift, "norm2_gain": norm2_gain, "norm2_shift": norm2_shift, "cotangent": cotangent}


@jax.custom_vjp
def low(v):
    return lax.optimization_barrier(v.astype(jnp.bfloat16)).astype(jnp.float32)

@jax.custom_vjp
def low_back(v):
    return v

def low_keep(v):
    return (low(v), None)

def low_pass(kept, grad):
    return (grad,)

def back_keep(v):
    return (v, None)

def back_low(kept, grad):
    return (low(grad),)
low.defvjp(low_keep, low_pass)
low_back.defvjp(back_keep, back_low)
EPSILON = 1e-06
MASKED = -1e+30
HIGHEST = lax.Precision.HIGHEST

def product(left, right):
    return jnp.dot(left, right, precision=HIGHEST, preferred_element_type=jnp.float32)

def layout(frames, patches):
    frame_tokens = (patches + 2).astype(jnp.int32)
    clip_tokens = (frames * frame_tokens).astype(jnp.int32)
    clip_starts = (jnp.cumsum(clip_tokens) - clip_tokens).astype(jnp.int32)
    positions = jnp.arange(TOK_DEV, dtype=jnp.int32)
    inside = ((positions[None, :] >= clip_starts[:, None]) & (positions[None, :] < (clip_starts + clip_tokens)[:, None])).astype(jnp.int32)
    slot_ids = jnp.arange(frames.shape[0], dtype=jnp.int32)
    present = lax.optimization_barrier(jnp.sum(inside, axis=0)).astype(jnp.int32) > 0
    segment = jnp.where(present, lax.optimization_barrier(jnp.sum(inside * slot_ids[:, None], axis=0)).astype(jnp.int32), -1).astype(jnp.int32)
    begins = lax.optimization_barrier(jnp.sum(inside * clip_starts[:, None], axis=0)).astype(jnp.int32)
    widths = jnp.maximum(lax.optimization_barrier(jnp.sum(inside * frame_tokens[:, None], axis=0)).astype(jnp.int32), 1)
    clip_sides = jnp.where(patches == SIDE_SMALL * SIDE_SMALL, SIDE_SMALL, SIDE_LARGE).astype(jnp.int32)
    sides_rows = jnp.maximum(lax.optimization_barrier(jnp.sum(inside * clip_sides[:, None], axis=0)).astype(jnp.int32), 1)
    offsets = (positions - begins).astype(jnp.int32)
    frame_index = (offsets // widths).astype(jnp.int32)
    within = (offsets % widths).astype(jnp.int32)
    patch_index = jnp.maximum(within - 2, 0).astype(jnp.int32)
    row_index = jnp.where(within >= 2, patch_index // sides_rows, 0).astype(jnp.int32)
    col_index = jnp.where(within >= 2, patch_index % sides_rows, 0).astype(jnp.int32)
    return (segment, frame_index, row_index, col_index)

def rotary_tables(frame_index, row_index, col_index):
    pair_count = HEAD // 2
    time_pairs = pair_count // 3
    row_pairs = (pair_count - time_pairs) // 2
    pair_ranks = np.arange(pair_count)
    group_ids = np.where(pair_ranks < time_pairs, 0, np.where(pair_ranks < time_pairs + row_pairs, 1, 2))
    group_first = np.array([0, time_pairs, time_pairs + row_pairs])[group_ids]
    group_sizes = np.array([time_pairs, row_pairs, pair_count - time_pairs - row_pairs])[group_ids]
    rate_table = 10000.0 ** (-(pair_ranks - group_first) / group_sizes)
    angles = jnp.zeros((TOK_DEV, pair_count), jnp.float32)
    for group_id, place in enumerate((frame_index, row_index, col_index)):
        table = jnp.asarray(np.where(group_ids == group_id, rate_table, 0.0), jnp.float32)
        angles = angles + place.astype(jnp.float32)[:, None] * table[None, :]
    return (jnp.cos(angles), jnp.sin(angles))

def rotate(inputs, cosine, sine):
    half_size = inputs.shape[-1] // 2
    first_half = inputs[..., :half_size]
    second_half = inputs[..., half_size:]
    cos_rows = cosine[:, None, :]
    sin_rows = sine[:, None, :]
    return jnp.concatenate([first_half * cos_rows - second_half * sin_rows, second_half * cos_rows + first_half * sin_rows], axis=-1)

def layer_norm(inputs, gain, shift):
    average = lax.optimization_barrier(jnp.mean(inputs, axis=-1, keepdims=True))
    centred = inputs - average
    variance = lax.optimization_barrier(jnp.mean(centred * centred, axis=-1, keepdims=True))
    return centred * lax.rsqrt(variance + EPSILON) * gain + shift

def allowed(begin, row_count, segment, frame_index):
    positions = jnp.arange(TOK_DEV, dtype=jnp.int32)
    row_ids = begin + jnp.arange(row_count, dtype=jnp.int32)
    row_segment = lax.dynamic_slice_in_dim(segment, begin, row_count, 0)
    row_frame = lax.dynamic_slice_in_dim(frame_index, begin, row_count, 0)
    same_clip = (row_segment[:, None] == segment[None, :]) & (row_segment[:, None] >= 0) & (frame_index[None, :] <= row_frame[:, None])
    return same_clip | (row_ids[:, None] == positions[None, :])

def head_attention(queries, keys_rot, values_in, segment, frame_index):
    row_count = min(512, TOK_DEV)

    def one_block(number):
        begin = (number * row_count).astype(jnp.int32)
        block_rows = lax.dynamic_slice_in_dim(queries, begin, row_count, 0)
        scores = product(block_rows, keys_rot.T) * HEAD ** (-0.5)
        scores = jnp.where(allowed(begin, row_count, segment, frame_index), scores, MASKED)
        scores = low_back(scores)
        highest = lax.optimization_barrier(jnp.max(scores, axis=1, keepdims=True))
        expo = jnp.exp(scores - highest)
        probs = expo / lax.optimization_barrier(jnp.sum(expo, axis=1, keepdims=True))
        return product(low(probs), values_in)
    blocks = lax.map(jax.checkpoint(one_block), jnp.arange(TOK_DEV // row_count, dtype=jnp.int32))
    return blocks.reshape(TOK_DEV, HEAD)

def layer(inputs, qkv_weight, qkv_bias, out_weight, out_bias, up_weight, up_bias, down_weight, down_bias, norm1_gain, norm1_shift, norm2_gain, norm2_shift, segment, frame_index, cosine, sine):
    normed_one = low(layer_norm(inputs, norm1_gain, norm1_shift))
    projected = low_back(product(normed_one, qkv_weight) + qkv_bias).reshape(TOK_DEV, 3, HEADS, HEAD)
    queries = low(rotate(projected[:, 0], cosine, sine))
    keys_rot = low(rotate(projected[:, 1], cosine, sine))
    values_in = low(projected[:, 2])

    def per_head(item):
        return head_attention(item[0], item[1], item[2], segment, frame_index)
    heads = lax.map(per_head, (queries.transpose(1, 0, 2), keys_rot.transpose(1, 0, 2), values_in.transpose(1, 0, 2)))
    mixed = low(low_back(heads.transpose(1, 0, 2).reshape(TOK_DEV, D)))
    resid = inputs + low_back(product(mixed, out_weight) + out_bias)
    normed_two = low(layer_norm(resid, norm2_gain, norm2_shift))
    pre_act = low_back(product(normed_two, up_weight) + up_bias)
    activ = low(jax.nn.gelu(pre_act, approximate=False))
    return resid + low_back(product(activ, down_weight) + down_bias)

def reference(tokens, clip_frames, clip_patches, qkv_weight, qkv_bias, out_weight, out_bias, up_weight, up_bias, down_weight, down_bias, norm1_gain, norm1_shift, norm2_gain, norm2_shift, cotangent):
    params = tuple((item.astype(jnp.float32) for item in (qkv_weight, qkv_bias, out_weight, out_bias, up_weight, up_bias, down_weight, down_bias, norm1_gain, norm1_shift, norm2_gain, norm2_shift)))
    inputs_all = tokens.astype(jnp.float32).reshape(DEVICES, TOK_DEV, D)
    cot_all = cotangent.astype(jnp.float32).reshape(DEVICES, TOK_DEV, D)

    def step(carry, item):
        inputs, cot_rows, frames, patches = item
        segment, frame_index, row_index, col_index = layout(frames, patches)
        cosine, sine = rotary_tables(frame_index, row_index, col_index)

        def forward(inputs_in, *weights):
            return layer(inputs_in, *weights, segment, frame_index, cosine, sine)
        result, pull = jax.vjp(forward, inputs, *params)
        grads = pull(cot_rows)
        summed = tuple((total + grad for total, grad in zip(carry, grads[1:])))
        return (summed, (result.astype(jnp.bfloat16), grads[0].astype(jnp.bfloat16)))
    start = tuple((jnp.zeros(item.shape, jnp.float32) for item in params))
    sums, (outputs, grad_inputs) = lax.scan(step, start, (inputs_all, cot_all, clip_frames, clip_patches))
    return (outputs.reshape(TOKENS, D), grad_inputs.reshape(TOKENS, D), sums[0], sums[1], sums[2], sums[3], sums[4], sums[5], sums[6], sums[7], sums[8], sums[9], sums[10], sums[11])
```

```python
import functools

import jax
import jax.numpy as jnp
import numpy as np
from jax import lax
from jax.experimental import pallas as pl
from jax.experimental.pallas import tpu as pltpu
from jax.sharding import PartitionSpec as P

D = 1024
HEADS = 16
HEAD = 64
FF = 4096
SIDE_SMALL = 16
SIDE_LARGE = 24
TOK_DEV = 1024
AXES = ("fsdp", "dp")
EPSILON = 1e-06
MASKED = -1e30
BQ = 256
BK = 128
LANES = 128
TILE = 512
ROWS = 256
F32 = jnp.float32
BF = jnp.bfloat16
VMEM_BYTES = 56 << 20
WEIGHT = 1.15e10


def cost(microseconds):
    return pl.CostEstimate(flops=int(microseconds * WEIGHT), bytes_accessed=0, transcendentals=0)


def nt(left, right):
    return lax.dot_general(left, right, (((1,), (1,)), ((), ())), preferred_element_type=F32)


def nn(left, right):
    return jnp.dot(left, right, preferred_element_type=F32)


SMEM = pl.BlockSpec(memory_space=pltpu.SMEM)
ANY = pl.BlockSpec(memory_space=pl.ANY)


def fixed(*shape):
    return pl.BlockSpec(shape, lambda *_: (0,) * len(shape))


def pallas(kernel, operands, in_specs, after=(), **kept):
    given = len(operands)

    def body(*refs):
        kernel(*refs[:given], *refs[given + len(after) :])

    return pl.pallas_call(
        body,
        in_specs=list(in_specs) + [ANY] * len(after),
        compiler_params=pltpu.CompilerParams(vmem_limit_bytes=VMEM_BYTES),
        **kept,
    )(*operands, *after)


class Relay:
    def __init__(self):
        self.inputs, self.outs, self.jobs = [], [], []

    def take(self, array):
        for place, known in enumerate(self.inputs):
            if known is array:
                return place
        self.inputs.append(array)
        return len(self.inputs) - 1

    def make(self, rows, columns, dtype):
        self.outs.append(((rows, columns), dtype))
        return len(self.outs) - 1

    def put(self, out, row, column, rows, columns, terms):
        self.jobs.append((out, row, column, rows, columns, [(self.take(array), *at) for array, *at in terms]))

    def run(self, after=(), name="relay"):
        jobs, given = self.jobs, len(self.inputs)

        def kernel(*refs):
            sources, targets = refs[:given], refs[given:]
            for out, row, column, rows, columns, terms in jobs:
                step = next(size for size in (64, 32, 16) if rows % size == 0)

                @pl.loop(0, rows // step)
                def _(index):
                    def part(ref, row, column):
                        begin = pl.multiple_of(row + index * step, 16)
                        return ref.at[pl.ds(begin, step), column : column + columns]

                    total = part(sources[terms[0][0]], *terms[0][1:])[...]
                    for source, *at in terms[1:]:
                        total = total.astype(F32) + part(sources[source], *at)[...].astype(F32)
                    part(targets[out], row, column)[...] = total.astype(targets[out].dtype)

        moved = sum(2 * shape[0] * shape[1] * 3 for shape, _ in self.outs)
        return pallas(
            kernel,
            self.inputs,
            [fixed(*array.shape) for array in self.inputs],
            after,
            out_specs=[fixed(*shape) for shape, _ in self.outs],
            out_shape=[jax.ShapeDtypeStruct(shape, dtype) for shape, dtype in self.outs],
            cost_estimate=cost(1 + moved * 0.4e-6),
            name=name,
        )


BLOCKS = 32
UPPER = ((16, 8), (8, 16))


class Net:
    def __init__(self, count):
        self.count, self.share = count, max(count // BLOCKS, 1)
        self.number = lax.axis_index(AXES).astype(jnp.int32)
        self.me = self.number // self.share

    def swap(self, value, mask):
        return self.permute(value, mask * self.share)

    def permute(self, value, mask):
        return lax.ppermute(value, AXES, [(number, number ^ mask) for number in range(self.count)])

    def bits(self):
        return [1 << place for place in range(self.share.bit_length() - 1)]

    def widen(self, shard):
        for bit in self.bits():
            other = self.permute(shard, bit)
            shard = jnp.where(
                self.number & bit, jnp.concatenate([other, shard], 0), jnp.concatenate([shard, other], 0)
            )
        return shard

    def narrow(self, total):
        for bit in self.bits()[::-1]:
            low, high = jnp.split(total, 2, 0)
            own = jnp.where(self.number & bit, high, low)
            total = own + self.permute(jnp.where(self.number & bit, low, high), bit)
        return total

    def over_all(self, value):
        for place in range(self.count.bit_length() - 1):
            value = value + self.permute(value, 1 << place)
        return value


def runs_of(places):
    runs = []
    for position, place in enumerate(places):
        if runs and runs[-1][1] + runs[-1][2] == place:
            runs[-1][2] += 1
        else:
            runs.append([position, place, 1])
    return runs


def parted(places, mask):
    return [[position for position, place in enumerate(places) if bool(place & mask) == with_it] for with_it in (False, True)]


class Gather:
    def __init__(self, net, shard):
        self.net, self.rows, self.half = net, shard.shape[0], shard.shape[1] // 2
        self.blocks = [[0]] * 2
        self.stage = 0
        self.held = [(shard, net.swap(shard, 2))]

    def join(self, relay):
        rows, half = self.rows, self.half
        self.made = []
        if self.stage == 0:
            self.made.append(relay.make(2 * rows, 2 * half, BF))
            for place, array in enumerate(self.held[0]):
                relay.put(self.made[0], place * rows, 0, rows, 2 * half, [(array, 0, 0)])
            self.blocks = [[0, 2]] * 2
        elif self.stage == 1:
            for side in range(2):
                self.made.append(relay.make(4 * rows, half, BF))
                for place, array in enumerate(self.held[0]):
                    relay.put(self.made[side], 2 * place * rows, 0, 2 * rows, half, [(array, 0, side * half)])
            self.blocks = [[0, 2, 4, 6]] * 2
        elif self.stage == 2:
            for side in range(2):
                self.made.append(relay.make(8 * rows, half, BF))
                for place, array in enumerate(self.held[side]):
                    relay.put(self.made[side], 4 * place * rows, 0, 4 * rows, half, [(array, 0, 0)])
                self.blocks[side] = self.blocks[side] + [block ^ UPPER[side][0] for block in self.blocks[side]]

    def follow(self, made):
        arrays = [made[place] for place in self.made]
        self.stage += 1
        if self.stage == 1:
            self.held = [(arrays[0], self.net.swap(arrays[0], 4))]
            return
        self.held = [(array, self.net.swap(array, UPPER[side][self.stage - 2])) for side, array in enumerate(arrays)]
        if self.stage == 3:
            self.pieces = []
            for side in range(2):
                own, come = self.held[side]
                blocks = self.blocks[side]
                others = [block ^ UPPER[side][1] for block in blocks]
                for here, array in ((blocks, own), (others, come)):
                    self.pieces += [(side, here, array), (side, [block ^ 1 for block in here], self.net.swap(array, 1))]

    def arrivals(self):
        return [come for _, come in self.held]


class Scatter:
    def __init__(self, net, sides):
        self.net = net
        self.stage = 0
        self.half = sides[0][0].shape[1]
        self.rows = sides[0][0].shape[0] // 8
        self.held = [(stays, net.swap(leaves, UPPER[side][0])) for side, (stays, leaves) in enumerate(sides)]

    def join(self, relay):
        rows, half = self.rows, self.half
        self.made = []
        if self.stage == 0:
            for side, (own, come) in enumerate(self.held):
                for leaving in range(2):
                    self.made.append(relay.make(4 * rows, half, BF if leaving else F32))
                    first = 4 * rows * leaving
                    relay.put(self.made[-1], 0, 0, 4 * rows, half, [(own, first, 0), (come, first, 0)])
        elif self.stage == 1:
            for leaving in range(2):
                self.made.append(relay.make(2 * rows, 2 * half, BF if leaving else F32))
                first = 2 * rows * leaving
                for side, (own, come) in enumerate(self.held):
                    relay.put(self.made[-1], 0, side * half, 2 * rows, half, [(own, first, 0), (come, first, 0)])
        elif self.stage == 2:
            own, come = self.held[0]
            for leaving in range(2):
                self.made.append(relay.make(rows, 2 * half, BF if leaving else F32))
                first = rows * leaving
                relay.put(self.made[-1], 0, 0, rows, 2 * half, [(own, first, 0), (come, first, 0)])

    def follow(self, made):
        arrays = [made[place] for place in self.made]
        self.stage += 1
        if self.stage == 1:
            self.held = [(arrays[2 * side], self.net.swap(arrays[2 * side + 1], UPPER[side][1])) for side in range(2)]
        elif self.stage == 2:
            self.held = [(arrays[0], self.net.swap(arrays[1], 4))]
        else:
            self.result = self.net.narrow(arrays[0] + self.net.swap(arrays[1], 2).astype(F32))


class Sum:
    def __init__(self, net, value):
        self.net, self.value, self.stage = net, value, 0
        self.send()

    def send(self):
        self.come = self.net.permute(self.value, 1 << self.stage)

    def join(self, relay):
        self.made = relay.make(*self.value.shape, self.value.dtype)
        relay.put(self.made, 0, 0, *self.value.shape, [(self.value, 0, 0), (self.come, 0, 0)])

    def follow(self, made):
        self.value = made[self.made]
        self.stage += 1
        self.send()

    def finish(self):
        for place in range(self.stage + 1, self.net.count.bit_length()):
            self.value = self.value + self.come
            if place < self.net.count.bit_length() - 1:
                self.come = self.net.permute(self.value, 1 << place)
        return self.value


def advance(moving, after=(), name="relay", extra=None):
    relay = Relay()
    if extra is not None:
        extra(relay)
    for each in moving:
        each.join(relay)
    made = relay.run(after, name)
    for each in moving:
        each.follow(made)
    return made


def fetch(me, pieces, refs, columns, target, sem):
    first, last = columns
    for (side, blocks, width, rows), ref in zip(pieces, refs):
        begin, end = max(first, side * width), min(last, (side + 1) * width)
        if begin >= end:
            continue
        for place, block in enumerate(blocks):
            row = pl.multiple_of((me ^ block) * rows, rows)
            pltpu.make_async_copy(
                ref.at[pl.ds(place * rows, rows), pl.ds(begin - side * width, end - begin)],
                target.at[pl.ds(row, rows), pl.ds(begin - first, end - begin)],
                sem,
            ).start()


def arrive(target, sem):
    pltpu.make_async_copy(target, target, sem).wait()


def describe(pieces):
    return [(side, tuple(blocks), array.shape[1], array.shape[0] // len(blocks)) for side, blocks, array in pieces]


def normed(inputs):
    average = jnp.mean(inputs, axis=-1, keepdims=True)
    centred = inputs - average
    scale = lax.rsqrt(jnp.mean(centred * centred, axis=-1, keepdims=True) + EPSILON)
    return centred * scale, scale


def norm_back(inputs, gain, upstream):
    unit, scale = normed(inputs)
    scaled = gain * upstream
    back = scale * (
        scaled
        - jnp.mean(scaled, axis=-1, keepdims=True)
        - unit * jnp.mean(scaled * unit, axis=-1, keepdims=True)
    )
    return back, jnp.sum(upstream * unit, axis=0, keepdims=True), jnp.sum(upstream, axis=0, keepdims=True)


def partner(values):
    half = HEAD // 2
    lane = lax.broadcasted_iota(jnp.int32, values.shape, 1)
    return jnp.where(
        lane % HEAD < half,
        pltpu.roll(values, values.shape[1] - half, 1),
        pltpu.roll(values, half, 1),
    )


def wide(table, width):
    return jnp.concatenate([table] * (width // LANES), 1)


def turn_out(me, values, kept, sent):
    turned = values.T
    rows = D // BLOCKS
    for number in range(BLOCKS):
        place = (number ^ me) >> 1
        block = turned[number * rows : (number + 1) * rows, :]
        own = ((number ^ me) & 1) == 0
        begin = pl.multiple_of(place * rows, rows)

        @pl.when(own)
        def _():
            kept[pl.ds(begin, rows), :] = block

        @pl.when(jnp.logical_not(own))
        def _():
            sent[pl.ds(begin, rows), :] = block


LINES = (3, 1, 1, 1, 1, 1, 1, 1)
LENGTHS = (96, 32, 128, 32, 32, 32, 32, 32)
QKV_B, OUT_B, UP_B, DOWN_B, GAIN_ONE, SHIFT_ONE, GAIN_TWO, SHIFT_TWO = 0, 3, 4, 8, 9, 10, 11, 12
TABLE = 16


def lines_of(me, small):
    flat = jnp.zeros((BLOCKS * LANES,), BF)
    line = 0
    for values, lines, length in zip(small, LINES, LENGTHS):
        place = line * LANES + (0 if length == LANES else (me % 4) * length)
        flat = lax.dynamic_update_slice(flat, values, (place,))
        line += lines
    return flat.reshape(BLOCKS, LANES)


def table_of(lines, table):
    row = line = 0
    values = lines.astype(F32)
    table[...] = jnp.zeros_like(table)
    for count, length in zip(LINES, LENGTHS):
        spans = []
        for group in range(BLOCKS // 4):
            blocks = [(4 * group + member) * BLOCKS + line for member in range(4)]
            if length == LANES:
                spans += [values[block : block + 1, :] for block in blocks]
            else:
                for part in range(count):
                    spans.append(sum((values[block + part : block + part + 1, :] for block in blocks[1:]), values[blocks[0] + part : blocks[0] + part + 1, :]))
        for begin in range(0, len(spans), D // LANES):
            table[row : row + 1, :] = jnp.concatenate(spans[begin : begin + D // LANES], 1)
            row += 1
        line += count


def project_kernel(layout_of, me_ref, tokens, cosine, sine, *rest):
    refs = rest[: len(layout_of)]
    normed_kept, normed_sent, qkv_out, table, weight, lines, normed_out, sem, lines_sem = rest[len(layout_of) :]
    step = pl.program_id(0)

    @pl.when(step == 0)
    def _():
        fetch(me_ref[0], layout_of, refs, (3 * D, 3 * D + LANES), lines, lines_sem)
        fetch(me_ref[0], layout_of, refs, (0, 3 * D), weight, sem)
        arrive(lines, lines_sem)
        table_of(lines[...], table)
        gain, shift = table[GAIN_ONE : GAIN_ONE + 1, :], table[SHIFT_ONE : SHIFT_ONE + 1, :]
        for begin in range(0, tokens.shape[0], ROWS):
            part = slice(begin, begin + ROWS)
            unit, _ = normed(tokens[part, :].astype(F32))
            normed_out[part, :] = (unit * gain + shift).astype(BF)
        turn_out(me_ref[0], normed_out[...], normed_kept, normed_sent)
        arrive(weight, sem)

    column = pl.multiple_of(step * TILE, TILE)
    heads_tiles = D // TILE
    bias = table[pl.ds(QKV_B + step // heads_tiles, 1), pl.ds(pl.multiple_of(step % heads_tiles * TILE, TILE), TILE)]

    @pl.when(step < 2 * heads_tiles)
    def _():
        scale = jnp.where(step < heads_tiles, HEAD**-0.5, 1.0).astype(F32)
        for begin in range(0, tokens.shape[0], ROWS):
            part = slice(begin, begin + ROWS)
            product = nn(normed_out[part, :], weight[:, pl.ds(column, TILE)]) + bias
            turned = product * wide(cosine[part, :], TILE) + partner(product) * wide(sine[part, :], TILE)
            qkv_out[part, :] = (turned * scale).astype(BF)

    @pl.when(step >= 2 * heads_tiles)
    def _():
        product = nn(normed_out[...], weight[:, pl.ds(column, TILE)]) + bias
        qkv_out[...] = product.astype(BF)


def project(me, tokens, cosine, sine, pieces, after=()):
    count = tokens.shape[0]
    layout_of = describe(pieces)
    return pallas(
        functools.partial(project_kernel, layout_of),
        grid=(3 * D // TILE,),
        in_specs=[SMEM, fixed(count, D), fixed(count, LANES), fixed(count, LANES)] + [ANY] * len(pieces),
        out_specs=[fixed(D // 2, count)] * 2 + [pl.BlockSpec((count, TILE), lambda step: (0, step)), fixed(TABLE, D)],
        out_shape=[jax.ShapeDtypeStruct((D // 2, count), BF)] * 2
        + [jax.ShapeDtypeStruct((count, 3 * D), BF), jax.ShapeDtypeStruct((TABLE, D), F32)],
        scratch_shapes=[
            pltpu.VMEM((D, 3 * D), BF),
            pltpu.VMEM((D, LANES), BF),
            pltpu.VMEM((count, D), BF),
            pltpu.SemaphoreType.DMA,
            pltpu.SemaphoreType.DMA,
        ],
        cost_estimate=cost(16),
        name="project",
        operands=(me, tokens, cosine, sine, *[array for _, _, array in pieces]),
        after=after,
    )


def line_of(table, line):
    return table[line : line + 1, :]


def branch_kernel(layout_of, me_ref, mixed, tokens, table, *rest):
    refs = rest[: len(layout_of)]
    resid, normed_two, normed_kept, normed_sent, mixed_kept, mixed_sent, weight, sem = rest[len(layout_of) :]

    @pl.when(pl.program_id(0) == 0)
    def _():
        fetch(me_ref[0], layout_of, refs, (0, D), weight, sem)
        arrive(weight, sem)

    value = tokens[...].astype(F32) + (nn(mixed[...], weight[...]) + line_of(table, OUT_B))
    resid[...] = value
    unit, _ = normed(value)
    low = (unit * line_of(table, GAIN_TWO) + line_of(table, SHIFT_TWO)).astype(BF)
    normed_two[...] = low
    turn_out(me_ref[0], low, normed_kept, normed_sent)
    turn_out(me_ref[0], mixed[...], mixed_kept, mixed_sent)


def branch(me, mixed, tokens, table, pieces, after=()):
    count = tokens.shape[0]
    layout_of = describe(pieces)
    rows = pl.BlockSpec((ROWS, D), lambda step: (step, 0))
    return pallas(
        functools.partial(branch_kernel, layout_of),
        grid=(count // ROWS,),
        in_specs=[SMEM, rows, rows, fixed(TABLE, D)] + [ANY] * len(pieces),
        out_specs=[rows, rows] + [pl.BlockSpec((D // 2, ROWS), lambda step: (0, step))] * 4,
        out_shape=[jax.ShapeDtypeStruct((count, D), F32), jax.ShapeDtypeStruct((count, D), BF)]
        + [jax.ShapeDtypeStruct((D // 2, count), BF)] * 4,
        scratch_shapes=[pltpu.VMEM((D, D), BF), pltpu.SemaphoreType.DMA],
        cost_estimate=cost(12),
        name="branch",
            operands=(me, mixed, tokens, table, *[array for _, _, array in pieces],),
        after=after,
    )


def gelu_parts(value):
    decay = jnp.exp(-0.5 * value * value)
    point = 1.0 / (1.0 + (0.3275911 * 2.0**-0.5) * jnp.abs(value))
    series = 0.5 * 1.061405429
    for factor in (-1.453152027, 1.421413741, -0.284496736, 0.254829592):
        series = series * point + 0.5 * factor
    tail = series * point * decay
    return jnp.where(value >= 0, 1.0 - tail, tail), decay * (2.0 * np.pi) ** -0.5


def up_kernel(layout_of, me_ref, normed_two, table, *rest):
    refs = rest[: len(layout_of)]
    activ, slope, activ_kept, activ_sent, weight, sem = rest[len(layout_of) :]
    step = pl.program_id(0)

    @pl.when(step == 0)
    def _():
        fetch(me_ref[0], layout_of, refs, (D, D + FF), weight, sem)
        arrive(weight, sem)

    column = pl.multiple_of(step * TILE, TILE)
    tiles = D // TILE
    bias = table[pl.ds(UP_B + step // tiles, 1), pl.ds(pl.multiple_of(step % tiles * TILE, TILE), TILE)]
    for begin in range(0, normed_two.shape[0], ROWS):
        part = slice(begin, begin + ROWS)
        value = nn(normed_two[part, :], weight[:, pl.ds(column, TILE)]) + bias
        share, density = gelu_parts(value)
        activ[part, :] = (value * share).astype(BF)
        slope[part, :] = (share + value * density).astype(BF)
        turned = activ[part, :].T
        rows = FF // BLOCKS
        parity = me_ref[0] & 1
        for block in range(TILE // rows):
            here = slice(block // 2 * rows, (block // 2 + 1) * rows)

            @pl.when(parity == block % 2)
            def _():
                activ_kept[here, part] = turned[block * rows : (block + 1) * rows, :]

            @pl.when(parity != block % 2)
            def _():
                activ_sent[here, part] = turned[block * rows : (block + 1) * rows, :]


def up(me, normed_two, table, pieces, after=()):
    count = normed_two.shape[0]
    layout_of = describe(pieces)
    tile = pl.BlockSpec((count, TILE), lambda step: (0, step))
    return pallas(
        functools.partial(up_kernel, layout_of),
        grid=(FF // TILE,),
        in_specs=[SMEM, fixed(count, D), fixed(TABLE, D)] + [ANY] * len(pieces),
        out_specs=[tile, tile] + [pl.BlockSpec((TILE // 2, count), lambda step: (step, 0))] * 2,
        out_shape=[jax.ShapeDtypeStruct((count, FF), BF)] * 2 + [jax.ShapeDtypeStruct((FF // 2, count), BF)] * 2,
        scratch_shapes=[pltpu.VMEM((D, FF), BF), pltpu.SemaphoreType.DMA],
        cost_estimate=cost(35),
        name="up",
            operands=(me, normed_two, table, *[array for _, _, array in pieces],),
        after=after,
    )


def down_kernel(layout_of, me_ref, activ, slope, cotangent, resid, table, *rest):
    refs = rest[: len(layout_of)]
    output, grad_pre, grad_bias, weight, total, sem = rest[len(layout_of) :]
    step = pl.program_id(0)

    @pl.when(step == 0)
    def _():
        fetch(me_ref[0], layout_of, refs, (0, D), weight, sem)
        total[...] = resid[...] + line_of(table, DOWN_B)
        arrive(weight, sem)

    rows = weight[pl.ds(pl.multiple_of(step * TILE, TILE), TILE), :]
    sums = jnp.zeros((1, TILE), F32)
    for begin in range(0, activ.shape[0], ROWS):
        part = slice(begin, begin + ROWS)
        total[part, :] += nn(activ[part, :], rows)
        back = (nt(cotangent[part, :], rows) * slope[part, :].astype(F32)).astype(BF)
        grad_pre[part, :] = back
        sums += jnp.sum(back.astype(F32), axis=0, keepdims=True)
    grad_bias[...] = sums

    @pl.when(step == pl.num_programs(0) - 1)
    def _():
        output[...] = total[...].astype(BF)


def down(me, activ, slope, cotangent, resid, table, pieces, after=()):
    count = activ.shape[0]
    layout_of = describe(pieces)
    tile = pl.BlockSpec((count, TILE), lambda step: (0, step))
    return pallas(
        functools.partial(down_kernel, layout_of),
        grid=(FF // TILE,),
        in_specs=[SMEM, tile, tile, fixed(count, D), fixed(count, D), fixed(TABLE, D)] + [ANY] * len(pieces),
        out_specs=[fixed(count, D), tile, pl.BlockSpec((1, TILE), lambda step: (0, step))],
        out_shape=[
            jax.ShapeDtypeStruct((count, D), BF),
            jax.ShapeDtypeStruct((count, FF), BF),
            jax.ShapeDtypeStruct((1, FF), F32),
        ],
        scratch_shapes=[pltpu.VMEM((FF, D), BF), pltpu.VMEM((count, D), F32), pltpu.SemaphoreType.DMA],
        cost_estimate=cost(29),
        name="down",
            operands=(me, activ, slope, cotangent, resid, table, *[array for _, _, array in pieces],),
        after=after,
    )


def outer_rows_kernel(me_ref, left, left_other, right, right_other, *rest):
    sides, grad_bias = rest[:4], rest[4]
    step = pl.program_id(0)
    rows = FF // BLOCKS
    half = right.shape[1] // 2

    def group(ref):
        places = [(4 * step + z) ^ (me_ref[0] >> 1) for z in range(4)]
        return jnp.concatenate([ref[pl.ds(pl.multiple_of(place * rows, rows), rows), :] for place in places], 0)

    product = nn(group(left), right[...]) + nn(group(left_other), right_other[...])
    for side in range(2):
        bit = (step >> (1 - side)) & 1
        values = product[:, side * half : (side + 1) * half]

        @pl.when(bit == 0)
        def _():
            sides[2 * side][...] = values

        @pl.when(bit == 1)
        def _():
            sides[2 * side + 1][...] = values.astype(BF)

    @pl.when(step == 0)
    def _():
        grad_bias[...] = jnp.sum(right[...].astype(F32), axis=0, keepdims=True)


def outer_rows(me, left, left_other, right, right_other, after=()):
    size, count = left.shape
    width = right.shape[1]
    block = (4 * FF // BLOCKS, width // 2)
    return pallas(
        outer_rows_kernel,
        grid=(4,),
        in_specs=[SMEM] + [fixed(size, count)] * 2 + [fixed(count, width)] * 2,
        out_specs=[
            pl.BlockSpec(block, lambda step: (jnp.minimum(step, 1), 0)),
            pl.BlockSpec(block, lambda step: (jnp.maximum(step - 2, 0), 0)),
            pl.BlockSpec(block, lambda step: (step // 2, 0)),
            pl.BlockSpec(block, lambda step: (step // 2, 0)),
            fixed(1, width),
        ],
        out_shape=[jax.ShapeDtypeStruct((size // 2, width // 2), kind) for kind in (F32, BF, F32, BF)]
        + [jax.ShapeDtypeStruct((1, width), F32)],
        cost_estimate=cost(17),
        name="outer_rows",
        operands=(me, left, left_other, right, right_other),
        after=after,
    )


def outer_kernel(tiles, parts, *refs):
    sides = refs[4 * len(parts) : 4 * len(parts) + 4]
    grad_bias = refs[4 * len(parts) + 4]
    step = pl.program_id(0)
    for number, (begin, end) in enumerate(parts):
        left, left_other, right, right_other = refs[4 * number : 4 * number + 4]
        rows = left.shape[0] // (BLOCKS // 2)

        @pl.when((step >= begin) & (step < end))
        def _():
            product = nn(left[...], right[...]) + nn(left_other[...], right_other[...])
            for side in range(2):

                @pl.when((step >= tiles // 2) == bool(side))
                def _():
                    for which, positions in enumerate(parted(list(range(BLOCKS // 2)), UPPER[side][0] >> 1)):
                        target = sides[2 * side + which]
                        for position, first, length in runs_of(positions):
                            part = product[first * rows : (first + length) * rows, :]
                            target[position * rows : (position + length) * rows, :] = part.astype(target.dtype)

            grad_bias[...] = jnp.sum(right[...].astype(F32), axis=0, keepdims=True)


def outer(sets, tile_width, after=()):
    size, count = sets[0][0].shape
    parts, tiles, in_specs = [], 0, []
    for _, _, right, _ in sets:
        begin, end = tiles, tiles + right.shape[1] // tile_width
        parts.append((begin, end))
        tiles = end

        def place(step, begin=begin, end=end):
            return 0, jnp.clip(step - begin, 0, end - begin - 1)

        in_specs += [fixed(size, count)] * 2 + [pl.BlockSpec((count, tile_width), place)] * 2
    width = tiles * tile_width
    block = (size // 2, tile_width)
    firsts = pl.BlockSpec(block, lambda step: (0, jnp.minimum(step, tiles // 2 - 1)))
    seconds = pl.BlockSpec(block, lambda step: (0, jnp.maximum(step - tiles // 2, 0)))
    return pallas(
        functools.partial(outer_kernel, tiles, parts),
        grid=(tiles,),
        in_specs=in_specs,
        out_specs=[firsts, firsts, seconds, seconds, pl.BlockSpec((1, tile_width), lambda step: (0, step))],
        out_shape=[jax.ShapeDtypeStruct((size // 2, width // 2), kind) for kind in (F32, BF, F32, BF)]
        + [jax.ShapeDtypeStruct((1, width), F32)],
        cost_estimate=cost(4 * count * size * width / 0.55e9),
        name="outer",
        operands=tuple(array for each in sets for array in each),
        after=after,
    )


def branch_back_kernel(layout_of, me_ref, grad_pre, resid, cotangent, table, *rest):
    refs = rest[: len(layout_of)]
    grad_resid, grad_branch, grad_mixed, grad_gain, grad_shift, grad_bias, up_weight, out_weight, up_sem, out_sem = rest[
        len(layout_of) :
    ]

    @pl.when(pl.program_id(0) == 0)
    def _():
        fetch(me_ref[0], layout_of, refs, (D, D + FF), up_weight, up_sem)
        fetch(me_ref[0], layout_of, refs, (0, D), out_weight, out_sem)
        grad_gain[...] = jnp.zeros_like(grad_gain)
        grad_shift[...] = jnp.zeros_like(grad_shift)
        grad_bias[...] = jnp.zeros_like(grad_bias)
        arrive(up_weight, up_sem)
        arrive(out_weight, out_sem)

    upstream = nt(grad_pre[...], up_weight[...])
    back, gain_part, shift_part = norm_back(resid[...], line_of(table, GAIN_TWO), upstream)
    total = cotangent[...].astype(F32) + back
    low = total.astype(BF)
    grad_resid[...] = total
    grad_branch[...] = low
    grad_gain[...] += gain_part
    grad_shift[...] += shift_part
    grad_bias[...] += jnp.sum(low.astype(F32), axis=0, keepdims=True)
    grad_mixed[...] = nt(low, out_weight[...]).astype(BF)


def branch_back(me, grad_pre, resid, cotangent, table, pieces, after=()):
    count = resid.shape[0]
    layout_of = describe(pieces)
    rows = pl.BlockSpec((ROWS, D), lambda step: (step, 0))
    vector = jax.ShapeDtypeStruct((1, D), F32)
    return pallas(
        functools.partial(branch_back_kernel, layout_of),
        grid=(count // ROWS,),
        in_specs=[SMEM, pl.BlockSpec((ROWS, FF), lambda step: (step, 0)), rows, rows, fixed(TABLE, D)]
        + [ANY] * len(pieces),
        out_specs=[rows, rows, rows] + [fixed(1, D)] * 3,
        out_shape=[
            jax.ShapeDtypeStruct((count, D), F32),
            jax.ShapeDtypeStruct((count, D), BF),
            jax.ShapeDtypeStruct((count, D), BF),
            vector,
            vector,
            vector,
        ],
        scratch_shapes=[
            pltpu.VMEM((D, FF), BF),
            pltpu.VMEM((D, D), BF),
            pltpu.SemaphoreType.DMA,
            pltpu.SemaphoreType.DMA,
        ],
        cost_estimate=cost(21),
        name="branch_back",
            operands=(me, grad_pre, resid, cotangent, table, *[array for _, _, array in pieces],),
        after=after,
    )


def tokens_back_kernel(layout_of, chunks, me_ref, *rest):
    grads, rest = rest[:chunks], rest[chunks:]
    tokens, grad_resid, table = rest[:3]
    refs = rest[3 : 3 + len(layout_of)]
    grad_tokens, grad_gain, grad_shift, weight, sem = rest[3 + len(layout_of) :]

    @pl.when(pl.program_id(0) == 0)
    def _():
        fetch(me_ref[0], layout_of, refs, (0, 3 * D), weight, sem)
        grad_gain[...] = jnp.zeros_like(grad_gain)
        grad_shift[...] = jnp.zeros_like(grad_shift)
        arrive(weight, sem)

    quads = [
        (ref, begin) for ref in grads for begin in range(0, ref.shape[1], 3 * QUAD)
    ]
    ordered = jnp.concatenate(
        [ref[:, begin + part * QUAD : begin + (part + 1) * QUAD] for part in range(3) for ref, begin in quads], 1
    )
    back, gain_part, shift_part = norm_back(
        tokens[...].astype(F32), line_of(table, GAIN_ONE), nt(ordered, weight[...])
    )
    grad_tokens[...] = (grad_resid[...] + back).astype(BF)
    grad_gain[...] += gain_part
    grad_shift[...] += shift_part


def tokens_back(me, grads, tokens, grad_resid, table, pieces, after=()):
    count = tokens.shape[0]
    layout_of = describe(pieces)
    rows = pl.BlockSpec((ROWS, D), lambda step: (step, 0))
    vector = jax.ShapeDtypeStruct((1, D), F32)
    return pallas(
        functools.partial(tokens_back_kernel, layout_of, len(grads)),
        grid=(count // ROWS,),
        in_specs=[SMEM]
        + [pl.BlockSpec((ROWS, part.shape[1]), lambda step: (step, 0)) for part in grads]
        + [rows, rows, fixed(TABLE, D)]
        + [ANY] * len(pieces),
        out_specs=[rows, fixed(1, D), fixed(1, D)],
        out_shape=[jax.ShapeDtypeStruct((count, D), BF), vector, vector],
        scratch_shapes=[pltpu.VMEM((D, 3 * D), BF), pltpu.SemaphoreType.DMA],
        cost_estimate=cost(15),
        name="tokens_back",
            operands=(me, *grads, tokens, grad_resid, table, *[array for _, _, array in pieces],),
        after=after,
    )


def key_runs(positions, frames, patches):
    first, last = positions, positions + 1
    start = jnp.int32(0)
    for slot in range(frames.shape[1]):
        width = patches[0, slot] + 2
        size = frames[0, slot] * width
        offset = positions - start
        inside = (offset >= 0) & (offset < size)
        end = start + width + jnp.where(offset >= width, width, 0) + jnp.where(offset >= 2 * width, width, 0)
        first = jnp.where(inside, start, first)
        last = jnp.where(inside, end, last)
        start = start + size
    return first, last


def fill_mask(frames, patches, mask, runs):
    count = mask.shape[0]
    first, last = key_runs(lax.broadcasted_iota(jnp.int32, (1, count), 1), frames, patches)
    keys = lax.broadcasted_iota(jnp.int32, (count, count), 0)
    mask[...] = jnp.where((keys >= first) & (keys < last), 0.0, MASKED)
    for block in range(count // BQ):
        part = slice(block * BQ, (block + 1) * BQ)
        begin = jnp.min(first[:, part]) // BK
        runs[0, block] = begin
        runs[1, block] = (jnp.max(last[:, part]) + (BK - 1)) // BK - begin


def each_block(count, runs, work):
    blocks = count // BQ

    @pl.loop(0, 2 * blocks)
    def _(index):
        block = lax.rem(index, blocks)
        pair = index // blocks
        for size in range(1, count // BK + 1):

            @pl.when(runs[1, block] == size)
            def _():
                work(
                    pair,
                    pl.multiple_of(block * BQ, BQ),
                    pl.multiple_of(runs[0, block] * BK, BK),
                    size * BK,
                )


def one_head(pair_values, head):
    lane = lax.broadcasted_iota(jnp.int32, pair_values.shape, 1)
    return jnp.where(lane // HEAD == head, pair_values, jnp.zeros_like(pair_values))


def attend_kernel(frames, patches, queries, keys, values, *rest):
    mixed, log_totals, mask, turned, runs = rest[-5:]
    count = queries.shape[0]

    @pl.when(pl.program_id(0) == 0)
    def _():
        fill_mask(frames, patches, mask, runs)

    turned[...] = values[...].T

    def work(pair, row, key, size):
        lanes = pl.ds(pl.multiple_of(pair * LANES, LANES), LANES)
        rows = queries[pl.ds(row, BQ), lanes]
        these = keys[pl.ds(key, size), lanes]
        bias = mask[pl.ds(key, size), pl.ds(row, BQ)]
        scores = [nt(these, one_head(rows, head)) + bias for head in range(2)]
        results = []
        for head in range(2):
            highest = jnp.max(scores[head], axis=0, keepdims=True)
            expo = jnp.exp(scores[head] - highest)
            totals = jnp.sum(expo, axis=0, keepdims=True)
            place = pl.multiple_of(pair * LANES + head * HEAD, HEAD)
            result = nn(turned[pl.ds(place, HEAD), pl.ds(key, size)], expo.astype(BF))
            results.append(result * (1.0 / totals))
            log_totals[pl.ds(2 * pair + head, 1), pl.ds(row, BQ)] = highest + jnp.log(totals)
        mixed[pl.ds(row, BQ), lanes] = jnp.concatenate(results, 0).T.astype(BF)

    each_block(count, runs, work)


QUAD = 4 * HEAD
QUADS = HEADS // 4


def attend(frames, patches, qkv, begin, quads, before=(), after=()):
    count = qkv.shape[0]

    def columns(part):
        return pl.BlockSpec((count, QUAD), lambda step: (0, part * QUADS + begin + step))

    return pallas(
        attend_kernel,
        grid=(quads,),
        in_specs=[SMEM, SMEM, columns(0), columns(1), columns(2)] + [ANY] * len(before),
        out_specs=[columns(0), pl.BlockSpec((None, 4, count), lambda step: (begin + step, 0, 0))],
        out_shape=[jax.ShapeDtypeStruct((count, D), BF), jax.ShapeDtypeStruct((QUADS, 4, count), F32)],
        scratch_shapes=[
            pltpu.VMEM((count, count), F32),
            pltpu.VMEM((QUAD, count), BF),
            pltpu.SMEM((2, count // BQ), jnp.int32),
        ],
        input_output_aliases={5 + place: place for place in range(len(before))},
        cost_estimate=cost(9 * quads),
        name="attend",
            operands=(frames, patches, qkv, qkv, qkv, *before,),
        after=after,
    )


def attend_back_kernel(
    frames,
    patches,
    queries,
    keys,
    values,
    mixed,
    grads,
    log_totals,
    cosine,
    sine,
    grad_projected,
    mask,
    turned,
    grad_keys,
    grad_values,
    inner,
    runs,
):
    count = queries.shape[0]

    @pl.when(pl.program_id(0) == 0)
    def _():
        fill_mask(frames, patches, mask, runs)

    turned[...] = keys[...].T
    grad_keys[...] = jnp.zeros_like(grad_keys)
    grad_values[...] = jnp.zeros_like(grad_values)
    product = mixed[...].astype(F32) * grads[...].astype(F32)
    own = (
        lax.broadcasted_iota(jnp.int32, (8, QUAD), 1) // HEAD == lax.broadcasted_iota(jnp.int32, (8, QUAD), 0)
    ).astype(F32)
    inner[...] = lax.dot_general(
        own, product, (((1,), (1,)), ((), ())), precision=lax.Precision.HIGHEST, preferred_element_type=F32
    )

    def work(pair, row, key, size):
        lanes = pl.ds(pl.multiple_of(pair * LANES, LANES), LANES)
        block = pl.ds(row, BQ)
        span = pl.ds(key, size)
        bias = mask[span, block]
        these, those = keys[span, lanes], values[span, lanes]
        rows = [one_head(queries[block, lanes], head) for head in range(2)]
        rows_grads = [one_head(grads[block, lanes], head) for head in range(2)]
        probs, grad_scores, grad_rows = [], [], []
        for head in range(2):
            here = pl.ds(2 * pair + head, 1)
            share = jnp.exp(nt(these, rows[head]) + bias - log_totals[here, block])
            change = (share * (nt(those, rows_grads[head]) - inner[here, block])).astype(BF)
            place = pl.multiple_of(pair * LANES + head * HEAD, HEAD)
            grad_rows.append(nn(turned[pl.ds(place, HEAD), span], change))
            probs.append(share.astype(BF))
            grad_scores.append(change)
        grad_values[span, lanes] += nn(jnp.concatenate(probs, 1), jnp.concatenate(rows_grads, 0))
        grad_keys[span, lanes] += nn(jnp.concatenate(grad_scores, 1), jnp.concatenate(rows, 0))
        turned_back = jnp.concatenate(grad_rows, 0).T * HEAD**-0.5
        turned_back = turned_back * cosine[block, :] - partner(turned_back) * sine[block, :]
        grad_projected[block, lanes] = turned_back.astype(BF)

    each_block(count, runs, work)
    back = grad_keys[...] * wide(cosine[...], QUAD) - partner(grad_keys[...]) * wide(sine[...], QUAD)
    grad_projected[:, QUAD : 2 * QUAD] = back.astype(BF)
    grad_projected[:, 2 * QUAD :] = grad_values[...].astype(BF)


def attend_back(frames, patches, qkv, mixed, grads, log_totals, cosine, sine, begin, quads, after=()):
    count = qkv.shape[0]

    def columns(part):
        return pl.BlockSpec((count, QUAD), lambda step: (0, part * QUADS + begin + step))

    return pallas(
        attend_back_kernel,
        grid=(quads,),
        in_specs=[
            SMEM,
            SMEM,
            columns(0),
            columns(1),
            columns(2),
            columns(0),
            columns(0),
            pl.BlockSpec((None, 4, count), lambda step: (begin + step, 0, 0)),
            fixed(count, LANES),
            fixed(count, LANES),
        ],
        out_specs=pl.BlockSpec((count, 3 * QUAD), lambda step: (0, step)),
        out_shape=jax.ShapeDtypeStruct((count, 3 * QUAD * quads), BF),
        scratch_shapes=[
            pltpu.VMEM((count, count), F32),
            pltpu.VMEM((QUAD, count), BF),
            pltpu.VMEM((count, QUAD), F32),
            pltpu.VMEM((count, QUAD), F32),
            pltpu.VMEM((8, count), F32),
            pltpu.SMEM((2, count // BQ), jnp.int32),
        ],
        cost_estimate=cost(15 * quads),
        name="attend_back",
            operands=(frames, patches, qkv, qkv, qkv, mixed, grads, log_totals, cosine, sine,),
        after=after,
    )


def positions_of(frames, patches):
    frame_tokens = patches + 2
    clip_tokens = frames * frame_tokens
    clip_starts = jnp.cumsum(clip_tokens) - clip_tokens
    positions = jnp.arange(TOK_DEV, dtype=jnp.int32)
    inside = (
        (positions[None, :] >= clip_starts[:, None])
        & (positions[None, :] < (clip_starts + clip_tokens)[:, None])
    ).astype(jnp.int32)
    begins = jnp.sum(inside * clip_starts[:, None], axis=0)
    widths = jnp.maximum(jnp.sum(inside * frame_tokens[:, None], axis=0), 1)
    clip_sides = jnp.where(patches == SIDE_SMALL * SIDE_SMALL, SIDE_SMALL, SIDE_LARGE).astype(jnp.int32)
    sides_rows = jnp.maximum(jnp.sum(inside * clip_sides[:, None], axis=0), 1)
    offsets = positions - begins
    frame_index = offsets // widths
    within = offsets % widths
    patch_index = jnp.maximum(within - 2, 0)
    row_index = jnp.where(within >= 2, patch_index // sides_rows, 0)
    col_index = jnp.where(within >= 2, patch_index % sides_rows, 0)
    return frame_index, row_index, col_index


def rotary_tables(places):
    pair_count = HEAD // 2
    time_pairs = pair_count // 3
    row_pairs = (pair_count - time_pairs) // 2
    pair_ranks = np.arange(pair_count)
    group_ids = np.where(pair_ranks < time_pairs, 0, np.where(pair_ranks < time_pairs + row_pairs, 1, 2))
    group_first = np.array([0, time_pairs, time_pairs + row_pairs])[group_ids]
    group_sizes = np.array([time_pairs, row_pairs, pair_count - time_pairs - row_pairs])[group_ids]
    rate_table = 10000.0 ** (-(pair_ranks - group_first) / group_sizes)
    angles = jnp.zeros((TOK_DEV, pair_count), F32)
    for group_id, place in enumerate(places):
        table = jnp.asarray(np.where(group_ids == group_id, rate_table, 0.0), F32)
        angles = angles + place.astype(F32)[:, None] * table[None, :]
    cosine, sine = jnp.cos(angles), jnp.sin(angles)
    return jnp.concatenate([cosine] * 4, 1), jnp.concatenate([-sine, sine] * 2, 1)


def by_side(made):
    return (made[0], made[1]), (made[2], made[3])


def local(
    count,
    tokens,
    clip_frames,
    clip_patches,
    qkv_weight,
    qkv_bias,
    out_weight,
    out_bias,
    up_weight,
    up_bias,
    down_weight,
    down_bias,
    norm1_gain,
    norm1_shift,
    norm2_gain,
    norm2_shift,
    cotangent,
):
    net = Net(count)
    me_ref = net.me.reshape(1)
    small = (qkv_bias, out_bias, up_bias, down_bias, norm1_gain, norm1_shift, norm2_gain, norm2_shift)
    sizes = [item.shape[0] * count for item in small]
    ends = list(np.cumsum(sizes))
    clips = (clip_frames, clip_patches)

    shard = net.widen(qkv_weight)
    lines = lines_of(net.me, [net.widen(values) for values in small])
    first = Gather(net, jnp.concatenate([shard, lines, jnp.zeros_like(lines)], 1))
    middle_shard = net.widen(jnp.concatenate([out_weight, up_weight], 1))
    final_shard = net.widen(down_weight)
    cosine, sine = rotary_tables(positions_of(clip_frames[0], clip_patches[0]))

    def copy_of(shard):
        def put(relay):
            relay.put(relay.make(*shard.shape, BF), 0, 0, *shard.shape, [(shard, 0, 0)])

        return put

    made = advance([first], extra=copy_of(middle_shard))
    middle = Gather(net, made[0])
    made = advance([first])
    made = advance([first, middle])
    made = advance([middle], after=first.arrivals(), extra=copy_of(final_shard))
    final = Gather(net, made[0])
    normed_kept, normed_sent, qkv, table = project(me_ref, tokens, cosine, sine, first.pieces, after=made)
    made = advance([middle, final], after=[qkv])
    attended = attend(*clips, qkv, 0, QUADS // 2, after=made)
    made = advance([final], after=[*attended, *middle.arrivals()])
    normed_other = net.swap(normed_sent, 1)
    mixed, log_totals = attend(*clips, qkv, QUADS // 2, QUADS // 2, attended, after=made)
    made = advance([final], after=[mixed])
    resid, normed_two, two_kept, two_sent, mixed_kept, mixed_sent = branch(
        me_ref, mixed, tokens, table, middle.pieces, after=made
    )
    two_other, mixed_other = net.swap(two_sent, 1), net.swap(mixed_sent, 1)
    cotangent_other = net.swap(cotangent, 1)
    activ, slope, activ_kept, activ_sent = up(
        me_ref, normed_two, table, middle.pieces, after=[*final.arrivals(), normed_other]
    )
    activ_other = net.swap(activ_sent, 1)
    output, grad_pre, grad_up_bias = down(
        me_ref,
        activ,
        slope,
        cotangent,
        resid,
        table,
        final.pieces,
        after=[activ_kept, two_other, mixed_other, cotangent_other],
    )
    grad_pre_other = net.swap(grad_pre, 1)
    *made, grad_down_bias = outer_rows(
        me_ref, activ_kept, activ_other, cotangent, cotangent_other, after=[grad_pre]
    )
    moving_down = Scatter(net, by_side(made))
    grad_resid, grad_branch, grad_mixed, grad_gain_two, grad_shift_two, grad_out_bias = branch_back(
        me_ref, grad_pre, resid, cotangent, table, middle.pieces, after=[*made, grad_pre_other]
    )
    grad_branch_other = net.swap(grad_branch, 1)
    made = advance([moving_down], after=[grad_branch])
    *made, _ = outer(
        [(mixed_kept, mixed_other, grad_branch, grad_branch_other), (two_kept, two_other, grad_pre, grad_pre_other)],
        TILE,
        after=made,
    )
    moving_up = Scatter(net, by_side(made))
    parts, others, grad_qkv_bias, moving_qkv = [], [], [], []

    def back(quad, after):
        parts.append(attend_back(*clips, qkv, mixed, grad_mixed, log_totals, cosine, sine, quad, 1, after=after))
        others.append(net.swap(parts[-1], 1))
        return [parts[-1]]

    def weigh(quads, after):
        sets = [(normed_kept, normed_other, parts[quad], others[quad]) for quad in quads]
        *made, bias = outer(sets, 3 * QUAD // 2, after=after)
        grad_qkv_bias.append(bias)
        moving_qkv.append(Scatter(net, by_side(made)))
        return made

    made = back(0, made)
    made = advance([moving_down], after=made)
    made = back(1, made)
    made = advance([moving_down, moving_up], after=made)
    made = weigh([0, 1], made)
    made = back(2, made)
    made = advance([moving_up, moving_qkv[0]], after=[*made, moving_down.result])
    made = back(3, made)
    made = advance([moving_up, moving_qkv[0]], after=made)
    made = weigh([2, 3], made)
    grad_tokens, grad_gain_one, grad_shift_one = tokens_back(
        me_ref, parts, tokens, grad_resid, table, first.pieces, after=made
    )

    def by_part(parts):
        whole = jnp.concatenate(parts, 1)
        return whole.reshape(-1, QUADS, 3, QUAD).transpose(0, 2, 1, 3).reshape(-1, 3 * D)

    grads = [by_part(grad_qkv_bias), grad_out_bias, grad_up_bias, grad_down_bias]
    grads += [grad_gain_one, grad_shift_one, grad_gain_two, grad_shift_two]
    total = Sum(net, jnp.pad(jnp.concatenate(grads, 1).reshape(-1, D), ((0, TABLE - 13), (0, 0))))
    made = advance([moving_qkv[1], moving_qkv[0], total], after=[grad_tokens])
    made = advance([moving_qkv[1], total], after=made[:1])
    made = advance([moving_qkv[1], total], after=made[:1])
    summed = total.finish().reshape(-1)
    own = [
        lax.dynamic_slice_in_dim(summed, end - size + net.number * (size // count), size // count)
        for size, end in zip(sizes, ends)
    ]
    out_up = moving_up.result
    return (
        output,
        grad_tokens,
        by_part([each.result for each in moving_qkv]),
        own[0],
        out_up[:, :D],
        own[1],
        out_up[:, D:],
        own[2],
        moving_down.result,
        own[3],
        own[4],
        own[5],
        own[6],
        own[7],
    )


def solution(mesh):
    count = mesh.shape["fsdp"] * mesh.shape["dp"]
    rows, vector = P(AXES, None), P(AXES)
    placed = (rows, rows, rows, rows, vector, rows, vector, rows, vector, rows, vector) + (vector,) * 4 + (rows,)
    given = (rows, rows, rows, vector, rows, vector, rows, vector, rows) + (vector,) * 5
    return jax.shard_map(
        functools.partial(local, count), mesh=mesh, in_specs=placed, out_specs=given, check_vma=False
    )
```

```python
import functools

import jax
import jax.numpy as jnp
import numpy as np
from jax import lax
from jax.experimental import pallas as pl
from jax.experimental.pallas import tpu as pltpu
from jax.sharding import PartitionSpec as P

D = 1024
HEADS = 16
HEAD = 64
FF = 4096
SIDE_SMALL = 16
SIDE_LARGE = 24
TOK_DEV = 1024
AXES = ("fsdp", "dp")
EPSILON = 1e-06
MASKED = -1e30
BQ = 256
BK = 128
LENGTHS_OF_RUNS = (3, 4, 5, 7, 8)
LANES = 128
TILE = 512
ROWS = 256
F32 = jnp.float32
BF = jnp.bfloat16
VMEM_BYTES = 28 << 20
ATTEND_BYTES = 40 << 20
WEIGHT = 1.15e10


def cost(microseconds):
    return pl.CostEstimate(flops=int(microseconds * WEIGHT), bytes_accessed=0, transcendentals=0)


def nt(left, right):
    return lax.dot_general(left, right, (((1,), (1,)), ((), ())), preferred_element_type=F32)


def nn(left, right):
    return jnp.dot(left, right, preferred_element_type=F32)


SMEM = pl.BlockSpec(memory_space=pltpu.SMEM)
ANY = pl.BlockSpec(memory_space=pl.ANY)


def fixed(*shape):
    return pl.BlockSpec(shape, lambda *_: (0,) * len(shape))


def far(*arrays):
    return [pltpu.with_memory_space_constraint(array, pltpu.HBM) for array in arrays]


def pallas(kernel, operands, in_specs, after=(), vmem=VMEM_BYTES, near=(), far_in=(), **kept):
    given = len(operands)
    shapes, specs = kept.pop("out_shape"), kept.pop("out_specs")
    single = not isinstance(shapes, (list, tuple))
    shapes, specs = ([shapes], [specs]) if single else (list(shapes), list(specs))
    shapes = [
        shape if near == "all" or number in near else pltpu.HBM(shape.shape, shape.dtype)
        for number, shape in enumerate(shapes)
    ]
    operands = [
        far(array)[0] if number in far_in else array for number, array in enumerate(operands)
    ]
    waited = [each if each.shape == (8, LANES) else far(each)[0] for each in after]

    def body(*refs):
        outs = given + len(after)
        refs[outs + len(shapes)][...] = jnp.zeros((8, LANES), F32)
        kernel(*refs[:given], *refs[outs : outs + len(shapes)], *refs[outs + len(shapes) + 1 :])

    *made, token = pl.pallas_call(
        body,
        in_specs=list(in_specs) + [ANY] * len(after),
        out_specs=specs + [fixed(8, LANES)],
        out_shape=shapes + [jax.ShapeDtypeStruct((8, LANES), F32)],
        compiler_params=pltpu.CompilerParams(vmem_limit_bytes=vmem),
        **kept,
    )(*operands, *waited)
    return (made[0] if single else made), token


class Relay:
    def __init__(self):
        self.inputs, self.outs, self.jobs = [], [], []

    def take(self, array):
        for place, known in enumerate(self.inputs):
            if known is array:
                return place
        self.inputs.append(array)
        return len(self.inputs) - 1

    def make(self, rows, columns, dtype):
        self.outs.append(((rows, columns), dtype))
        return len(self.outs) - 1

    def put(self, out, row, column, rows, columns, terms):
        self.jobs.append((out, row, column, rows, columns, [(self.take(array), *at) for array, *at in terms]))

    def run(self, after=(), name="relay"):
        jobs, given = self.jobs, len(self.inputs)

        def kernel(*refs):
            sources, targets = refs[:given], refs[given:]
            for out, row, column, rows, columns, terms in jobs:
                step = next(size for size in (64, 32, 16) if rows % size == 0)

                @pl.loop(0, rows // step)
                def _(index):
                    def part(ref, row, column):
                        begin = pl.multiple_of(row + index * step, 16)
                        return ref.at[pl.ds(begin, step), column : column + columns]

                    total = part(sources[terms[0][0]], *terms[0][1:])[...]
                    for source, *at in terms[1:]:
                        total = total.astype(F32) + part(sources[source], *at)[...].astype(F32)
                    part(targets[out], row, column)[...] = total.astype(targets[out].dtype)

        moved = sum(2 * shape[0] * shape[1] * 3 for shape, _ in self.outs)
        return pallas(
            kernel,
            self.inputs,
            [fixed(*array.shape) for array in self.inputs],
            after,
            out_specs=[fixed(*shape) for shape, _ in self.outs],
            out_shape=[jax.ShapeDtypeStruct(shape, dtype) for shape, dtype in self.outs],
            cost_estimate=cost(1 + moved * 0.4e-6),
            name=name,
            near="all",
        )


BLOCKS = 32
UPPER = ((16, 8), (8, 16))


class Net:
    def __init__(self, count):
        self.count, self.share = count, max(count // BLOCKS, 1)
        self.number = lax.axis_index(AXES).astype(jnp.int32)
        self.me = self.number // self.share

    def swap(self, value, mask):
        return self.permute(value, mask * self.share)

    def permute(self, value, mask):
        return lax.ppermute(value, AXES, [(number, number ^ mask) for number in range(self.count)])

    def bits(self):
        return [1 << place for place in range(self.share.bit_length() - 1)]

    def widen(self, shard):
        for bit in self.bits():
            other = self.permute(shard, bit)
            shard = jnp.where(
                self.number & bit, jnp.concatenate([other, shard], 0), jnp.concatenate([shard, other], 0)
            )
        return shard

    def narrow(self, total):
        for bit in self.bits()[::-1]:
            low, high = jnp.split(total, 2, 0)
            own = jnp.where(self.number & bit, high, low)
            total = own + self.permute(jnp.where(self.number & bit, low, high), bit)
        return total

    def over_all(self, value):
        for place in range(self.count.bit_length() - 1):
            value = value + self.permute(value, 1 << place)
        return value


def runs_of(places):
    runs = []
    for position, place in enumerate(places):
        if runs and runs[-1][1] + runs[-1][2] == place:
            runs[-1][2] += 1
        else:
            runs.append([position, place, 1])
    return runs


def parted(places, mask):
    return [[position for position, place in enumerate(places) if bool(place & mask) == with_it] for with_it in (False, True)]


class Gather:
    def __init__(self, net, shard):
        self.net, self.rows, self.half = net, shard.shape[0], shard.shape[1] // 2
        self.blocks = [[0, 2, 4, 6]] * 2
        self.stage = 0
        self.held = [[shard] + [net.swap(shard, mask) for mask in (2, 4, 6)]] * 2

    def join(self, relay):
        self.made = []
        for side in range(2):
            size = self.held[side][0].shape[0]
            self.made.append(relay.make(len(self.held[side]) * size, self.half, BF))
            column = side * self.half if self.stage == 0 else 0
            for place, array in enumerate(self.held[side]):
                relay.put(self.made[side], place * size, 0, size, self.half, [(array, 0, column)])
            if self.stage == 1:
                self.blocks[side] = self.blocks[side] + [block ^ UPPER[side][0] for block in self.blocks[side]]

    def follow(self, made):
        arrays = [made[place] for place in self.made]
        self.held = [(array, self.net.swap(array, UPPER[side][self.stage])) for side, array in enumerate(arrays)]
        self.stage += 1
        if self.stage == 2:
            self.kept = [self.net.swap(array, 1) for array in arrays]

    def finish(self, after=()):
        sent = [come for _, come in self.held]
        if after:
            relay = Relay()
            for array in sent:
                relay.put(relay.make(*array.shape, BF), 0, 0, *array.shape, [(array, 0, 0)])
            sent, token = relay.run(after, "hold")
        self.pieces = []
        for side in range(2):
            blocks = self.blocks[side]
            others = [block ^ UPPER[side][1] for block in blocks]
            self.pieces += [
                (side, blocks, self.held[side][0]),
                (side, [block ^ 1 for block in blocks], self.kept[side]),
                (side, others, self.held[side][1]),
                (side, [block ^ 1 for block in others], self.net.swap(sent[side], 1)),
            ]
        return token if after else None

    def arrivals(self):
        return [array for held in self.held for array in held[1:]]


def whole(array):
    return [(0, None, array)]


class Scatter:
    def __init__(self, net, sides, widths=()):
        self.net = net
        self.stage = 0
        self.half = sides[0][0].shape[1]
        self.rows = sides[0][0].shape[0] // 8
        self.widths = widths or (2 * self.half,)
        self.held = [(stays, net.swap(leaves, UPPER[side][0])) for side, (stays, leaves) in enumerate(sides)]

    def join(self, relay):
        rows, half = self.rows, self.half
        self.made = []
        if self.stage == 0:
            for side, (own, come) in enumerate(self.held):
                for leaving in range(2):
                    self.made.append(relay.make(4 * rows, half, BF if leaving else F32))
                    first = 4 * rows * leaving
                    relay.put(self.made[-1], 0, 0, 4 * rows, half, [(own, first, 0), (come, first, 0)])
        elif self.stage == 1:
            for z in range(4):
                self.made.append(relay.make(rows, 2 * half, BF if z else F32))
                for side, (own, come) in enumerate(self.held):
                    relay.put(self.made[-1], 0, side * half, rows, half, [(own, z * rows, 0), (come, z * rows, 0)])
        else:
            column = 0
            for width in self.widths:
                self.made.append(relay.make(rows, width, F32))
                relay.put(self.made[-1], 0, 0, rows, width, [(array, 0, column) for array in self.held])
                column += width

    def follow(self, made):
        arrays = [made[place] for place in self.made]
        self.stage += 1
        if self.stage == 1:
            self.held = [(arrays[2 * side], self.net.swap(arrays[2 * side + 1], UPPER[side][1])) for side in range(2)]
        elif self.stage == 2:
            self.held = [arrays[0]] + [self.net.swap(arrays[z], 2 * z) for z in range(1, 4)]
        else:
            self.result = [self.net.narrow(array) for array in arrays]


class Sum:
    def __init__(self, net, value):
        self.net, self.value = net, value
        bits = [1 << place for place in range(net.count.bit_length() - 1)]
        self.groups = [(1,)] + [(bit,) for bit in bits[3:]] + [(2, 4, 6)]
        self.send()

    def send(self):
        self.come = [self.net.permute(self.value, mask) for mask in self.groups.pop(0)]

    def join(self, relay):
        self.made = relay.make(*self.value.shape, self.value.dtype)
        relay.put(self.made, 0, 0, *self.value.shape, [(array, 0, 0) for array in (self.value, *self.come)])

    def follow(self, made):
        self.value = made[self.made]
        self.send()

    def finish(self):
        while self.groups:
            self.value = self.value + sum(self.come)
            self.send()
        return (self.value, *self.come)


def advance(moving, after=(), name="relay", extra=None):
    relay = Relay()
    if extra is not None:
        extra(relay)
    for each in moving:
        each.join(relay)
    made, token = relay.run(after, name)
    for each in moving:
        each.follow(made)
    return made, token


def fetch(me, pieces, refs, columns, target, sem):
    first, last = columns
    for (side, blocks, width, rows), ref in zip(pieces, refs):
        begin, end = max(first, side * width), min(last, (side + 1) * width)
        if begin >= end:
            continue
        if blocks is None:
            pltpu.make_async_copy(ref.at[:, pl.ds(begin, end - begin)], target, sem).start()
            continue
        for place, block in enumerate(blocks):
            row = pl.multiple_of((me ^ block) * rows, rows)
            pltpu.make_async_copy(
                ref.at[pl.ds(place * rows, rows), pl.ds(begin - side * width, end - begin)],
                target.at[pl.ds(row, rows), pl.ds(begin - first, end - begin)],
                sem,
            ).start()


def arrive(target, sem):
    pltpu.make_async_copy(target, target, sem).wait()


def describe(pieces):
    return [
        (side, blocks and tuple(blocks), array.shape[1], array.shape[0] // len(blocks or (0,)))
        for side, blocks, array in pieces
    ]


def normed(inputs):
    average = jnp.mean(inputs, axis=-1, keepdims=True)
    centred = inputs - average
    scale = lax.rsqrt(jnp.mean(centred * centred, axis=-1, keepdims=True) + EPSILON)
    return centred * scale, scale


def norm_back(inputs, gain, upstream):
    unit, scale = normed(inputs)
    scaled = gain * upstream
    back = scale * (
        scaled
        - jnp.mean(scaled, axis=-1, keepdims=True)
        - unit * jnp.mean(scaled * unit, axis=-1, keepdims=True)
    )
    return back, jnp.sum(upstream * unit, axis=0, keepdims=True), jnp.sum(upstream, axis=0, keepdims=True)


def partner(values):
    half = HEAD // 2
    lane = lax.broadcasted_iota(jnp.int32, values.shape, 1)
    return jnp.where(
        lane % HEAD < half,
        pltpu.roll(values, values.shape[1] - half, 1),
        pltpu.roll(values, half, 1),
    )


def wide(table, width):
    return jnp.concatenate([table] * (width // LANES), 1)


def turn_out(me, values, kept, sent):
    turned = values.T
    rows = D // BLOCKS
    for number in range(BLOCKS):
        place = (number ^ me) >> 1
        block = turned[number * rows : (number + 1) * rows, :]
        own = ((number ^ me) & 1) == 0
        begin = pl.multiple_of(place * rows, rows)

        @pl.when(own)
        def _():
            kept[pl.ds(begin, rows), :] = block

        @pl.when(jnp.logical_not(own))
        def _():
            sent[pl.ds(begin, rows), :] = block


LINES = (3, 1, 1, 1, 1, 1, 1, 1)
LENGTHS = (96, 32, 128, 32, 32, 32, 32, 32)
QKV_B, OUT_B, UP_B, DOWN_B, GAIN_ONE, SHIFT_ONE, GAIN_TWO, SHIFT_TWO = 0, 3, 4, 8, 9, 10, 11, 12
TABLE = 16


def prepare_kernel(me_ref, shard, *rest):
    small, (joined, row, rows) = rest[:-3], rest[-3:]
    joined[:, : 3 * D] = shard[...]
    rows[...] = jnp.zeros_like(rows)
    line = 0
    for values, lines, length in zip(small, LINES, LENGTHS):
        row[...] = jnp.zeros_like(row)
        row[0:1, :length] = values[...].astype(F32)
        place = 0 if length == LANES else (me_ref[0] % 4) * length
        turned = pltpu.roll(row[:, : lines * LANES], place, 1)
        for part in range(lines):
            rows[line + part : line + part + 1, :] = turned[0:1, part * LANES : (part + 1) * LANES]
        line += lines
    joined[:, 3 * D : 3 * D + LANES] = rows[...].astype(BF)
    joined[:, 3 * D + LANES :] = jnp.zeros((BLOCKS, LANES), BF)


def prepare(me, shard, small):
    small = [values.reshape(1, -1) for values in small]
    return pallas(
        prepare_kernel,
        in_specs=[SMEM, fixed(*shard.shape)] + [fixed(*values.shape) for values in small],
        out_specs=fixed(BLOCKS, 3 * D + 2 * LANES),
        out_shape=jax.ShapeDtypeStruct((BLOCKS, 3 * D + 2 * LANES), BF),
        scratch_shapes=[pltpu.VMEM((8, 3 * LANES), F32), pltpu.VMEM((BLOCKS, LANES), F32)],
        cost_estimate=cost(2),
        name="prepare",
        near="all",
        far_in=range(1, 10),
        operands=(me, shard, *small),
    )


def table_of(lines, table):
    row = line = 0
    values = lines.astype(F32)
    table[...] = jnp.zeros_like(table)
    for count, length in zip(LINES, LENGTHS):
        spans = []
        for group in range(BLOCKS // 4):
            blocks = [(4 * group + member) * BLOCKS + line for member in range(4)]
            if length == LANES:
                spans += [values[block : block + 1, :] for block in blocks]
            else:
                for part in range(count):
                    spans.append(sum((values[block + part : block + part + 1, :] for block in blocks[1:]), values[blocks[0] + part : blocks[0] + part + 1, :]))
        for begin in range(0, len(spans), D // LANES):
            table[row : row + 1, :] = jnp.concatenate(spans[begin : begin + D // LANES], 1)
            row += 1
        line += count


def project_kernel(layout_of, me_ref, tokens, cosine, sine, *rest):
    refs = rest[: len(layout_of)]
    normed_kept, normed_sent, qkv_out, table, weight, lines, normed_out, sem, lines_sem = rest[len(layout_of) :]
    step = pl.program_id(0)

    @pl.when(step == 0)
    def _():
        fetch(me_ref[0], layout_of, refs, (3 * D, 3 * D + LANES), lines, lines_sem)
        fetch(me_ref[0], layout_of, refs, (0, 3 * D), weight, sem)
        arrive(lines, lines_sem)
        table_of(lines[...], table)
        gain, shift = table[GAIN_ONE : GAIN_ONE + 1, :], table[SHIFT_ONE : SHIFT_ONE + 1, :]
        for begin in range(0, tokens.shape[0], ROWS):
            part = slice(begin, begin + ROWS)
            unit, _ = normed(tokens[part, :].astype(F32))
            normed_out[part, :] = (unit * gain + shift).astype(BF)
        turn_out(me_ref[0], normed_out[...], normed_kept, normed_sent)
        arrive(weight, sem)

    column = pl.multiple_of(step * TILE, TILE)
    heads_tiles = D // TILE
    bias = table[pl.ds(QKV_B + step // heads_tiles, 1), pl.ds(pl.multiple_of(step % heads_tiles * TILE, TILE), TILE)]

    @pl.when(step < 2 * heads_tiles)
    def _():
        scale = jnp.where(step < heads_tiles, HEAD**-0.5, 1.0).astype(F32)
        for begin in range(0, tokens.shape[0], ROWS):
            part = slice(begin, begin + ROWS)
            product = nn(normed_out[part, :], weight[:, pl.ds(column, TILE)]) + bias
            turned = product * wide(cosine[part, :], TILE) + partner(product) * wide(sine[part, :], TILE)
            qkv_out[part, :] = (turned * scale).astype(BF)

    @pl.when(step >= 2 * heads_tiles)
    def _():
        product = nn(normed_out[...], weight[:, pl.ds(column, TILE)]) + bias
        qkv_out[...] = product.astype(BF)


def project(me, tokens, cosine, sine, pieces, after=()):
    count = tokens.shape[0]
    layout_of = describe(pieces)
    return pallas(
        functools.partial(project_kernel, layout_of),
        grid=(3 * D // TILE,),
        in_specs=[SMEM, fixed(count, D), fixed(count, LANES), fixed(count, LANES)] + [ANY] * len(pieces),
        out_specs=[fixed(D // 2, count)] * 2 + [pl.BlockSpec((count, TILE), lambda step: (0, step)), fixed(TABLE, D)],
        out_shape=[jax.ShapeDtypeStruct((D // 2, count), BF)] * 2
        + [jax.ShapeDtypeStruct((count, 3 * D), BF), jax.ShapeDtypeStruct((TABLE, D), F32)],
        scratch_shapes=[
            pltpu.VMEM((D, 3 * D), BF),
            pltpu.VMEM((D, LANES), BF),
            pltpu.VMEM((count, D), BF),
            pltpu.SemaphoreType.DMA,
            pltpu.SemaphoreType.DMA,
        ],
        cost_estimate=cost(16 / 4),
        name="project",
        far_in=(1, *range(4, 4 + len(pieces))),
        near=(1, 3),
        operands=(me, tokens, cosine, sine, *[array for _, _, array in pieces]),
        after=after,
    )


def line_of(table, line):
    return table[line : line + 1, :]


def branch_kernel(layout_of, me_ref, mixed, tokens, table, *rest):
    refs = rest[: len(layout_of)]
    resid, normed_two, normed_kept, normed_sent, mixed_kept, mixed_sent, weight, sem = rest[len(layout_of) :]

    @pl.when(pl.program_id(0) == 0)
    def _():
        fetch(me_ref[0], layout_of, refs, (0, D), weight, sem)
        arrive(weight, sem)

    value = tokens[...].astype(F32) + (nn(mixed[...], weight[...]) + line_of(table, OUT_B))
    resid[...] = value
    unit, _ = normed(value)
    low = (unit * line_of(table, GAIN_TWO) + line_of(table, SHIFT_TWO)).astype(BF)
    normed_two[...] = low
    turn_out(me_ref[0], low, normed_kept, normed_sent)
    turn_out(me_ref[0], mixed[...], mixed_kept, mixed_sent)


def branch(me, mixed, tokens, table, pieces, after=()):
    count = tokens.shape[0]
    layout_of = describe(pieces)
    rows = pl.BlockSpec((ROWS, D), lambda step: (step, 0))
    return pallas(
        functools.partial(branch_kernel, layout_of),
        grid=(count // ROWS,),
        in_specs=[SMEM, rows, rows, fixed(TABLE, D)] + [ANY] * len(pieces),
        out_specs=[rows, rows] + [pl.BlockSpec((D // 2, ROWS), lambda step: (0, step))] * 4,
        out_shape=[jax.ShapeDtypeStruct((count, D), F32), jax.ShapeDtypeStruct((count, D), BF)]
        + [jax.ShapeDtypeStruct((D // 2, count), BF)] * 4,
        scratch_shapes=[pltpu.VMEM((D, D), BF), pltpu.SemaphoreType.DMA],
        cost_estimate=cost(12 / 4),
        name="branch",
        far_in=(1, 2, *range(4, 4 + len(pieces))),
        near=(1, 3, 5),
            operands=(me, mixed, tokens, table, *[array for _, _, array in pieces],),
        after=after,
    )


def gelu_parts(value):
    decay = jnp.exp(-0.5 * value * value)
    point = 1.0 / (1.0 + (0.3275911 * 2.0**-0.5) * jnp.abs(value))
    series = 0.5 * 1.061405429
    for factor in (-1.453152027, 1.421413741, -0.284496736, 0.254829592):
        series = series * point + 0.5 * factor
    tail = series * point * decay
    return jnp.where(value >= 0, 1.0 - tail, tail), decay * (2.0 * np.pi) ** -0.5


def up_kernel(layout_of, me_ref, normed_two, table, *rest):
    refs = rest[: len(layout_of)]
    activ, slope, activ_sent, weight, sem = rest[len(layout_of) :]
    step = pl.program_id(0)

    @pl.when(step == 0)
    def _():
        fetch(me_ref[0], layout_of, refs, (D, D + FF), weight, sem)
        arrive(weight, sem)

    column = pl.multiple_of(step * TILE, TILE)
    tiles = D // TILE
    bias = table[pl.ds(UP_B + step // tiles, 1), pl.ds(pl.multiple_of(step % tiles * TILE, TILE), TILE)]
    for begin in range(0, normed_two.shape[0], ROWS):
        part = slice(begin, begin + ROWS)
        value = nn(normed_two[part, :], weight[:, pl.ds(column, TILE)]) + bias
        share, density = gelu_parts(value)
        low = (value * share).astype(BF)
        activ[part, :] = low
        slope[part, :] = (share + value * density).astype(BF)
        rows = FF // BLOCKS
        odd = (me_ref[0] & 1) == 1
        pairs = [low[:, begin : begin + 2 * rows] for begin in range(0, TILE, 2 * rows)]
        sent = [jnp.where(odd, pair[:, :rows], pair[:, rows:]) for pair in pairs]
        activ_sent[part, :] = jnp.concatenate(sent, 1)


def up(me, normed_two, table, pieces, after=()):
    count = normed_two.shape[0]
    layout_of = describe(pieces)
    tile = pl.BlockSpec((count, TILE), lambda step: (0, step))
    return pallas(
        functools.partial(up_kernel, layout_of),
        grid=(FF // TILE,),
        in_specs=[SMEM, fixed(count, D), fixed(TABLE, D)] + [ANY] * len(pieces),
        out_specs=[tile, tile, pl.BlockSpec((count, TILE // 2), lambda step: (0, step))],
        out_shape=[jax.ShapeDtypeStruct((count, FF), BF)] * 2 + [jax.ShapeDtypeStruct((count, FF // 2), BF)],
        scratch_shapes=[pltpu.VMEM((D, FF), BF), pltpu.SemaphoreType.DMA],
        cost_estimate=cost(35 / 4),
        name="up",
        far_in=range(3, 3 + len(pieces)),
            operands=(me, normed_two, table, *[array for _, _, array in pieces],),
        after=after,
    )


def pre_kernel(slope, cotangent, weight, grad_pre, grad_bias):
    sums = jnp.zeros((1, TILE), F32)
    for begin in range(0, slope.shape[0], ROWS):
        part = slice(begin, begin + ROWS)
        back = (nt(cotangent[part, :], weight[...]) * slope[part, :].astype(F32)).astype(BF)
        grad_pre[part, :] = back
        sums += jnp.sum(back.astype(F32), axis=0, keepdims=True)
    grad_bias[...] = sums


def pre(slope, cotangent, weight, after=()):
    count = slope.shape[0]
    tile = pl.BlockSpec((count, TILE), lambda step: (0, step))
    return pallas(
        pre_kernel,
        grid=(FF // TILE,),
        in_specs=[tile, fixed(count, D), pl.BlockSpec((TILE, D), lambda step: (step, 0))],
        out_specs=[tile, pl.BlockSpec((1, TILE), lambda step: (0, step))],
        out_shape=[jax.ShapeDtypeStruct((count, FF), BF), jax.ShapeDtypeStruct((1, FF), F32)],
        cost_estimate=cost(16),
        name="pre",
        far_in=(0, 1, 2),
        operands=(slope, cotangent, weight),
        after=after,
    )


def output_kernel(activ, resid, table, weight, *rest):
    output, total = rest[-2:]
    step = pl.program_id(0)

    @pl.when(step == 0)
    def _():
        total[...] = resid[...] + line_of(table, DOWN_B)

    total[...] += nn(activ[...], weight[...])

    @pl.when(step == pl.num_programs(0) - 1)
    def _():
        output[...] = total[...].astype(BF)


def output_rows(activ, resid, table, weight, part, parts, before=(), after=()):
    count = activ.shape[0]
    rows = count // parts
    wide_tile = 2 * TILE
    mine = pl.BlockSpec((rows, D), lambda step: (part, 0))
    return pallas(
        output_kernel,
        grid=(FF // wide_tile,),
        in_specs=[
            pl.BlockSpec((rows, wide_tile), lambda step: (part, step)),
            mine,
            fixed(TABLE, D),
            pl.BlockSpec((wide_tile, D), lambda step: (step, 0)),
        ]
        + [ANY] * len(before),
        out_specs=mine,
        out_shape=jax.ShapeDtypeStruct((count, D), BF),
        scratch_shapes=[pltpu.VMEM((rows, D), F32)],
        input_output_aliases={4 + place: place for place in range(len(before))},
        cost_estimate=cost(16 // parts),
        name="output",
        far_in=(0, 1, 3),
        operands=(activ, resid, table, weight, *before),
        after=after,
    )


def tn(left, right):
    return lax.dot_general(left, right, (((0,), (0,)), ((), ())), preferred_element_type=F32)


def outer_rows_kernel(me_ref, left, left_other, right, right_other, *rest):
    sides, grad_bias = rest[:4], rest[4]
    step = pl.program_id(0)
    rows = FF // BLOCKS
    half = right.shape[1] // 2

    def group(ref, places):
        return jnp.concatenate([ref[:, pl.ds(pl.multiple_of(place * rows, rows), rows)] for place in places], 1)

    own = group(left, [me_ref[0] ^ (2 * (4 * step + z)) for z in range(4)])
    other = group(left_other, [(me_ref[0] >> 1) ^ (4 * step + z) for z in range(4)])
    product = tn(own, right[...]) + tn(other, right_other[...])
    for side in range(2):
        bit = (step >> (1 - side)) & 1
        values = product[:, side * half : (side + 1) * half]

        @pl.when(bit == 0)
        def _():
            sides[2 * side][...] = values

        @pl.when(bit == 1)
        def _():
            sides[2 * side + 1][...] = values.astype(BF)

    @pl.when(step == 0)
    def _():
        grad_bias[...] = jnp.sum(right[...].astype(F32), axis=0, keepdims=True)


def outer_rows(me, left, left_other, right, right_other, after=()):
    count, size = left_other.shape
    width = right.shape[1]
    block = (4 * FF // BLOCKS, width // 2)
    return pallas(
        outer_rows_kernel,
        grid=(4,),
        in_specs=[SMEM, fixed(count, 2 * size), fixed(count, size)] + [fixed(count, width)] * 2,
        out_specs=[
            pl.BlockSpec(block, lambda step: (jnp.minimum(step, 1), 0)),
            pl.BlockSpec(block, lambda step: (jnp.maximum(step - 2, 0), 0)),
            pl.BlockSpec(block, lambda step: (step // 2, 0)),
            pl.BlockSpec(block, lambda step: (step // 2, 0)),
            fixed(1, width),
        ],
        out_shape=[jax.ShapeDtypeStruct((size // 2, width // 2), kind) for kind in (F32, BF, F32, BF)]
        + [jax.ShapeDtypeStruct((1, width), F32)],
        cost_estimate=cost(16),
        name="outer_rows",
        far_in=(1, 2, 3, 4),
        near=(0, 1, 2, 3),
        operands=(me, left, left_other, right, right_other),
        after=after,
    )


def outer_kernel(tiles, parts, *refs):
    sides, grad_bias = refs[-5:-1], refs[-1]
    step = pl.program_id(0)
    for begin, end, *places in parts:
        left, left_other, right, right_other = [refs[place] for place in places]
        rows = left.shape[0] // (BLOCKS // 2)

        @pl.when((step >= begin) & (step < end))
        def _():
            product = nn(left[...], right[...]) + nn(left_other[...], right_other[...])
            for side in range(2):

                @pl.when((step >= tiles // 2) == bool(side))
                def _():
                    for which, positions in enumerate(parted(list(range(BLOCKS // 2)), UPPER[side][0] >> 1)):
                        target = sides[2 * side + which]
                        for position, first, length in runs_of(positions):
                            part = product[first * rows : (first + length) * rows, :]
                            target[position * rows : (position + length) * rows, :] = part.astype(target.dtype)

            grad_bias[...] = jnp.sum(right[...].astype(F32), axis=0, keepdims=True)


def outer(sets, tile_width, after=()):
    size, count = sets[0][0].shape
    parts, tiles, operands, in_specs = [], 0, [], []

    def take(array, spec):
        for place, known in enumerate(operands):
            if known is array:
                return place
        operands.append(array)
        in_specs.append(spec)
        return len(operands) - 1

    for left, left_other, right, right_other in sets:
        begin, end = tiles, tiles + right.shape[1] // tile_width

        def tile_of(step, begin=begin, end=end):
            return 0, jnp.clip(step - begin, 0, end - begin - 1)

        spec = pl.BlockSpec((count, tile_width), tile_of)
        places = [take(each, fixed(size, count)) for each in (left, left_other)]
        places += [take(each, spec) for each in (right, right_other)]
        parts.append((begin, end, *places))
        tiles = end

    width = tiles * tile_width
    block = (size // 2, tile_width)
    firsts = pl.BlockSpec(block, lambda step: (0, jnp.minimum(step, tiles // 2 - 1)))
    seconds = pl.BlockSpec(block, lambda step: (0, jnp.maximum(step - tiles // 2, 0)))
    return pallas(
        functools.partial(outer_kernel, tiles, parts),
        grid=(tiles,),
        in_specs=in_specs,
        out_specs=[firsts, firsts, seconds, seconds, pl.BlockSpec((1, tile_width), lambda step: (0, step))],
        out_shape=[jax.ShapeDtypeStruct((size // 2, width // 2), kind) for kind in (F32, BF, F32, BF)]
        + [jax.ShapeDtypeStruct((1, width), F32)],
        cost_estimate=cost(4 * count * size * width / 0.55e9),
        name="outer",
        far_in=range(len(operands)),
        near=(0, 1, 2, 3),
        operands=tuple(operands),
        after=after,
    )


def branch_back_kernel(layout_of, me_ref, grad_pre, resid, cotangent, table, *rest):
    refs = rest[: len(layout_of)]
    grad_resid, grad_branch, grad_mixed, grad_gain, grad_shift, grad_bias, up_weight, out_weight, up_sem, out_sem = rest[
        len(layout_of) :
    ]

    @pl.when(pl.program_id(0) == 0)
    def _():
        fetch(me_ref[0], layout_of, refs, (D, D + FF), up_weight, up_sem)
        fetch(me_ref[0], layout_of, refs, (0, D), out_weight, out_sem)
        grad_gain[...] = jnp.zeros_like(grad_gain)
        grad_shift[...] = jnp.zeros_like(grad_shift)
        grad_bias[...] = jnp.zeros_like(grad_bias)
        arrive(up_weight, up_sem)
        arrive(out_weight, out_sem)

    upstream = nt(grad_pre[...], up_weight[...])
    back, gain_part, shift_part = norm_back(resid[...], line_of(table, GAIN_TWO), upstream)
    total = cotangent[...].astype(F32) + back
    low = total.astype(BF)
    grad_resid[...] = total
    grad_branch[...] = low
    grad_gain[...] += gain_part
    grad_shift[...] += shift_part
    grad_bias[...] += jnp.sum(low.astype(F32), axis=0, keepdims=True)
    grad_mixed[...] = nt(low, out_weight[...]).astype(BF)


def branch_back(me, grad_pre, resid, cotangent, table, pieces, after=()):
    count = resid.shape[0]
    layout_of = describe(pieces)
    rows = pl.BlockSpec((ROWS, D), lambda step: (step, 0))
    vector = jax.ShapeDtypeStruct((1, D), F32)
    return pallas(
        functools.partial(branch_back_kernel, layout_of),
        grid=(count // ROWS,),
        in_specs=[SMEM, pl.BlockSpec((ROWS, FF), lambda step: (step, 0)), rows, rows, fixed(TABLE, D)]
        + [ANY] * len(pieces),
        out_specs=[rows, rows, rows] + [fixed(1, D)] * 3,
        out_shape=[
            jax.ShapeDtypeStruct((count, D), F32),
            jax.ShapeDtypeStruct((count, D), BF),
            jax.ShapeDtypeStruct((count, D), BF),
            vector,
            vector,
            vector,
        ],
        scratch_shapes=[
            pltpu.VMEM((D, FF), BF),
            pltpu.VMEM((D, D), BF),
            pltpu.SemaphoreType.DMA,
            pltpu.SemaphoreType.DMA,
        ],
        cost_estimate=cost(21),
        name="branch_back",
        far_in=(1, 2, 3, *range(5, 5 + len(pieces))),
        near=(1, 2),
            operands=(me, grad_pre, resid, cotangent, table, *[array for _, _, array in pieces],),
        after=after,
    )


def tokens_back_kernel(layout_of, chunks, biases, me_ref, *rest):
    grads, rest = rest[:chunks], rest[chunks:]
    qkv_biases, rest = rest[:biases], rest[biases:]
    tokens, grad_resid, table, out_bias, up_bias, down_bias, gain_two, shift_two = rest[:8]
    refs = rest[8 : 8 + len(layout_of)]
    grad_tokens, grad_table, weight, sem = rest[8 + len(layout_of) :]

    @pl.when(pl.program_id(0) == 0)
    def _():
        fetch(me_ref[0], layout_of, refs, (0, 3 * D), weight, sem)
        grad_table[...] = jnp.zeros_like(grad_table)
        for ref, row in ((out_bias, OUT_B), (down_bias, DOWN_B), (gain_two, GAIN_TWO), (shift_two, SHIFT_TWO)):
            grad_table[row : row + 1, :] = ref[...]
        for part in range(FF // D):
            grad_table[UP_B + part : UP_B + part + 1, :] = up_bias[:, part * D : (part + 1) * D]
        groups = [(ref, begin) for ref in qkv_biases for begin in range(0, ref.shape[1], 3 * QUAD)]
        for quad, (ref, begin) in enumerate(groups):
            for part in range(3):
                values = ref[:, begin + part * QUAD : begin + (part + 1) * QUAD]
                grad_table[QKV_B + part : QKV_B + part + 1, quad * QUAD : (quad + 1) * QUAD] = values
        arrive(weight, sem)

    quads = [(ref, begin) for ref in grads for begin in range(0, ref.shape[1], 3 * QUAD)]
    ordered = jnp.concatenate(
        [ref[:, begin + part * QUAD : begin + (part + 1) * QUAD] for part in range(3) for ref, begin in quads], 1
    )
    back, gain_part, shift_part = norm_back(
        tokens[...].astype(F32), line_of(table, GAIN_ONE), nt(ordered, weight[...])
    )
    grad_tokens[...] = (grad_resid[...] + back).astype(BF)
    grad_table[GAIN_ONE : GAIN_ONE + 1, :] += gain_part
    grad_table[SHIFT_ONE : SHIFT_ONE + 1, :] += shift_part


def tokens_back(me, grads, qkv_biases, tokens, grad_resid, table, biases, pieces, after=()):
    count = tokens.shape[0]
    layout_of = describe(pieces)
    rows = pl.BlockSpec((ROWS, D), lambda step: (step, 0))
    return pallas(
        functools.partial(tokens_back_kernel, layout_of, len(grads), len(qkv_biases)),
        grid=(count // ROWS,),
        in_specs=[SMEM]
        + [pl.BlockSpec((ROWS, part.shape[1]), lambda step: (step, 0)) for part in grads]
        + [fixed(*part.shape) for part in qkv_biases]
        + [rows, rows, fixed(TABLE, D)]
        + [fixed(*part.shape) for part in biases]
        + [ANY] * len(pieces),
        out_specs=[rows, fixed(TABLE, D)],
        out_shape=[jax.ShapeDtypeStruct((count, D), BF), jax.ShapeDtypeStruct((TABLE, D), F32)],
        scratch_shapes=[pltpu.VMEM((D, 3 * D), BF), pltpu.SemaphoreType.DMA],
        cost_estimate=cost(15),
        name="tokens_back",
        far_in=range(len(grads) + len(qkv_biases) + 1, len(grads) + len(qkv_biases) + 3),
        operands=(me, *grads, *qkv_biases, tokens, grad_resid, table, *biases, *[array for _, _, array in pieces]),
        after=after,
    )


def finish_kernel(lengths, number, *refs):
    weights, sums, outs = refs[:8], refs[8:12], refs[12:]
    for chunk in range(2):
        arrived = weights[4 * chunk : 4 * chunk + 4]
        for half in range(2):
            for part in range(3):
                source = slice((3 * half + part) * QUAD, (3 * half + part + 1) * QUAD)
                target = part * D + (2 * chunk + half) * QUAD
                total = arrived[0][:, source]
                for ref in arrived[1:]:
                    total = total + ref[:, source].astype(F32)
                outs[0][:, target : target + QUAD] = total
    row = 0
    for place, (length, lines) in enumerate(lengths):
        place_in = number[0] * length
        wide_row = jnp.concatenate(
            [sum(line_of(ref, row + line) for ref in sums) for line in range(lines)], 1
        )
        wide_row = jnp.broadcast_to(wide_row, (8, lines * D))
        turned = pltpu.roll(wide_row, lines * D - place_in, 1)
        outs[1 + place][...] = turned[0:1, :length]
        row += lines


def finish(number, weights, total, sizes, count, after):
    lengths = [(size // count, size // D) for size in sizes]
    rows = weights[0].shape[0]
    return pallas(
        functools.partial(finish_kernel, lengths),
        in_specs=[SMEM] + [fixed(*array.shape) for array in (*weights, *total)],
        out_specs=[fixed(rows, 3 * D)] + [fixed(1, length) for length, _ in lengths],
        out_shape=[jax.ShapeDtypeStruct((rows, 3 * D), F32)]
        + [jax.ShapeDtypeStruct((1, length), F32) for length, _ in lengths],
        cost_estimate=cost(3),
        name="finish",
        near="all",
        operands=(number, *weights, *total),
        after=after,
    )


def key_runs(positions, frames, patches):
    first, last = positions, positions + 1
    start = jnp.int32(0)
    for slot in range(frames.shape[1]):
        width = patches[0, slot] + 2
        size = frames[0, slot] * width
        offset = positions - start
        inside = (offset >= 0) & (offset < size)
        end = start + width + jnp.where(offset >= width, width, 0) + jnp.where(offset >= 2 * width, width, 0)
        first = jnp.where(inside, start, first)
        last = jnp.where(inside, end, last)
        start = start + size
    return first, last


def fill_mask(frames, patches, mask, runs):
    count = mask.shape[0]
    first, last = key_runs(lax.broadcasted_iota(jnp.int32, (1, count), 1), frames, patches)
    keys = lax.broadcasted_iota(jnp.int32, (count, count), 0)
    mask[...] = jnp.where((keys >= first) & (keys < last), 0.0, MASKED)
    for block in range(count // BQ):
        part = slice(block * BQ, (block + 1) * BQ)
        begin = jnp.min(first[:, part]) // BK
        needed = (jnp.max(last[:, part]) + (BK - 1)) // BK - begin
        length = jnp.int32(LENGTHS_OF_RUNS[-1])
        for size in LENGTHS_OF_RUNS[-2::-1]:
            length = jnp.where(needed <= size, size, length)
        runs[0, block] = jnp.minimum(begin, count // BK - length)
        runs[1, block] = length


def each_block(count, runs, work):
    @pl.loop(0, count // BQ)
    def _(block):
        for size in LENGTHS_OF_RUNS:

            @pl.when(runs[1, block] == size)
            def _():
                work(pl.multiple_of(block * BQ, BQ), pl.multiple_of(runs[0, block] * BK, BK), size * BK)


def pair_of(head):
    return slice(head // 2 * LANES, (head // 2 + 1) * LANES)


def one_head(pair_values, head):
    lane = lax.broadcasted_iota(jnp.int32, pair_values.shape, 1)
    return jnp.where(lane // HEAD == head, pair_values, jnp.zeros_like(pair_values))


def attend_kernel(frames, patches, queries, keys, values, *rest):
    mixed, log_totals, mask, turned, runs = rest[-5:]
    count = queries.shape[0]

    @pl.when(pl.program_id(0) == 0)
    def _():
        fill_mask(frames, patches, mask, runs)

    turned[...] = values[...].T

    heads = queries.shape[1] // HEAD

    def work(row, key, size):
        block, span = pl.ds(row, BQ), pl.ds(key, size)
        bias = mask[span, block]
        scores = [
            nt(keys[span, pair_of(head)], one_head(queries[block, pair_of(head)], head % 2)) + bias
            for head in range(heads)
        ]
        results = []
        for head in range(heads):
            highest = jnp.max(scores[head], axis=0, keepdims=True)
            expo = jnp.exp(scores[head] - highest)
            totals = jnp.sum(expo, axis=0, keepdims=True)
            result = nn(turned[head * HEAD : (head + 1) * HEAD, span], expo.astype(BF))
            results.append(result * (1.0 / totals))
            log_totals[head : head + 1, block] = highest + jnp.log(totals)
        mixed[block, :] = jnp.concatenate(results, 0).T.astype(BF)

    each_block(count, runs, work)


QUAD = 4 * HEAD
QUADS = HEADS // 4


def attend(frames, patches, qkv, after=()):
    count = qkv.shape[0]
    groups, wide_block = QUADS // 2, 2 * QUAD

    def columns(part):
        return pl.BlockSpec((count, wide_block), lambda step: (0, part * groups + step))

    (mixed, log_totals), token = pallas(
        attend_kernel,
        grid=(groups,),
        in_specs=[SMEM, SMEM, columns(0), columns(1), columns(2)],
        out_specs=[columns(0), pl.BlockSpec((None, 8, count), lambda step: (step, 0, 0))],
        out_shape=[jax.ShapeDtypeStruct((count, D), BF), jax.ShapeDtypeStruct((groups, 8, count), F32)],
        scratch_shapes=[
            pltpu.VMEM((count, count), F32),
            pltpu.VMEM((wide_block, count), BF),
            pltpu.SMEM((2, count // BQ), jnp.int32),
        ],
        cost_estimate=cost(26 / 4),
        name="attend",
        far_in=(2, 3, 4),
        vmem=ATTEND_BYTES,
        operands=(frames, patches, qkv, qkv, qkv),
        after=after,
    )
    return (mixed, log_totals.reshape(QUADS, 4, count)), token


def attend_back_kernel(
    frames,
    patches,
    queries,
    keys,
    values,
    mixed,
    grads,
    log_totals,
    cosine,
    sine,
    grad_projected,
    mask,
    turned,
    grad_keys,
    grad_values,
    inner,
    runs,
):
    count = queries.shape[0]

    @pl.when(pl.program_id(0) == 0)
    def _():
        fill_mask(frames, patches, mask, runs)

    turned[...] = keys[...].T
    grad_keys[...] = jnp.zeros_like(grad_keys)
    grad_values[...] = jnp.zeros_like(grad_values)
    product = mixed[...].astype(F32) * grads[...].astype(F32)
    own = (
        lax.broadcasted_iota(jnp.int32, (8, QUAD), 1) // HEAD == lax.broadcasted_iota(jnp.int32, (8, QUAD), 0)
    ).astype(F32)
    inner[...] = lax.dot_general(
        own, product, (((1,), (1,)), ((), ())), precision=lax.Precision.HIGHEST, preferred_element_type=F32
    )

    def work(row, key, size):
        block, span = pl.ds(row, BQ), pl.ds(key, size)
        bias = mask[span, block]
        heads = range(QUAD // HEAD)
        rows = [one_head(queries[block, pair_of(head)], head % 2) for head in heads]
        rows_grads = [one_head(grads[block, pair_of(head)], head % 2) for head in heads]
        shares = [nt(keys[span, pair_of(head)], rows[head]) + bias for head in heads]
        changes = [nt(values[span, pair_of(head)], rows_grads[head]) for head in heads]
        probs, grad_scores, grad_rows = [], [], []
        for head in heads:
            share = jnp.exp(shares[head] - log_totals[head : head + 1, block])
            change = (share * (changes[head] - inner[head : head + 1, block])).astype(BF)
            grad_rows.append(nn(turned[head * HEAD : (head + 1) * HEAD, span], change))
            probs.append(share.astype(BF))
            grad_scores.append(change)
        for pair in range(QUAD // LANES):
            lanes, two = slice(pair * LANES, (pair + 1) * LANES), slice(2 * pair, 2 * pair + 2)
            grad_values[span, lanes] += nn(jnp.concatenate(probs[two], 1), jnp.concatenate(rows_grads[two], 0))
            grad_keys[span, lanes] += nn(jnp.concatenate(grad_scores[two], 1), jnp.concatenate(rows[two], 0))
        back = jnp.concatenate(grad_rows, 0).T * HEAD**-0.5
        back = back * wide(cosine[block, :], QUAD) - partner(back) * wide(sine[block, :], QUAD)
        grad_projected[block, :QUAD] = back.astype(BF)

    each_block(count, runs, work)
    back = grad_keys[...] * wide(cosine[...], QUAD) - partner(grad_keys[...]) * wide(sine[...], QUAD)
    grad_projected[:, QUAD : 2 * QUAD] = back.astype(BF)
    grad_projected[:, 2 * QUAD :] = grad_values[...].astype(BF)


def attend_back(frames, patches, qkv, mixed, grads, log_totals, cosine, sine, begin, quads, after=()):
    count = qkv.shape[0]

    def columns(part):
        return pl.BlockSpec((count, QUAD), lambda step: (0, part * QUADS + begin + step))

    return pallas(
        attend_back_kernel,
        grid=(quads,),
        in_specs=[
            SMEM,
            SMEM,
            columns(0),
            columns(1),
            columns(2),
            columns(0),
            columns(0),
            pl.BlockSpec((None, 4, count), lambda step: (begin + step, 0, 0)),
            fixed(count, LANES),
            fixed(count, LANES),
        ],
        out_specs=pl.BlockSpec((count, 3 * QUAD), lambda step: (0, step)),
        out_shape=jax.ShapeDtypeStruct((count, 3 * QUAD * quads), BF),
        scratch_shapes=[
            pltpu.VMEM((count, count), F32),
            pltpu.VMEM((QUAD, count), BF),
            pltpu.VMEM((count, QUAD), F32),
            pltpu.VMEM((count, QUAD), F32),
            pltpu.VMEM((8, count), F32),
            pltpu.SMEM((2, count // BQ), jnp.int32),
        ],
        cost_estimate=cost(15 * quads),
        name="attend_back",
        far_in=(2, 3, 4, 5),
        near=(0,),
            operands=(frames, patches, qkv, qkv, qkv, mixed, grads, log_totals, cosine, sine,),
        after=after,
    )


def positions_of(frames, patches):
    frame_tokens = patches + 2
    clip_tokens = frames * frame_tokens
    clip_starts = jnp.cumsum(clip_tokens) - clip_tokens
    positions = jnp.arange(TOK_DEV, dtype=jnp.int32)
    inside = (
        (positions[None, :] >= clip_starts[:, None])
        & (positions[None, :] < (clip_starts + clip_tokens)[:, None])
    ).astype(jnp.int32)
    begins = jnp.sum(inside * clip_starts[:, None], axis=0)
    widths = jnp.maximum(jnp.sum(inside * frame_tokens[:, None], axis=0), 1)
    clip_sides = jnp.where(patches == SIDE_SMALL * SIDE_SMALL, SIDE_SMALL, SIDE_LARGE).astype(jnp.int32)
    sides_rows = jnp.maximum(jnp.sum(inside * clip_sides[:, None], axis=0), 1)
    offsets = positions - begins
    frame_index = offsets // widths
    within = offsets % widths
    patch_index = jnp.maximum(within - 2, 0)
    row_index = jnp.where(within >= 2, patch_index // sides_rows, 0)
    col_index = jnp.where(within >= 2, patch_index % sides_rows, 0)
    return frame_index, row_index, col_index


def rotary_tables(places):
    pair_count = HEAD // 2
    time_pairs = pair_count // 3
    row_pairs = (pair_count - time_pairs) // 2
    pair_ranks = np.arange(pair_count)
    group_ids = np.where(pair_ranks < time_pairs, 0, np.where(pair_ranks < time_pairs + row_pairs, 1, 2))
    group_first = np.array([0, time_pairs, time_pairs + row_pairs])[group_ids]
    group_sizes = np.array([time_pairs, row_pairs, pair_count - time_pairs - row_pairs])[group_ids]
    rate_table = 10000.0 ** (-(pair_ranks - group_first) / group_sizes)
    angles = jnp.zeros((TOK_DEV, pair_count), F32)
    for group_id, place in enumerate(places):
        table = jnp.asarray(np.where(group_ids == group_id, rate_table, 0.0), F32)
        angles = angles + place.astype(F32)[:, None] * table[None, :]
    cosine, sine = jnp.cos(angles), jnp.sin(angles)
    return jnp.concatenate([cosine] * 4, 1), jnp.concatenate([-sine, sine] * 2, 1)


def by_side(made):
    return (made[0], made[1]), (made[2], made[3])


def local(
    count,
    tokens,
    clip_frames,
    clip_patches,
    qkv_weight,
    qkv_bias,
    out_weight,
    out_bias,
    up_weight,
    up_bias,
    down_weight,
    down_bias,
    norm1_gain,
    norm1_shift,
    norm2_gain,
    norm2_shift,
    cotangent,
):
    net = Net(count)
    me_ref = net.me.reshape(1)
    small = (qkv_bias, out_bias, up_bias, down_bias, norm1_gain, norm1_shift, norm2_gain, norm2_shift)
    sizes = [item.shape[0] * count for item in small]
    clips = (clip_frames, clip_patches)

    joined, _ = prepare(me_ref, net.widen(qkv_weight), [net.widen(values) for values in small])
    first = Gather(net, joined)
    middle_shard = net.widen(jnp.concatenate([out_weight, up_weight], 1))
    cosine, sine = rotary_tables(positions_of(clip_frames[0], clip_patches[0]))

    def copy_of(shard):
        def put(relay):
            relay.put(relay.make(*shard.shape, BF), 0, 0, *shard.shape, [(shard, 0, 0)])

        return put

    made, _ = advance([first], extra=copy_of(middle_shard))
    middle = Gather(net, made[0])
    advance([first], after=[middle.held[0][2]])
    first.finish()
    made, token = advance([middle], after=first.arrivals(), extra=copy_of(down_weight))
    final = lax.all_gather(made[0], AXES, axis=0, tiled=True)
    (normed_kept, normed_sent, qkv, table), token = project(
        me_ref, tokens, cosine, sine, first.pieces, after=[token]
    )
    normed_other = net.swap(normed_sent, 1)
    _, token = advance([middle], after=[token])
    (mixed, log_totals), token = attend(*clips, qkv, after=[token])
    token = middle.finish([token])
    cotangent_other = net.swap(cotangent, 1)
    (resid, normed_two, two_kept, two_sent, mixed_kept, mixed_sent), token = branch(
        me_ref, mixed, tokens, table, [piece for piece in middle.pieces if piece[0] == 0], after=[token]
    )
    two_other, mixed_other = net.swap(two_sent, 1), net.swap(mixed_sent, 1)
    (activ, slope, activ_sent), token = up(me_ref, normed_two, table, middle.pieces, after=[token])
    activ_other = net.swap(activ_sent, 1)
    (grad_pre, grad_up_bias), token = pre(slope, cotangent, final, after=[token])
    grad_pre_other = net.swap(grad_pre, 1)
    (*sides, grad_down_bias), token = outer_rows(
        me_ref, activ, activ_other, cotangent, cotangent_other, after=[token]
    )
    moving_down = Scatter(net, by_side(sides))
    (grad_resid, grad_branch, grad_mixed, grad_gain_two, grad_shift_two, grad_out_bias), token = branch_back(
        me_ref, grad_pre, resid, cotangent, table, middle.pieces, after=[token]
    )
    grad_branch_other = net.swap(grad_branch, 1)
    _, token = advance([moving_down], after=[token])
    (*sides, _), token = outer(
        [(mixed_kept, mixed_other, grad_branch, grad_branch_other), (two_kept, two_other, grad_pre, grad_pre_other)],
        TILE,
        after=[token],
    )
    moving_up = Scatter(net, by_side(sides), (D, FF))
    parts, others, grad_qkv_bias, moving_qkv = [], [], [], []

    def back(quad, token):
        part, token = attend_back(
            *clips, qkv, mixed, grad_mixed, log_totals, cosine, sine, quad, 1, after=[token]
        )
        parts.append(part)
        others.append(net.swap(part, 1))
        return token

    def weigh(quads, token):
        sets = [(normed_kept, normed_other, parts[quad], others[quad]) for quad in quads]
        (*sides, bias), token = outer(sets, QUAD, after=[token])
        grad_qkv_bias.append(bias)
        moving_qkv.append(Scatter(net, by_side(sides)))
        return token

    token = back(0, token)
    _, token = advance([moving_down], after=[token])
    token = back(1, token)
    _, token = advance([moving_up], after=[token])
    token = weigh([0, 1], token)
    _, token = advance([moving_up], after=[token])
    token = back(2, token)
    _, token = advance([moving_down, moving_qkv[0]], after=[token])
    token = back(3, token)
    _, token = advance([moving_qkv[0]], after=[token])
    token = weigh([2, 3], token)
    (grad_tokens, grad_table), token = tokens_back(
        me_ref,
        parts,
        grad_qkv_bias,
        tokens,
        grad_resid,
        table,
        (grad_out_bias, grad_up_bias, grad_down_bias, grad_gain_two, grad_shift_two),
        first.pieces,
        after=[token],
    )
    total = Sum(net, grad_table)
    def rows_of(part, token, before=()):
        return output_rows(activ, resid, table, final, part, 4, before, after=[token])

    _, token = advance([moving_qkv[1], moving_up], after=[token, *moving_qkv[0].held[1:]])
    output, token = rows_of(0, token)
    _, token = advance([total], after=[token])
    output, token = rows_of(1, token, [output])
    _, token = advance([moving_qkv[1], total], after=[token])
    output, token = rows_of(2, token, [output])
    _, token = advance([total], after=[token])
    output, token = rows_of(3, token, [output])
    (grad_qkv_weight, *own), _ = finish(
        net.number.reshape(1), (*moving_qkv[0].held, *moving_qkv[1].held), total.finish(), sizes, count, [token]
    )
    own = [values.reshape(-1) for values in own]
    return (
        output,
        grad_tokens,
        net.narrow(grad_qkv_weight),
        own[0],
        moving_up.result[0],
        own[1],
        moving_up.result[1],
        own[2],
        moving_down.result[0],
        own[3],
        own[4],
        own[5],
        own[6],
        own[7],
    )


def solution(mesh):
    count = mesh.shape["fsdp"] * mesh.shape["dp"]
    rows, vector = P(AXES, None), P(AXES)
    placed = (rows, rows, rows, rows, vector, rows, vector, rows, vector, rows, vector) + (vector,) * 4 + (rows,)
    given = (rows, rows, rows, vector, rows, vector, rows, vector, rows) + (vector,) * 5
    return jax.shard_map(
        functools.partial(local, count), mesh=mesh, in_specs=placed, out_specs=given, check_vma=False
    )
```

```python
import functools

import jax
import jax.numpy as jnp
import numpy as np
from jax import lax
from jax.experimental import pallas as pl
from jax.experimental.pallas import tpu as pltpu
from jax.sharding import PartitionSpec as P

D = 1024
HEADS = 16
HEAD = 64
FF = 4096
SIDE_SMALL = 16
SIDE_LARGE = 24
TOK_DEV = 1024
AXES = ("fsdp", "dp")
EPSILON = 1e-06
MASKED = -1e30
BQ = 256
BK = 128
LENGTHS_OF_RUNS = (3, 4, 5, 7, 8)
LANES = 128
TILE = 512
WIDE_TILE = 1024
ROWS = 256
UP_ROWS = 128
F32 = jnp.float32
BF = jnp.bfloat16
VMEM_BYTES = 28 << 20
ATTEND_BYTES = 40 << 20
WEIGHT = 1.15e10


def cost(microseconds):
    return pl.CostEstimate(flops=int(microseconds * WEIGHT), bytes_accessed=0, transcendentals=0)


def nt(left, right):
    return lax.dot_general(left, right, (((1,), (1,)), ((), ())), preferred_element_type=F32)


def nn(left, right):
    return jnp.dot(left, right, preferred_element_type=F32)


SMEM = pl.BlockSpec(memory_space=pltpu.SMEM)
ANY = pl.BlockSpec(memory_space=pl.ANY)


def fixed(*shape):
    return pl.BlockSpec(shape, lambda *_: (0,) * len(shape))


def far(*arrays):
    return [pltpu.with_memory_space_constraint(array, pltpu.HBM) for array in arrays]


def pallas(kernel, operands, in_specs, after=(), vmem=VMEM_BYTES, near=(), far_in=(), prefetch=0, **kept):
    given = len(operands)
    shapes, specs = kept.pop("out_shape"), kept.pop("out_specs")
    single = not isinstance(shapes, (list, tuple))
    shapes, specs = ([shapes], [specs]) if single else (list(shapes), list(specs))
    shapes = [
        shape if near == "all" or number in near else pltpu.HBM(shape.shape, shape.dtype)
        for number, shape in enumerate(shapes)
    ]
    operands = [
        far(array)[0] if number in far_in else array for number, array in enumerate(operands)
    ]
    waited = [each if each.shape == (8, LANES) else far(each)[0] for each in after]

    def body(*refs):
        outs = given + len(after)
        refs[outs + len(shapes)][...] = jnp.zeros((8, LANES), F32)
        kernel(*refs[:given], *refs[outs : outs + len(shapes)], *refs[outs + len(shapes) + 1 :])

    places = dict(in_specs=list(in_specs) + [ANY] * len(after), out_specs=specs + [fixed(8, LANES)])
    if prefetch:
        places |= dict(grid=kept.pop("grid"), scratch_shapes=kept.pop("scratch_shapes", ()))
        places = dict(grid_spec=pltpu.PrefetchScalarGridSpec(num_scalar_prefetch=prefetch, **places))
    *made, token = pl.pallas_call(
        body,
        **places,
        out_shape=shapes + [jax.ShapeDtypeStruct((8, LANES), F32)],
        compiler_params=pltpu.CompilerParams(vmem_limit_bytes=vmem),
        **kept,
    )(*operands, *waited)
    return (made[0] if single else made), token


def hold(arrays, after):
    return pallas(
        lambda *refs: None,
        arrays,
        [ANY] * len(arrays),
        after,
        out_specs=[ANY] * len(arrays),
        out_shape=[jax.ShapeDtypeStruct(array.shape, array.dtype) for array in arrays],
        input_output_aliases={place: place for place in range(len(arrays))},
        far_in=range(len(arrays)),
        cost_estimate=cost(1),
        name="hold",
    )


class Relay:
    def __init__(self):
        self.inputs, self.outs, self.jobs = [], [], []

    def take(self, array):
        for place, known in enumerate(self.inputs):
            if known is array:
                return place
        self.inputs.append(array)
        return len(self.inputs) - 1

    def make(self, rows, columns, dtype):
        self.outs.append(((rows, columns), dtype))
        return len(self.outs) - 1

    def put(self, out, row, column, rows, columns, terms):
        self.jobs.append((out, row, column, rows, columns, [(self.take(array), *at) for array, *at in terms]))

    def run(self, after=(), name="relay"):
        jobs, given = self.jobs, len(self.inputs)

        def kernel(*refs):
            sources, targets = refs[:given], refs[given:]
            for out, row, column, rows, columns, terms in jobs:
                step = next(size for size in (64, 32, 16) if rows % size == 0)

                @pl.loop(0, rows // step)
                def _(index):
                    def part(ref, row, column):
                        begin = pl.multiple_of(row + index * step, 16)
                        return ref.at[pl.ds(begin, step), column : column + columns]

                    total = part(sources[terms[0][0]], *terms[0][1:])[...]
                    for source, *at in terms[1:]:
                        total = total.astype(F32) + part(sources[source], *at)[...].astype(F32)
                    part(targets[out], row, column)[...] = total.astype(targets[out].dtype)

        moved = sum(2 * shape[0] * shape[1] * 3 for shape, _ in self.outs)
        return pallas(
            kernel,
            self.inputs,
            [fixed(*array.shape) for array in self.inputs],
            after,
            out_specs=[fixed(*shape) for shape, _ in self.outs],
            out_shape=[jax.ShapeDtypeStruct(shape, dtype) for shape, dtype in self.outs],
            cost_estimate=cost(1 + moved * 0.4e-6),
            name=name,
            near="all",
        )


BLOCKS = 32
UPPER = ((16, 8), (8, 16))


class Net:
    def __init__(self, count):
        self.count, self.share = count, max(count // BLOCKS, 1)
        self.number = lax.axis_index(AXES).astype(jnp.int32)
        self.me = self.number // self.share

    def swap(self, value, mask):
        return self.permute(value, mask * self.share)

    def permute(self, value, mask):
        return lax.ppermute(value, AXES, [(number, number ^ mask) for number in range(self.count)])

    def bits(self):
        return [1 << place for place in range(self.share.bit_length() - 1)]

    def widen(self, shard):
        for bit in self.bits():
            other = self.permute(shard, bit)
            shard = jnp.where(
                self.number & bit, jnp.concatenate([other, shard], 0), jnp.concatenate([shard, other], 0)
            )
        return shard

    def narrow(self, total):
        for bit in self.bits()[::-1]:
            low, high = jnp.split(total, 2, 0)
            own = jnp.where(self.number & bit, high, low)
            total = own + self.permute(jnp.where(self.number & bit, low, high), bit)
        return total

    def over_all(self, value):
        for place in range(self.count.bit_length() - 1):
            value = value + self.permute(value, 1 << place)
        return value


def runs_of(places):
    runs = []
    for position, place in enumerate(places):
        if runs and runs[-1][1] + runs[-1][2] == place:
            runs[-1][2] += 1
        else:
            runs.append([position, place, 1])
    return runs


def parted(places, mask):
    return [[position for position, place in enumerate(places) if bool(place & mask) == with_it] for with_it in (False, True)]


class Gather:
    def __init__(self, net, shard):
        self.net, self.rows, self.half = net, shard.shape[0], shard.shape[1] // 2
        self.blocks = [[0, 2, 4, 6]] * 2
        self.stage = 0
        self.held = [[shard] + [net.swap(shard, mask) for mask in (2, 4, 6)]] * 2

    def join(self, relay):
        self.made = []
        for side in range(2):
            size = self.held[side][0].shape[0]
            self.made.append(relay.make(len(self.held[side]) * size, self.half, BF))
            column = side * self.half if self.stage == 0 else 0
            for place, array in enumerate(self.held[side]):
                relay.put(self.made[side], place * size, 0, size, self.half, [(array, 0, column)])
            if self.stage == 1:
                self.blocks[side] = self.blocks[side] + [block ^ UPPER[side][0] for block in self.blocks[side]]

    def follow(self, made):
        arrays = [made[place] for place in self.made]
        self.held = [(array, self.net.swap(array, UPPER[side][self.stage])) for side, array in enumerate(arrays)]
        self.stage += 1
        if self.stage == 2:
            self.kept = [self.net.swap(array, 1) for array in arrays]

    def finish(self, after=()):
        come, token = [come for _, come in self.held], None
        if after:
            come, token = hold(come, after)
        self.pieces = []
        for side in range(2):
            blocks = self.blocks[side]
            others = [block ^ UPPER[side][1] for block in blocks]
            self.pieces += [
                (side, blocks, self.held[side][0]),
                (side, [block ^ 1 for block in blocks], self.kept[side]),
                (side, others, come[side]),
                (side, [block ^ 1 for block in others], self.net.swap(come[side], 1)),
            ]
        return token

    def arrivals(self):
        return [array for held in self.held for array in held[1:]]


def whole(array):
    return [(0, None, array)]


class Scatter:
    def __init__(self, net, sides, widths=()):
        self.net = net
        self.stage = 0
        self.half = sides[0][0].shape[1]
        self.rows = sides[0][0].shape[0] // 8
        self.widths = widths or (2 * self.half,)
        self.held = [(stays, net.swap(leaves, UPPER[side][0])) for side, (stays, leaves) in enumerate(sides)]

    def join(self, relay):
        rows, half = self.rows, self.half
        self.made = []
        if self.stage == 0:
            for side, (own, come) in enumerate(self.held):
                for leaving in range(2):
                    self.made.append(relay.make(4 * rows, half, BF if leaving else F32))
                    first = 4 * rows * leaving
                    relay.put(self.made[-1], 0, 0, 4 * rows, half, [(own, first, 0), (come, first, 0)])
        elif self.stage == 1:
            for z in range(4):
                self.made.append(relay.make(rows, 2 * half, BF if z else F32))
                for side, (own, come) in enumerate(self.held):
                    relay.put(self.made[-1], 0, side * half, rows, half, [(own, z * rows, 0), (come, z * rows, 0)])
        else:
            column = 0
            for width in self.widths:
                self.made.append(relay.make(rows, width, F32))
                relay.put(self.made[-1], 0, 0, rows, width, [(array, 0, column) for array in self.held])
                column += width

    def follow(self, made):
        arrays = [made[place] for place in self.made]
        self.stage += 1
        if self.stage == 1:
            self.held = [(arrays[2 * side], self.net.swap(arrays[2 * side + 1], UPPER[side][1])) for side in range(2)]
        elif self.stage == 2:
            self.held = [arrays[0]] + [self.net.swap(arrays[z], 2 * z) for z in range(1, 4)]
        else:
            self.result = [self.net.narrow(array) for array in arrays]


class Sum:
    def __init__(self, net, value):
        self.net, self.value = net, value
        bits = [1 << place for place in range(net.count.bit_length() - 1)]
        self.groups = [(1,), (2, 4, 6)] + [(bit,) for bit in bits[3:]]
        self.send()

    def send(self):
        self.come = [self.net.permute(self.value, mask) for mask in self.groups.pop(0)]

    def join(self, relay):
        self.made = relay.make(*self.value.shape, self.value.dtype)
        relay.put(self.made, 0, 0, *self.value.shape, [(array, 0, 0) for array in (self.value, *self.come)])

    def follow(self, made):
        self.value = made[self.made]
        self.send()

    def finish(self):
        while self.groups:
            self.value = self.value + sum(self.come)
            self.send()
        return (self.value, *self.come)


def advance(moving, after=(), name="relay", extra=None):
    relay = Relay()
    if extra is not None:
        extra(relay)
    for each in moving:
        each.join(relay)
    made, token = relay.run(after, name)
    for each in moving:
        each.follow(made)
    return made, token


def fetch(me, pieces, refs, columns, target, sem):
    first, last = columns
    for (side, blocks, width, rows), ref in zip(pieces, refs):
        begin, end = max(first, side * width), min(last, (side + 1) * width)
        if begin >= end:
            continue
        if blocks is None:
            pltpu.make_async_copy(ref.at[:, pl.ds(begin, end - begin)], target, sem).start()
            continue
        for place, block in enumerate(blocks):
            row = pl.multiple_of((me ^ block) * rows, rows)
            pltpu.make_async_copy(
                ref.at[pl.ds(place * rows, rows), pl.ds(begin - side * width, end - begin)],
                target.at[pl.ds(row, rows), pl.ds(begin - first, end - begin)],
                sem,
            ).start()


def arrive(target, sem):
    pltpu.make_async_copy(target, target, sem).wait()


def describe(pieces):
    return [
        (side, blocks and tuple(blocks), array.shape[1], array.shape[0] // len(blocks or (0,)))
        for side, blocks, array in pieces
    ]


def normed(inputs):
    average = jnp.mean(inputs, axis=-1, keepdims=True)
    centred = inputs - average
    scale = lax.rsqrt(jnp.mean(centred * centred, axis=-1, keepdims=True) + EPSILON)
    return centred * scale, scale


def norm_back(inputs, gain, upstream):
    unit, scale = normed(inputs)
    scaled = gain * upstream
    back = scale * (
        scaled
        - jnp.mean(scaled, axis=-1, keepdims=True)
        - unit * jnp.mean(scaled * unit, axis=-1, keepdims=True)
    )
    return back, jnp.sum(upstream * unit, axis=0, keepdims=True), jnp.sum(upstream, axis=0, keepdims=True)


def partner(values):
    half = HEAD // 2
    lane = lax.broadcasted_iota(jnp.int32, values.shape, 1)
    return jnp.where(
        lane % HEAD < half,
        pltpu.roll(values, values.shape[1] - half, 1),
        pltpu.roll(values, half, 1),
    )


def wide(table, width):
    return jnp.concatenate([table] * (width // LANES), 1)


def turn_out(me, values, kept, sent, turned):
    turned[...] = values.T
    rows = D // BLOCKS
    for place in range(BLOCKS // 2):
        here = slice(place * rows, (place + 1) * rows)
        for target, parity in ((kept, 0), (sent, 1)):
            block = pl.multiple_of(((2 * place + parity) ^ me) * rows, rows)
            target[here, :] = turned[pl.ds(block, rows), :]


LINES = (3, 1, 1, 1, 1, 1, 1, 1)
LENGTHS = (96, 32, 128, 32, 32, 32, 32, 32)
QKV_B, OUT_B, UP_B, DOWN_B, GAIN_ONE, SHIFT_ONE, GAIN_TWO, SHIFT_TWO = 0, 3, 4, 8, 9, 10, 11, 12
TABLE = 16


def prepare_kernel(me_ref, shard, second, *rest):
    small, (joined, row, rows) = rest[:-3], rest[-3:]
    joined[:, : 3 * D] = shard[...]
    joined[:, 3 * D : 4 * D] = second[...]
    rows[...] = jnp.zeros_like(rows)
    line = 0
    for values, lines, length in zip(small, LINES, LENGTHS):
        row[...] = jnp.zeros_like(row)
        row[0:1, :length] = values[...].astype(F32)
        place = 0 if length == LANES else (me_ref[0] % 4) * length
        turned = pltpu.roll(row[:, : lines * LANES], place, 1)
        for part in range(lines):
            rows[line + part : line + part + 1, :] = turned[0:1, part * LANES : (part + 1) * LANES]
        line += lines
    joined[:, 4 * D : 4 * D + LANES] = rows[...].astype(BF)
    joined[:, 4 * D + LANES :] = jnp.zeros((BLOCKS, LANES), BF)


def prepare(me, shard, second, small):
    small = [values.reshape(1, -1) for values in small]
    return pallas(
        prepare_kernel,
        in_specs=[SMEM, fixed(*shard.shape), fixed(*second.shape)] + [fixed(*values.shape) for values in small],
        out_specs=fixed(BLOCKS, 4 * D + 2 * LANES),
        out_shape=jax.ShapeDtypeStruct((BLOCKS, 4 * D + 2 * LANES), BF),
        scratch_shapes=[pltpu.VMEM((8, 3 * LANES), F32), pltpu.VMEM((BLOCKS, LANES), F32)],
        cost_estimate=cost(2),
        name="prepare",
        near="all",
        far_in=range(1, 11),
        operands=(me, shard, second, *small),
    )


def table_of(lines, table):
    row = line = 0
    values = lines.astype(F32)
    table[...] = jnp.zeros_like(table)
    for count, length in zip(LINES, LENGTHS):
        spans = []
        for group in range(BLOCKS // 4):
            blocks = [(4 * group + member) * BLOCKS + line for member in range(4)]
            if length == LANES:
                spans += [values[block : block + 1, :] for block in blocks]
            else:
                for part in range(count):
                    spans.append(sum((values[block + part : block + part + 1, :] for block in blocks[1:]), values[blocks[0] + part : blocks[0] + part + 1, :]))
        for begin in range(0, len(spans), D // LANES):
            table[row : row + 1, :] = jnp.concatenate(spans[begin : begin + D // LANES], 1)
            row += 1
        line += count


def project_kernel(layout_of, me_ref, tokens, cosine, sine, *rest):
    refs = rest[: len(layout_of)]
    normed_kept, normed_sent, qkv_out, table, weight, lines, normed_out, turned, sem, lines_sem = rest[len(layout_of) :]
    step = pl.program_id(0)

    @pl.when(step == 0)
    def _():
        fetch(me_ref[0], layout_of, refs, (4 * D, 4 * D + LANES), lines, lines_sem)
        fetch(me_ref[0], layout_of, refs, (0, 3 * D), weight, sem)
        arrive(lines, lines_sem)
        table_of(lines[...], table)
        gain, shift = table[GAIN_ONE : GAIN_ONE + 1, :], table[SHIFT_ONE : SHIFT_ONE + 1, :]
        for begin in range(0, tokens.shape[0], ROWS):
            part = slice(begin, begin + ROWS)
            unit, _ = normed(tokens[part, :].astype(F32))
            normed_out[part, :] = (unit * gain + shift).astype(BF)
        turn_out(me_ref[0], normed_out[...], normed_kept, normed_sent, turned)
        arrive(weight, sem)

    column = pl.multiple_of(step * TILE, TILE)
    heads_tiles = D // TILE
    bias = table[pl.ds(QKV_B + step // heads_tiles, 1), pl.ds(pl.multiple_of(step % heads_tiles * TILE, TILE), TILE)]

    @pl.when(step < 2 * heads_tiles)
    def _():
        scale = jnp.where(step < heads_tiles, HEAD**-0.5, 1.0).astype(F32)
        for begin in range(0, tokens.shape[0], ROWS):
            part = slice(begin, begin + ROWS)
            product = nn(normed_out[part, :], weight[:, pl.ds(column, TILE)]) + bias
            turned = product * wide(cosine[part, :], TILE) + partner(product) * wide(sine[part, :], TILE)
            qkv_out[part, :] = (turned * scale).astype(BF)

    @pl.when(step >= 2 * heads_tiles)
    def _():
        product = nn(normed_out[...], weight[:, pl.ds(column, TILE)]) + bias
        qkv_out[...] = product.astype(BF)


def project(me, tokens, cosine, sine, pieces, after=()):
    count = tokens.shape[0]
    layout_of = describe(pieces)
    return pallas(
        functools.partial(project_kernel, layout_of),
        grid=(3 * D // TILE,),
        in_specs=[SMEM, fixed(count, D), fixed(count, LANES), fixed(count, LANES)] + [ANY] * len(pieces),
        out_specs=[fixed(D // 2, count)] * 2 + [pl.BlockSpec((count, TILE), lambda step: (0, step)), fixed(TABLE, D)],
        out_shape=[jax.ShapeDtypeStruct((D // 2, count), BF)] * 2
        + [jax.ShapeDtypeStruct((count, 3 * D), BF), jax.ShapeDtypeStruct((TABLE, D), F32)],
        scratch_shapes=[
            pltpu.VMEM((D, 3 * D), BF),
            pltpu.VMEM((D, LANES), BF),
            pltpu.VMEM((count, D), BF),
            pltpu.VMEM((D, count), BF),
            pltpu.SemaphoreType.DMA,
            pltpu.SemaphoreType.DMA,
        ],
        cost_estimate=cost(16 / 4),
        name="project",
        far_in=(1, *range(4, 4 + len(pieces))),
        near=(1, 3),
        operands=(me, tokens, cosine, sine, *[array for _, _, array in pieces]),
        after=after,
    )


def line_of(table, line):
    return table[line : line + 1, :]


def branch_kernel(layout_of, me_ref, mixed, tokens, table, *rest):
    refs = rest[: len(layout_of)]
    resid, normed_two, normed_kept, normed_sent, mixed_kept, mixed_sent, weight, turned, sem = rest[len(layout_of) :]

    @pl.when(pl.program_id(0) == 0)
    def _():
        fetch(me_ref[0], layout_of, refs, (3 * D, 4 * D), weight, sem)
        arrive(weight, sem)

    value = tokens[...].astype(F32) + (nn(mixed[...], weight[...]) + line_of(table, OUT_B))
    resid[...] = value
    unit, _ = normed(value)
    low = (unit * line_of(table, GAIN_TWO) + line_of(table, SHIFT_TWO)).astype(BF)
    normed_two[...] = low
    turn_out(me_ref[0], low, normed_kept, normed_sent, turned)
    turn_out(me_ref[0], mixed[...], mixed_kept, mixed_sent, turned)


def branch(me, mixed, tokens, table, pieces, after=()):
    count = tokens.shape[0]
    layout_of = describe(pieces)
    rows = pl.BlockSpec((ROWS, D), lambda step: (step, 0))
    return pallas(
        functools.partial(branch_kernel, layout_of),
        grid=(count // ROWS,),
        in_specs=[SMEM, rows, rows, fixed(TABLE, D)] + [ANY] * len(pieces),
        out_specs=[rows, rows] + [pl.BlockSpec((D // 2, ROWS), lambda step: (0, step))] * 4,
        out_shape=[jax.ShapeDtypeStruct((count, D), F32), jax.ShapeDtypeStruct((count, D), BF)]
        + [jax.ShapeDtypeStruct((D // 2, count), BF)] * 4,
        scratch_shapes=[pltpu.VMEM((D, D), BF), pltpu.VMEM((D, ROWS), BF), pltpu.SemaphoreType.DMA],
        cost_estimate=cost(12 / 4),
        name="branch",
        far_in=(1, 2, *range(4, 4 + len(pieces))),
        near=(1, 3, 5),
            operands=(me, mixed, tokens, table, *[array for _, _, array in pieces],),
        after=after,
    )


def gelu_parts(value):
    decay = jnp.exp(-0.5 * value * value)
    point = 1.0 / (1.0 + (0.3275911 * 2.0**-0.5) * jnp.abs(value))
    series = 0.5 * 1.061405429
    for factor in (-1.453152027, 1.421413741, -0.284496736, 0.254829592):
        series = series * point + 0.5 * factor
    tail = series * point * decay
    return jnp.where(value >= 0, 1.0 - tail, tail), decay * (2.0 * np.pi) ** -0.5


def up_kernel(layout_of, me_ref, normed_two, table, *rest):
    refs = rest[: len(layout_of)]
    activ, slope, activ_sent, weight, sem = rest[len(layout_of) :]
    step = pl.program_id(0)

    @pl.when(step == 0)
    def _():
        fetch(me_ref[0], layout_of, refs, (0, FF), weight, sem)
        arrive(weight, sem)

    column = pl.multiple_of(step * TILE, TILE)
    tiles = D // TILE
    bias = table[pl.ds(UP_B + step // tiles, 1), pl.ds(pl.multiple_of(step % tiles * TILE, TILE), TILE)]
    rows = FF // BLOCKS
    odd = (me_ref[0] & 1) == 1
    parts = [slice(begin, begin + UP_ROWS) for begin in range(0, normed_two.shape[0], UP_ROWS)]

    def product(part):
        return nn(normed_two[part, :], weight[:, pl.ds(column, TILE)])

    ahead = product(parts[0])
    for number, part in enumerate(parts):
        value = ahead + bias
        if number + 1 < len(parts):
            ahead = product(parts[number + 1])
        share, density = gelu_parts(value)
        low = (value * share).astype(BF)
        activ[part, :] = low
        slope[part, :] = (share + value * density).astype(BF)
        pairs = [low[:, begin : begin + 2 * rows] for begin in range(0, TILE, 2 * rows)]
        sent = [jnp.where(odd, pair[:, :rows], pair[:, rows:]) for pair in pairs]
        activ_sent[part, :] = jnp.concatenate(sent, 1)


def up(me, normed_two, table, pieces, after=()):
    count = normed_two.shape[0]
    layout_of = describe(pieces)
    tile = pl.BlockSpec((count, TILE), lambda step: (0, step))
    return pallas(
        functools.partial(up_kernel, layout_of),
        grid=(FF // TILE,),
        in_specs=[SMEM, fixed(count, D), fixed(TABLE, D)] + [ANY] * len(pieces),
        out_specs=[tile, tile, pl.BlockSpec((count, TILE // 2), lambda step: (0, step))],
        out_shape=[jax.ShapeDtypeStruct((count, FF), BF)] * 2 + [jax.ShapeDtypeStruct((count, FF // 2), BF)],
        scratch_shapes=[pltpu.VMEM((D, FF), BF), pltpu.SemaphoreType.DMA],
        cost_estimate=cost(35 / 4),
        name="up",
        far_in=range(3, 3 + len(pieces)),
            operands=(me, normed_two, table, *[array for _, _, array in pieces],),
        after=after,
    )


def pre_kernel(slope, cotangent, weight, grad_pre, grad_bias):
    sums = jnp.zeros((1, WIDE_TILE), F32)
    for begin in range(0, slope.shape[0], ROWS):
        part = slice(begin, begin + ROWS)
        back = (nt(cotangent[part, :], weight[...]) * slope[part, :].astype(F32)).astype(BF)
        grad_pre[part, :] = back
        sums += jnp.sum(back.astype(F32), axis=0, keepdims=True)
    grad_bias[...] = sums


def pre(slope, cotangent, weight, after=()):
    count = slope.shape[0]
    tile = pl.BlockSpec((count, WIDE_TILE), lambda step: (0, step))
    return pallas(
        pre_kernel,
        grid=(FF // WIDE_TILE,),
        in_specs=[tile, fixed(count, D), pl.BlockSpec((WIDE_TILE, D), lambda step: (step, 0))],
        out_specs=[tile, pl.BlockSpec((1, WIDE_TILE), lambda step: (0, step))],
        out_shape=[jax.ShapeDtypeStruct((count, FF), BF), jax.ShapeDtypeStruct((1, FF), F32)],
        cost_estimate=cost(15),
        name="pre",
        far_in=(0, 1, 2),
        operands=(slope, cotangent, weight),
        after=after,
    )


def output_kernel(activ, resid, table, weight, *rest):
    output, total = rest[-2:]
    step = pl.program_id(0)

    @pl.when(step == 0)
    def _():
        total[...] = resid[...] + line_of(table, DOWN_B)

    total[...] += nn(activ[...], weight[...])

    @pl.when(step == pl.num_programs(0) - 1)
    def _():
        output[...] = total[...].astype(BF)


def output_rows(activ, resid, table, weight, part, parts, before=(), after=()):
    count = activ.shape[0]
    rows = count // parts
    wide_tile = WIDE_TILE
    mine = pl.BlockSpec((rows, D), lambda step: (part, 0))
    return pallas(
        output_kernel,
        grid=(FF // wide_tile,),
        in_specs=[
            pl.BlockSpec((rows, wide_tile), lambda step: (part, step)),
            mine,
            fixed(TABLE, D),
            pl.BlockSpec((wide_tile, D), lambda step: (step, 0)),
        ]
        + [ANY] * len(before),
        out_specs=mine,
        out_shape=jax.ShapeDtypeStruct((count, D), BF),
        scratch_shapes=[pltpu.VMEM((rows, D), F32)],
        input_output_aliases={4 + place: place for place in range(len(before))},
        cost_estimate=cost(16 // parts),
        name="output",
        far_in=(0, 1, 3),
        operands=(activ, resid, table, weight, *before),
        after=after,
    )


def tn(left, right):
    return lax.dot_general(left, right, (((0,), (0,)), ((), ())), preferred_element_type=F32)


def outer_rows_kernel(me_ref, *refs):
    own, other, (right, right_other), sides, grad_bias = refs[:4], refs[4:8], refs[8:10], refs[10:14], refs[14]
    step = pl.program_id(0)
    half = right.shape[1] // 2

    def group(blocks):
        return jnp.concatenate([ref[...] for ref in blocks], 1)

    product = tn(group(own), right[...]) + tn(group(other), right_other[...])
    for side in range(2):
        bit = (step >> (1 - side)) & 1
        values = product[:, side * half : (side + 1) * half]

        @pl.when(bit == 0)
        def _():
            sides[2 * side][...] = values

        @pl.when(bit == 1)
        def _():
            sides[2 * side + 1][...] = values.astype(BF)

    @pl.when(step == 0)
    def _():
        grad_bias[...] = jnp.sum(right[...].astype(F32), axis=0, keepdims=True)


def outer_rows(me, left, left_other, right, right_other, after=()):
    count, size = left_other.shape
    width = right.shape[1]
    rows = FF // BLOCKS
    block = (4 * rows, width // 2)
    own = [
        pl.BlockSpec((count, rows), lambda step, me, z=z: (0, me[0] ^ (2 * (4 * step + z)))) for z in range(4)
    ]
    other = [
        pl.BlockSpec((count, rows), lambda step, me, z=z: (0, (me[0] >> 1) ^ (4 * step + z))) for z in range(4)
    ]
    return pallas(
        outer_rows_kernel,
        grid=(4,),
        prefetch=1,
        in_specs=own + other + [fixed(count, width)] * 2,
        out_specs=[
            pl.BlockSpec(block, lambda step, me: (jnp.minimum(step, 1), 0)),
            pl.BlockSpec(block, lambda step, me: (jnp.maximum(step - 2, 0), 0)),
            pl.BlockSpec(block, lambda step, me: (step // 2, 0)),
            pl.BlockSpec(block, lambda step, me: (step // 2, 0)),
            fixed(1, width),
        ],
        out_shape=[jax.ShapeDtypeStruct((size // 2, width // 2), kind) for kind in (F32, BF, F32, BF)]
        + [jax.ShapeDtypeStruct((1, width), F32)],
        cost_estimate=cost(16),
        name="outer_rows",
        far_in=range(1, 11),
        near=(0, 1, 2, 3),
        operands=(me, *[left] * 4, *[left_other] * 4, right, right_other),
        after=after,
    )


def outer_kernel(tiles, parts, *refs):
    sides, grad_bias = refs[-5:-1], refs[-1]
    step = pl.program_id(0)
    for begin, end, *places in parts:
        left, left_other, right, right_other = [refs[place] for place in places]
        rows = left.shape[0] // (BLOCKS // 2)

        @pl.when((step >= begin) & (step < end))
        def _():
            product = nn(left[...], right[...]) + nn(left_other[...], right_other[...])
            for side in range(2):

                @pl.when((step >= tiles // 2) == bool(side))
                def _():
                    for which, positions in enumerate(parted(list(range(BLOCKS // 2)), UPPER[side][0] >> 1)):
                        target = sides[2 * side + which]
                        for position, first, length in runs_of(positions):
                            part = product[first * rows : (first + length) * rows, :]
                            target[position * rows : (position + length) * rows, :] = part.astype(target.dtype)

            grad_bias[...] = jnp.sum(right[...].astype(F32), axis=0, keepdims=True)


def outer(sets, tile_width, after=(), free=()):
    size, count = sets[0][0].shape
    parts, tiles, operands, in_specs = [], 0, [], []

    def take(array, spec):
        for place, known in enumerate(operands):
            if known is array:
                return place
        operands.append(array)
        in_specs.append(spec)
        return len(operands) - 1

    for left, left_other, right, right_other in sets:
        begin, end = tiles, tiles + right.shape[1] // tile_width

        def tile_of(step, begin=begin, end=end):
            return 0, jnp.clip(step - begin, 0, end - begin - 1)

        spec = pl.BlockSpec((count, tile_width), tile_of)
        places = [take(each, fixed(size, count)) for each in (left, left_other)]
        places += [take(each, spec) for each in (right, right_other)]
        parts.append((begin, end, *places))
        tiles = end

    width = tiles * tile_width
    block = (size // 2, tile_width)
    firsts = pl.BlockSpec(block, lambda step: (0, jnp.minimum(step, tiles // 2 - 1)))
    seconds = pl.BlockSpec(block, lambda step: (0, jnp.maximum(step - tiles // 2, 0)))
    return pallas(
        functools.partial(outer_kernel, tiles, parts),
        grid=(tiles,),
        in_specs=in_specs,
        out_specs=[firsts, firsts, seconds, seconds, pl.BlockSpec((1, tile_width), lambda step: (0, step))],
        out_shape=[jax.ShapeDtypeStruct((size // 2, width // 2), kind) for kind in (F32, BF, F32, BF)]
        + [jax.ShapeDtypeStruct((1, width), F32)],
        cost_estimate=cost(4 * count * size * width / 0.55e9),
        name="outer",
        far_in=[place for place, array in enumerate(operands) if not any(array is each for each in free)],
        near=(0, 1, 2, 3),
        operands=tuple(operands),
        after=after,
    )


def branch_back_kernel(layout_of, out_layout, me_ref, grad_pre, resid, cotangent, table, *rest):
    refs, rest = rest[: len(layout_of)], rest[len(layout_of) :]
    out_refs, rest = rest[: len(out_layout)], rest[len(out_layout) :]
    grad_resid, grad_branch, grad_mixed, grad_gain, grad_shift, grad_bias, up_weight, out_weight, up_sem, out_sem = rest

    @pl.when(pl.program_id(0) == 0)
    def _():
        fetch(me_ref[0], layout_of, refs, (0, FF), up_weight, up_sem)
        fetch(me_ref[0], out_layout, out_refs, (3 * D, 4 * D), out_weight, out_sem)
        grad_gain[...] = jnp.zeros_like(grad_gain)
        grad_shift[...] = jnp.zeros_like(grad_shift)
        grad_bias[...] = jnp.zeros_like(grad_bias)
        arrive(up_weight, up_sem)

    upstream = nt(grad_pre[...], up_weight[...])
    back, gain_part, shift_part = norm_back(resid[...], line_of(table, GAIN_TWO), upstream)
    total = cotangent[...].astype(F32) + back
    low = total.astype(BF)
    grad_resid[...] = total
    grad_branch[...] = low
    grad_gain[...] += gain_part
    grad_shift[...] += shift_part
    grad_bias[...] += jnp.sum(low.astype(F32), axis=0, keepdims=True)

    @pl.when(pl.program_id(0) == 0)
    def _():
        arrive(out_weight, out_sem)

    grad_mixed[...] = nt(low, out_weight[...]).astype(BF)


def branch_back(me, grad_pre, resid, cotangent, table, pieces, out_pieces, after=()):
    count = resid.shape[0]
    layout_of, out_layout = describe(pieces), describe(out_pieces)
    rows = pl.BlockSpec((ROWS, D), lambda step: (step, 0))
    vector = jax.ShapeDtypeStruct((1, D), F32)
    return pallas(
        functools.partial(branch_back_kernel, layout_of, out_layout),
        grid=(count // ROWS,),
        in_specs=[SMEM, pl.BlockSpec((ROWS, FF), lambda step: (step, 0)), rows, rows, fixed(TABLE, D)]
        + [ANY] * (len(pieces) + len(out_pieces)),
        out_specs=[rows, rows, rows] + [fixed(1, D)] * 3,
        out_shape=[
            jax.ShapeDtypeStruct((count, D), F32),
            jax.ShapeDtypeStruct((count, D), BF),
            jax.ShapeDtypeStruct((count, D), BF),
            vector,
            vector,
            vector,
        ],
        scratch_shapes=[
            pltpu.VMEM((D, FF), BF),
            pltpu.VMEM((D, D), BF),
            pltpu.SemaphoreType.DMA,
            pltpu.SemaphoreType.DMA,
        ],
        cost_estimate=cost(21),
        name="branch_back",
        far_in=(1, 2, 3, *range(5, 5 + len(pieces) + len(out_pieces))),
        near=(1, 2),
            operands=(me, grad_pre, resid, cotangent, table, *[array for _, _, array in (*pieces, *out_pieces)],),
        after=after,
    )


def tokens_back_kernel(layout_of, chunks, me_ref, *rest):
    grads, rest = rest[:chunks], rest[chunks:]
    tokens, grad_resid, table, out_bias, up_bias, down_bias, gain_two, shift_two = rest[:8]
    refs = rest[8 : 8 + len(layout_of)]
    grad_tokens, grad_table, weight, sem = rest[8 + len(layout_of) :]

    @pl.when(pl.program_id(0) == 0)
    def _():
        fetch(me_ref[0], layout_of, refs, (0, 3 * D), weight, sem)
        grad_table[...] = jnp.zeros_like(grad_table)
        for ref, row in ((out_bias, OUT_B), (down_bias, DOWN_B), (gain_two, GAIN_TWO), (shift_two, SHIFT_TWO)):
            grad_table[row : row + 1, :] = ref[...]
        for part in range(FF // D):
            grad_table[UP_B + part : UP_B + part + 1, :] = up_bias[:, part * D : (part + 1) * D]
        arrive(weight, sem)

    quads = [(ref, begin) for ref in grads for begin in range(0, ref.shape[1], 3 * QUAD)]
    ordered = jnp.concatenate(
        [ref[:, begin + part * QUAD : begin + (part + 1) * QUAD] for part in range(3) for ref, begin in quads], 1
    )
    for part in range(3):
        sums = jnp.sum(ordered[:, part * D : (part + 1) * D].astype(F32), axis=0, keepdims=True)
        grad_table[QKV_B + part : QKV_B + part + 1, :] += sums
    back, gain_part, shift_part = norm_back(
        tokens[...].astype(F32), line_of(table, GAIN_ONE), nt(ordered, weight[...])
    )
    grad_tokens[...] = (grad_resid[...] + back).astype(BF)
    grad_table[GAIN_ONE : GAIN_ONE + 1, :] += gain_part
    grad_table[SHIFT_ONE : SHIFT_ONE + 1, :] += shift_part


def tokens_back(me, grads, tokens, grad_resid, table, biases, pieces, after=()):
    count = tokens.shape[0]
    layout_of = describe(pieces)
    rows = pl.BlockSpec((ROWS, D), lambda step: (step, 0))
    return pallas(
        functools.partial(tokens_back_kernel, layout_of, len(grads)),
        grid=(count // ROWS,),
        in_specs=[SMEM]
        + [pl.BlockSpec((ROWS, part.shape[1]), lambda step: (step, 0)) for part in grads]
        + [rows, rows, fixed(TABLE, D)]
        + [fixed(*part.shape) for part in biases]
        + [ANY] * len(pieces),
        out_specs=[rows, fixed(TABLE, D)],
        out_shape=[jax.ShapeDtypeStruct((count, D), BF), jax.ShapeDtypeStruct((TABLE, D), F32)],
        scratch_shapes=[pltpu.VMEM((D, 3 * D), BF), pltpu.SemaphoreType.DMA],
        cost_estimate=cost(15),
        name="tokens_back",
        far_in=range(len(grads) + 1, len(grads) + 3),
        operands=(me, *grads, tokens, grad_resid, table, *biases, *[array for _, _, array in pieces]),
        after=after,
    )


def finish_kernel(lengths, terms, number, *refs):
    weights, sums, outs = refs[:8], refs[8 : 8 + terms], refs[8 + terms :]
    for chunk in range(2):
        arrived = weights[4 * chunk : 4 * chunk + 4]
        for half in range(2):
            for part in range(3):
                source = slice((3 * half + part) * QUAD, (3 * half + part + 1) * QUAD)
                target = part * D + (2 * chunk + half) * QUAD
                total = arrived[0][:, source]
                for ref in arrived[1:]:
                    total = total + ref[:, source].astype(F32)
                outs[0][:, target : target + QUAD] = total
    row = 0
    for place, (length, lines) in enumerate(lengths):
        place_in = number[0] * length
        wide_row = jnp.concatenate(
            [sum(line_of(ref, row + line) for ref in sums) for line in range(lines)], 1
        )
        wide_row = jnp.broadcast_to(wide_row, (8, lines * D))
        turned = pltpu.roll(wide_row, lines * D - place_in, 1)
        outs[1 + place][...] = turned[0:1, :length]
        row += lines


def finish(number, weights, total, sizes, count, after):
    lengths = [(size // count, size // D) for size in sizes]
    rows = weights[0].shape[0]
    return pallas(
        functools.partial(finish_kernel, lengths, len(total)),
        in_specs=[SMEM] + [fixed(*array.shape) for array in (*weights, *total)],
        out_specs=[fixed(rows, 3 * D)] + [fixed(1, length) for length, _ in lengths],
        out_shape=[jax.ShapeDtypeStruct((rows, 3 * D), F32)]
        + [jax.ShapeDtypeStruct((1, length), F32) for length, _ in lengths],
        cost_estimate=cost(3),
        name="finish",
        near="all",
        operands=(number, *weights, *total),
        after=after,
    )


def key_runs(positions, frames, patches):
    first, last = positions, positions + 1
    start = jnp.int32(0)
    for slot in range(frames.shape[1]):
        width = patches[0, slot] + 2
        size = frames[0, slot] * width
        offset = positions - start
        inside = (offset >= 0) & (offset < size)
        end = start + width + jnp.where(offset >= width, width, 0) + jnp.where(offset >= 2 * width, width, 0)
        first = jnp.where(inside, start, first)
        last = jnp.where(inside, end, last)
        start = start + size
    return first, last


def fill_mask(frames, patches, mask, runs):
    count = mask.shape[0]
    first, last = key_runs(lax.broadcasted_iota(jnp.int32, (1, count), 1), frames, patches)
    keys = lax.broadcasted_iota(jnp.int32, (count, count), 0)
    mask[...] = jnp.where((keys >= first) & (keys < last), 0.0, MASKED)
    for block in range(count // BQ):
        part = slice(block * BQ, (block + 1) * BQ)
        begin = jnp.min(first[:, part]) // BK
        needed = (jnp.max(last[:, part]) + (BK - 1)) // BK - begin
        length = jnp.int32(LENGTHS_OF_RUNS[-1])
        for size in LENGTHS_OF_RUNS[-2::-1]:
            length = jnp.where(needed <= size, size, length)
        runs[0, block] = jnp.minimum(begin, count // BK - length)
        runs[1, block] = length


def each_block(count, runs, work):
    @pl.loop(0, count // BQ)
    def _(block):
        for size in LENGTHS_OF_RUNS:

            @pl.when(runs[1, block] == size)
            def _():
                work(pl.multiple_of(block * BQ, BQ), pl.multiple_of(runs[0, block] * BK, BK), size * BK)


def pair_of(head):
    return slice(head // 2 * LANES, (head // 2 + 1) * LANES)


def one_head(pair_values, head):
    lane = lax.broadcasted_iota(jnp.int32, pair_values.shape, 1)
    return jnp.where(lane // HEAD == head, pair_values, jnp.zeros_like(pair_values))


def attend_kernel(frames, patches, queries, keys, values, *rest):
    mixed, log_totals, mask, turned, runs = rest[-5:]
    count = queries.shape[0]

    @pl.when(pl.program_id(0) == 0)
    def _():
        fill_mask(frames, patches, mask, runs)

    turned[...] = values[...].T

    heads = queries.shape[1] // HEAD

    def work(row, key, size):
        block, span = pl.ds(row, BQ), pl.ds(key, size)
        bias = mask[span, block]
        scores = [
            nt(keys[span, pair_of(head)], one_head(queries[block, pair_of(head)], head % 2)) + bias
            for head in range(heads)
        ]
        results = []
        for head in range(heads):
            highest = jnp.max(scores[head], axis=0, keepdims=True)
            expo = jnp.exp(scores[head] - highest)
            totals = jnp.sum(expo, axis=0, keepdims=True)
            result = nn(turned[head * HEAD : (head + 1) * HEAD, span], expo.astype(BF))
            results.append(result * (1.0 / totals))
            log_totals[head : head + 1, block] = highest + jnp.log(totals)
        mixed[block, :] = jnp.concatenate(results, 0).T.astype(BF)

    each_block(count, runs, work)


QUAD = 4 * HEAD
QUADS = HEADS // 4


def attend(frames, patches, qkv, after=()):
    count = qkv.shape[0]
    groups, wide_block = QUADS // 2, 2 * QUAD

    def columns(part):
        return pl.BlockSpec((count, wide_block), lambda step: (0, part * groups + step))

    (mixed, log_totals), token = pallas(
        attend_kernel,
        grid=(groups,),
        in_specs=[SMEM, SMEM, columns(0), columns(1), columns(2)],
        out_specs=[columns(0), pl.BlockSpec((None, 8, count), lambda step: (step, 0, 0))],
        out_shape=[jax.ShapeDtypeStruct((count, D), BF), jax.ShapeDtypeStruct((groups, 8, count), F32)],
        scratch_shapes=[
            pltpu.VMEM((count, count), F32),
            pltpu.VMEM((wide_block, count), BF),
            pltpu.SMEM((2, count // BQ), jnp.int32),
        ],
        cost_estimate=cost(26 / 4),
        name="attend",
        far_in=(2, 3, 4),
        vmem=ATTEND_BYTES,
        operands=(frames, patches, qkv, qkv, qkv),
        after=after,
    )
    return (mixed, log_totals.reshape(QUADS, 4, count)), token


def attend_back_kernel(
    frames,
    patches,
    queries,
    keys,
    values,
    mixed,
    grads,
    log_totals,
    cosine,
    sine,
    grad_projected,
    mask,
    turned,
    grad_keys,
    grad_values,
    inner,
    runs,
):
    count = queries.shape[0]

    @pl.when(pl.program_id(0) == 0)
    def _():
        fill_mask(frames, patches, mask, runs)

    turned[...] = keys[...].T
    grad_keys[...] = jnp.zeros_like(grad_keys)
    grad_values[...] = jnp.zeros_like(grad_values)
    product = mixed[...].astype(F32) * grads[...].astype(F32)
    own = (
        lax.broadcasted_iota(jnp.int32, (8, QUAD), 1) // HEAD == lax.broadcasted_iota(jnp.int32, (8, QUAD), 0)
    ).astype(F32)
    inner[...] = lax.dot_general(
        own, product, (((1,), (1,)), ((), ())), precision=lax.Precision.HIGHEST, preferred_element_type=F32
    )

    def work(row, key, size):
        block, span = pl.ds(row, BQ), pl.ds(key, size)
        bias = mask[span, block]
        heads = range(QUAD // HEAD)
        rows = [one_head(queries[block, pair_of(head)], head % 2) for head in heads]
        rows_grads = [one_head(grads[block, pair_of(head)], head % 2) for head in heads]
        shares = [nt(keys[span, pair_of(head)], rows[head]) + bias for head in heads]
        changes = [nt(values[span, pair_of(head)], rows_grads[head]) for head in heads]
        probs, grad_scores, grad_rows = [], [], []
        for head in heads:
            share = jnp.exp(shares[head] - log_totals[head : head + 1, block])
            change = (share * (changes[head] - inner[head : head + 1, block])).astype(BF)
            grad_rows.append(nn(turned[head * HEAD : (head + 1) * HEAD, span], change))
            probs.append(share.astype(BF))
            grad_scores.append(change)
        for pair in range(QUAD // LANES):
            lanes, two = slice(pair * LANES, (pair + 1) * LANES), slice(2 * pair, 2 * pair + 2)
            grad_values[span, lanes] += nn(jnp.concatenate(probs[two], 1), jnp.concatenate(rows_grads[two], 0))
            grad_keys[span, lanes] += nn(jnp.concatenate(grad_scores[two], 1), jnp.concatenate(rows[two], 0))
        back = jnp.concatenate(grad_rows, 0).T * HEAD**-0.5
        back = back * wide(cosine[block, :], QUAD) - partner(back) * wide(sine[block, :], QUAD)
        grad_projected[block, :QUAD] = back.astype(BF)

    each_block(count, runs, work)
    back = grad_keys[...] * wide(cosine[...], QUAD) - partner(grad_keys[...]) * wide(sine[...], QUAD)
    grad_projected[:, QUAD : 2 * QUAD] = back.astype(BF)
    grad_projected[:, 2 * QUAD :] = grad_values[...].astype(BF)


def attend_back(frames, patches, qkv, mixed, grads, log_totals, cosine, sine, begin, quads, after=()):
    count = qkv.shape[0]

    def columns(part):
        return pl.BlockSpec((count, QUAD), lambda step: (0, part * QUADS + begin + step))

    return pallas(
        attend_back_kernel,
        grid=(quads,),
        in_specs=[
            SMEM,
            SMEM,
            columns(0),
            columns(1),
            columns(2),
            columns(0),
            columns(0),
            pl.BlockSpec((None, 4, count), lambda step: (begin + step, 0, 0)),
            fixed(count, LANES),
            fixed(count, LANES),
        ],
        out_specs=pl.BlockSpec((count, 3 * QUAD), lambda step: (0, step)),
        out_shape=jax.ShapeDtypeStruct((count, 3 * QUAD * quads), BF),
        scratch_shapes=[
            pltpu.VMEM((count, count), F32),
            pltpu.VMEM((QUAD, count), BF),
            pltpu.VMEM((count, QUAD), F32),
            pltpu.VMEM((count, QUAD), F32),
            pltpu.VMEM((8, count), F32),
            pltpu.SMEM((2, count // BQ), jnp.int32),
        ],
        cost_estimate=cost(15 * quads),
        name="attend_back",
        far_in=(2, 3, 4, 5),
        near=(0,),
            operands=(frames, patches, qkv, qkv, qkv, mixed, grads, log_totals, cosine, sine,),
        after=after,
    )


def positions_of(frames, patches):
    frame_tokens = patches + 2
    clip_tokens = frames * frame_tokens
    clip_starts = jnp.cumsum(clip_tokens) - clip_tokens
    positions = jnp.arange(TOK_DEV, dtype=jnp.int32)
    inside = (
        (positions[None, :] >= clip_starts[:, None])
        & (positions[None, :] < (clip_starts + clip_tokens)[:, None])
    ).astype(jnp.int32)
    begins = jnp.sum(inside * clip_starts[:, None], axis=0)
    widths = jnp.maximum(jnp.sum(inside * frame_tokens[:, None], axis=0), 1)
    clip_sides = jnp.where(patches == SIDE_SMALL * SIDE_SMALL, SIDE_SMALL, SIDE_LARGE).astype(jnp.int32)
    sides_rows = jnp.maximum(jnp.sum(inside * clip_sides[:, None], axis=0), 1)
    offsets = positions - begins
    frame_index = offsets // widths
    within = offsets % widths
    patch_index = jnp.maximum(within - 2, 0)
    row_index = jnp.where(within >= 2, patch_index // sides_rows, 0)
    col_index = jnp.where(within >= 2, patch_index % sides_rows, 0)
    return frame_index, row_index, col_index


def rotary_tables(places):
    pair_count = HEAD // 2
    time_pairs = pair_count // 3
    row_pairs = (pair_count - time_pairs) // 2
    pair_ranks = np.arange(pair_count)
    group_ids = np.where(pair_ranks < time_pairs, 0, np.where(pair_ranks < time_pairs + row_pairs, 1, 2))
    group_first = np.array([0, time_pairs, time_pairs + row_pairs])[group_ids]
    group_sizes = np.array([time_pairs, row_pairs, pair_count - time_pairs - row_pairs])[group_ids]
    rate_table = 10000.0 ** (-(pair_ranks - group_first) / group_sizes)
    angles = jnp.zeros((TOK_DEV, pair_count), F32)
    for group_id, place in enumerate(places):
        table = jnp.asarray(np.where(group_ids == group_id, rate_table, 0.0), F32)
        angles = angles + place.astype(F32)[:, None] * table[None, :]
    cosine, sine = jnp.cos(angles), jnp.sin(angles)
    return jnp.concatenate([cosine] * 4, 1), jnp.concatenate([-sine, sine] * 2, 1)


def by_side(made):
    return (made[0], made[1]), (made[2], made[3])


def local(
    count,
    tokens,
    clip_frames,
    clip_patches,
    qkv_weight,
    qkv_bias,
    out_weight,
    out_bias,
    up_weight,
    up_bias,
    down_weight,
    down_bias,
    norm1_gain,
    norm1_shift,
    norm2_gain,
    norm2_shift,
    cotangent,
):
    net = Net(count)
    me_ref = net.me.reshape(1)
    small = (qkv_bias, out_bias, up_bias, down_bias, norm1_gain, norm1_shift, norm2_gain, norm2_shift)
    sizes = [item.shape[0] * count for item in small]
    clips = (clip_frames, clip_patches)

    joined, _ = prepare(me_ref, net.widen(qkv_weight), net.widen(out_weight), [net.widen(values) for values in small])
    first = Gather(net, joined)
    middle_shard = net.widen(up_weight)
    cosine, sine = rotary_tables(positions_of(clip_frames[0], clip_patches[0]))

    def copy_of(shard):
        def put(relay):
            relay.put(relay.make(*shard.shape, BF), 0, 0, *shard.shape, [(shard, 0, 0)])

        return put

    made, _ = advance([first], extra=copy_of(middle_shard))
    middle = Gather(net, made[0])
    advance([first], after=[middle.held[0][1]])
    first.finish()
    made, token = advance([middle], after=first.arrivals(), extra=copy_of(down_weight))
    final = lax.all_gather(made[0], AXES, axis=0, tiled=True)
    (normed_kept, normed_sent, qkv, table), token = project(
        me_ref, tokens, cosine, sine, first.pieces, after=[token]
    )
    normed_other = net.swap(normed_sent, 1)
    _, token = advance([middle], after=[token])
    (mixed, log_totals), token = attend(*clips, qkv, after=[token])
    cotangent_other = net.swap(cotangent, 1)
    (resid, normed_two, two_kept, two_sent, mixed_kept, mixed_sent), token = branch(
        me_ref, mixed, tokens, table, [piece for piece in first.pieces if piece[0] == 1], after=[token]
    )
    token = middle.finish([token])
    two_other, mixed_other = net.swap(two_sent, 1), net.swap(mixed_sent, 1)
    (activ, slope, activ_sent), token = up(me_ref, normed_two, table, middle.pieces, after=[token])
    activ_other = net.swap(activ_sent, 1)
    (grad_pre, grad_up_bias), token = pre(slope, cotangent, final, after=[token])
    grad_pre_other = net.swap(grad_pre, 1)
    (*sides, grad_down_bias), token = outer_rows(
        me_ref, activ, activ_other, cotangent, cotangent_other, after=[token]
    )
    moving_down = Scatter(net, by_side(sides))
    (grad_resid, grad_branch, grad_mixed, grad_gain_two, grad_shift_two, grad_out_bias), token = branch_back(
        me_ref, grad_pre, resid, cotangent, table, middle.pieces, first.pieces[4:], after=[token]
    )
    grad_branch_other = net.swap(grad_branch, 1)
    _, token = advance([moving_down], after=[token])
    (*sides, _), token = outer(
        [(mixed_kept, mixed_other, grad_branch, grad_branch_other), (two_kept, two_other, grad_pre, grad_pre_other)],
        TILE,
        after=[token],
        free=(grad_branch, grad_branch_other),
    )
    moving_up = Scatter(net, by_side(sides), (D, FF))
    parts, others, moving_qkv = [], [], []

    def back(quad, token):
        part, token = attend_back(
            *clips, qkv, mixed, grad_mixed, log_totals, cosine, sine, quad, 1, after=[token]
        )
        parts.append(part)
        others.append(net.swap(part, 1))
        return token

    def weigh(quads, token):
        sets = [(normed_kept, normed_other, parts[quad], others[quad]) for quad in quads]
        (*sides, _), token = outer(sets, 3 * QUAD, after=[token], free=(*parts, *others))
        moving_qkv.append(Scatter(net, by_side(sides)))
        return token

    token = back(0, token)
    _, token = advance([moving_down], after=[token])
    token = back(1, token)
    _, token = advance([moving_up], after=[token])
    token = back(2, token)
    _, token = advance([moving_up, moving_down], after=[token])
    token = weigh([0, 1], token)
    token = back(3, token)
    _, token = advance([moving_qkv[0]], after=[token])
    (grad_tokens, grad_table), token = tokens_back(
        me_ref,
        parts,
        tokens,
        grad_resid,
        table,
        (grad_out_bias, grad_up_bias, grad_down_bias, grad_gain_two, grad_shift_two),
        first.pieces,
        after=[token],
    )
    total = Sum(net, grad_table)
    _, token = advance([moving_qkv[0], moving_up], after=[token])
    token = weigh([2, 3], token)
    _, token = advance([total], after=[token, *moving_qkv[0].held[1:]])
    output, token = output_rows(activ, resid, table, final, 0, 2, after=[token])
    _, token = advance([moving_qkv[1], total], after=[token])
    output, token = output_rows(activ, resid, table, final, 2, 4, [output], after=[token])
    _, token = advance([moving_qkv[1], total], after=[token])
    output, token = output_rows(activ, resid, table, final, 3, 4, [output], after=[token])
    (grad_qkv_weight, *own), _ = finish(
        net.number.reshape(1), (*moving_qkv[0].held, *moving_qkv[1].held), total.finish(), sizes, count, [token]
    )
    own = [values.reshape(-1) for values in own]
    return (
        output,
        grad_tokens,
        net.narrow(grad_qkv_weight),
        own[0],
        moving_up.result[0],
        own[1],
        moving_up.result[1],
        own[2],
        moving_down.result[0],
        own[3],
        own[4],
        own[5],
        own[6],
        own[7],
    )


def solution(mesh):
    count = mesh.shape["fsdp"] * mesh.shape["dp"]
    rows, vector = P(AXES, None), P(AXES)
    placed = (rows, rows, rows, rows, vector, rows, vector, rows, vector, rows, vector) + (vector,) * 4 + (rows,)
    given = (rows, rows, rows, vector, rows, vector, rows, vector, rows) + (vector,) * 5
    return jax.shard_map(
        functools.partial(local, count), mesh=mesh, in_specs=placed, out_specs=given, check_vma=False
    )
```

```python
import functools

import jax
import jax.numpy as jnp
import numpy as np
from jax import lax
from jax.experimental import pallas as pl
from jax.experimental.pallas import tpu as pltpu
from jax.sharding import PartitionSpec as P

D = 1024
HEADS = 16
HEAD = 64
FF = 4096
SIDE_SMALL = 16
SIDE_LARGE = 24
TOK_DEV = 1024
AXES = ("fsdp", "dp")
EPSILON = 1e-06
MASKED = -1e30
BQ = 256
BK = 128
LENGTHS_OF_RUNS = (3, 5, 7, 8)
LANES = 128
TILE = 512
WIDE_TILE = 1024
ROWS = 256
UP_ROWS = 128
F32 = jnp.float32
BF = jnp.bfloat16
VMEM_BYTES = 28 << 20
ATTEND_BYTES = 40 << 20
WEIGHT = 1.15e10


def cost(microseconds):
    return pl.CostEstimate(flops=int(microseconds * WEIGHT), bytes_accessed=0, transcendentals=0)


def nt(left, right):
    return lax.dot_general(left, right, (((1,), (1,)), ((), ())), preferred_element_type=F32)


def nn(left, right):
    return jnp.dot(left, right, preferred_element_type=F32)


SMEM = pl.BlockSpec(memory_space=pltpu.SMEM)
ANY = pl.BlockSpec(memory_space=pl.ANY)


def fixed(*shape):
    return pl.BlockSpec(shape, lambda *_: (0,) * len(shape))


def far(*arrays):
    return [pltpu.with_memory_space_constraint(array, pltpu.HBM) for array in arrays]


def pallas(kernel, operands, in_specs, after=(), vmem=VMEM_BYTES, near=(), far_in=(), prefetch=0, **kept):
    given = len(operands)
    shapes, specs = kept.pop("out_shape"), kept.pop("out_specs")
    single = not isinstance(shapes, (list, tuple))
    shapes, specs = ([shapes], [specs]) if single else (list(shapes), list(specs))
    shapes = [
        shape if near == "all" or number in near else pltpu.HBM(shape.shape, shape.dtype)
        for number, shape in enumerate(shapes)
    ]
    operands = [
        far(array)[0] if number in far_in else array for number, array in enumerate(operands)
    ]
    waited = [each if each.shape == (8, LANES) else far(each)[0] for each in after]

    def body(*refs):
        outs = given + len(after)
        refs[outs + len(shapes)][...] = jnp.zeros((8, LANES), F32)
        kernel(*refs[:given], *refs[outs : outs + len(shapes)], *refs[outs + len(shapes) + 1 :])

    places = dict(in_specs=list(in_specs) + [ANY] * len(after), out_specs=specs + [fixed(8, LANES)])
    if prefetch:
        places |= dict(grid=kept.pop("grid"), scratch_shapes=kept.pop("scratch_shapes", ()))
        places = dict(grid_spec=pltpu.PrefetchScalarGridSpec(num_scalar_prefetch=prefetch, **places))
    *made, token = pl.pallas_call(
        body,
        **places,
        out_shape=shapes + [jax.ShapeDtypeStruct((8, LANES), F32)],
        compiler_params=pltpu.CompilerParams(vmem_limit_bytes=vmem),
        **kept,
    )(*operands, *waited)
    return (made[0] if single else made), token


def hold(arrays, after):
    return pallas(
        lambda *refs: None,
        arrays,
        [ANY] * len(arrays),
        after,
        out_specs=[ANY] * len(arrays),
        out_shape=[jax.ShapeDtypeStruct(array.shape, array.dtype) for array in arrays],
        input_output_aliases={place: place for place in range(len(arrays))},
        far_in=range(len(arrays)),
        cost_estimate=cost(1),
        name="hold",
    )


class Relay:
    def __init__(self):
        self.inputs, self.outs, self.jobs = [], [], []

    def take(self, array):
        for place, known in enumerate(self.inputs):
            if known is array:
                return place
        self.inputs.append(array)
        return len(self.inputs) - 1

    def make(self, rows, columns, dtype):
        self.outs.append(((rows, columns), dtype))
        return len(self.outs) - 1

    def put(self, out, row, column, rows, columns, terms):
        self.jobs.append((out, row, column, rows, columns, [(self.take(array), *at) for array, *at in terms]))

    def run(self, after=(), name="relay"):
        jobs, given = self.jobs, len(self.inputs)

        def kernel(*refs):
            sources, targets = refs[:given], refs[given:]
            for out, row, column, rows, columns, terms in jobs:
                step = next(size for size in (64, 32, 16) if rows % size == 0)

                @pl.loop(0, rows // step)
                def _(index):
                    def part(ref, row, column):
                        begin = pl.multiple_of(row + index * step, 16)
                        return ref.at[pl.ds(begin, step), column : column + columns]

                    total = part(sources[terms[0][0]], *terms[0][1:])[...]
                    for source, *at in terms[1:]:
                        total = total.astype(F32) + part(sources[source], *at)[...].astype(F32)
                    part(targets[out], row, column)[...] = total.astype(targets[out].dtype)

        moved = sum(2 * shape[0] * shape[1] * 3 for shape, _ in self.outs)
        return pallas(
            kernel,
            self.inputs,
            [fixed(*array.shape) for array in self.inputs],
            after,
            out_specs=[fixed(*shape) for shape, _ in self.outs],
            out_shape=[jax.ShapeDtypeStruct(shape, dtype) for shape, dtype in self.outs],
            cost_estimate=cost(1 + moved * 0.4e-6),
            name=name,
            near="all",
        )


BLOCKS = 32
UPPER = ((16, 8), (8, 16))


class Net:
    def __init__(self, count):
        self.count, self.share = count, max(count // BLOCKS, 1)
        self.number = lax.axis_index(AXES).astype(jnp.int32)
        self.me = self.number // self.share

    def swap(self, value, mask):
        return self.permute(value, mask * self.share)

    def permute(self, value, mask):
        return lax.ppermute(value, AXES, [(number, number ^ mask) for number in range(self.count)])

    def bits(self):
        return [1 << place for place in range(self.share.bit_length() - 1)]

    def widen(self, shard):
        for bit in self.bits():
            other = self.permute(shard, bit)
            shard = jnp.where(
                self.number & bit, jnp.concatenate([other, shard], 0), jnp.concatenate([shard, other], 0)
            )
        return shard

    def narrow(self, total):
        for bit in self.bits()[::-1]:
            low, high = jnp.split(total, 2, 0)
            own = jnp.where(self.number & bit, high, low)
            total = own + self.permute(jnp.where(self.number & bit, low, high), bit)
        return total

    def over_all(self, value):
        for place in range(self.count.bit_length() - 1):
            value = value + self.permute(value, 1 << place)
        return value


def runs_of(places):
    runs = []
    for position, place in enumerate(places):
        if runs and runs[-1][1] + runs[-1][2] == place:
            runs[-1][2] += 1
        else:
            runs.append([position, place, 1])
    return runs


def parted(places, mask):
    return [[position for position, place in enumerate(places) if bool(place & mask) == with_it] for with_it in (False, True)]


class Gather:
    def __init__(self, net, shard):
        self.net, self.rows, self.half = net, shard.shape[0], shard.shape[1] // 2
        self.blocks = [[0, 2, 4, 6]] * 2
        self.stage = 0
        self.held = [[shard] + [net.swap(shard, mask) for mask in (2, 4, 6)]] * 2

    def join(self, relay):
        self.made = []
        for side in range(2):
            size = self.held[side][0].shape[0]
            self.made.append(relay.make(len(self.held[side]) * size, self.half, BF))
            column = side * self.half if self.stage == 0 else 0
            for place, array in enumerate(self.held[side]):
                relay.put(self.made[side], place * size, 0, size, self.half, [(array, 0, column)])
            if self.stage == 1:
                self.blocks[side] = self.blocks[side] + [block ^ UPPER[side][0] for block in self.blocks[side]]

    def follow(self, made):
        arrays = [made[place] for place in self.made]
        self.held = [(array, self.net.swap(array, UPPER[side][self.stage])) for side, array in enumerate(arrays)]
        self.stage += 1
        if self.stage == 2:
            self.kept = [self.net.swap(array, 1) for array in arrays]

    def finish(self, after=()):
        come, token = [come for _, come in self.held], None
        if after:
            come, token = hold(come, after)
        self.pieces = []
        for side in range(2):
            blocks = self.blocks[side]
            others = [block ^ UPPER[side][1] for block in blocks]
            self.pieces += [
                (side, blocks, self.held[side][0]),
                (side, [block ^ 1 for block in blocks], self.kept[side]),
                (side, others, come[side]),
                (side, [block ^ 1 for block in others], self.net.swap(come[side], 1)),
            ]
        return token

    def arrivals(self):
        return [array for held in self.held for array in held[1:]]


def whole(array):
    return [(0, None, array)]


class Scatter:
    def __init__(self, net, sides, widths=()):
        self.net = net
        self.stage = 0
        self.half = sides[0][0].shape[1]
        self.rows = sides[0][0].shape[0] // 8
        self.widths = widths or (2 * self.half,)
        self.held = [(stays, net.swap(leaves, UPPER[side][0])) for side, (stays, leaves) in enumerate(sides)]

    def join(self, relay):
        rows, half = self.rows, self.half
        self.made = []
        if self.stage == 0:
            for side, (own, come) in enumerate(self.held):
                for leaving in range(2):
                    self.made.append(relay.make(4 * rows, half, BF if leaving else F32))
                    first = 4 * rows * leaving
                    relay.put(self.made[-1], 0, 0, 4 * rows, half, [(own, first, 0), (come, first, 0)])
        elif self.stage == 1:
            for z in range(4):
                self.made.append(relay.make(rows, 2 * half, BF if z else F32))
                for side, (own, come) in enumerate(self.held):
                    relay.put(self.made[-1], 0, side * half, rows, half, [(own, z * rows, 0), (come, z * rows, 0)])
        else:
            column = 0
            for width in self.widths:
                self.made.append(relay.make(rows, width, F32))
                relay.put(self.made[-1], 0, 0, rows, width, [(array, 0, column) for array in self.held])
                column += width

    def follow(self, made):
        arrays = [made[place] for place in self.made]
        self.stage += 1
        if self.stage == 1:
            self.held = [(arrays[2 * side], self.net.swap(arrays[2 * side + 1], UPPER[side][1])) for side in range(2)]
        elif self.stage == 2:
            self.held = [arrays[0]] + [self.net.swap(arrays[z], 2 * z) for z in range(1, 4)]
        else:
            self.result = [self.net.narrow(array) for array in arrays]


class Sum:
    def __init__(self, net, value):
        self.net, self.value = net, value
        bits = [1 << place for place in range(net.count.bit_length() - 1)]
        self.groups = [(1,), (2, 4, 6)] + [(bit,) for bit in bits[3:]]
        self.send()

    def send(self):
        self.come = [self.net.permute(self.value, mask) for mask in self.groups.pop(0)]

    def join(self, relay):
        self.made = relay.make(*self.value.shape, self.value.dtype)
        relay.put(self.made, 0, 0, *self.value.shape, [(array, 0, 0) for array in (self.value, *self.come)])

    def follow(self, made):
        self.value = made[self.made]
        self.send()

    def finish(self):
        while self.groups:
            self.value = self.value + sum(self.come)
            self.send()
        return (self.value, *self.come)


def advance(moving, after=(), name="relay", extra=None):
    relay = Relay()
    if extra is not None:
        extra(relay)
    for each in moving:
        each.join(relay)
    made, token = relay.run(after, name)
    for each in moving:
        each.follow(made)
    return made, token


def fetch(me, pieces, refs, columns, target, sem):
    first, last = columns
    for (side, blocks, width, rows), ref in zip(pieces, refs):
        begin, end = max(first, side * width), min(last, (side + 1) * width)
        if begin >= end:
            continue
        if blocks is None:
            pltpu.make_async_copy(ref.at[:, pl.ds(begin, end - begin)], target, sem).start()
            continue
        for place, block in enumerate(blocks):
            row = pl.multiple_of((me ^ block) * rows, rows)
            pltpu.make_async_copy(
                ref.at[pl.ds(place * rows, rows), pl.ds(begin - side * width, end - begin)],
                target.at[pl.ds(row, rows), pl.ds(begin - first, end - begin)],
                sem,
            ).start()


def arrive(target, sem):
    pltpu.make_async_copy(target, target, sem).wait()


def describe(pieces):
    return [
        (side, blocks and tuple(blocks), array.shape[1], array.shape[0] // len(blocks or (0,)))
        for side, blocks, array in pieces
    ]


def normed(inputs):
    average = jnp.mean(inputs, axis=-1, keepdims=True)
    centred = inputs - average
    scale = lax.rsqrt(jnp.mean(centred * centred, axis=-1, keepdims=True) + EPSILON)
    return centred * scale, scale


def norm_back(inputs, gain, upstream):
    unit, scale = normed(inputs)
    scaled = gain * upstream
    back = scale * (
        scaled
        - jnp.mean(scaled, axis=-1, keepdims=True)
        - unit * jnp.mean(scaled * unit, axis=-1, keepdims=True)
    )
    return back, jnp.sum(upstream * unit, axis=0, keepdims=True), jnp.sum(upstream, axis=0, keepdims=True)


def partner(values):
    half = HEAD // 2
    lane = lax.broadcasted_iota(jnp.int32, values.shape, 1)
    return jnp.where(
        lane % HEAD < half,
        pltpu.roll(values, values.shape[1] - half, 1),
        pltpu.roll(values, half, 1),
    )


def wide(table, width):
    return jnp.concatenate([table] * (width // LANES), 1)


def turn_out(me, values, kept, sent, turned):
    turned[...] = values.T
    rows = D // BLOCKS
    for place in range(BLOCKS // 2):
        here = slice(place * rows, (place + 1) * rows)
        for target, parity in ((kept, 0), (sent, 1)):
            block = pl.multiple_of(((2 * place + parity) ^ me) * rows, rows)
            target[here, :] = turned[pl.ds(block, rows), :]


LINES = (3, 1, 1, 1, 1, 1, 1, 1)
LENGTHS = (96, 32, 128, 32, 32, 32, 32, 32)
QKV_B, OUT_B, UP_B, DOWN_B, GAIN_ONE, SHIFT_ONE, GAIN_TWO, SHIFT_TWO = 0, 3, 4, 8, 9, 10, 11, 12
TABLE = 16


def prepare_kernel(me_ref, shard, second, *rest):
    small, (joined, row, rows) = rest[:-3], rest[-3:]
    joined[:, : 3 * D] = shard[...]
    joined[:, 3 * D : 4 * D] = second[...]
    rows[...] = jnp.zeros_like(rows)
    line = 0
    for values, lines, length in zip(small, LINES, LENGTHS):
        row[...] = jnp.zeros_like(row)
        row[0:1, :length] = values[...].astype(F32)
        place = 0 if length == LANES else (me_ref[0] % 4) * length
        turned = pltpu.roll(row[:, : lines * LANES], place, 1)
        for part in range(lines):
            rows[line + part : line + part + 1, :] = turned[0:1, part * LANES : (part + 1) * LANES]
        line += lines
    joined[:, 4 * D : 4 * D + LANES] = rows[...].astype(BF)
    joined[:, 4 * D + LANES :] = jnp.zeros((BLOCKS, LANES), BF)


def prepare(me, shard, second, small):
    small = [values.reshape(1, -1) for values in small]
    return pallas(
        prepare_kernel,
        in_specs=[SMEM, fixed(*shard.shape), fixed(*second.shape)] + [fixed(*values.shape) for values in small],
        out_specs=fixed(BLOCKS, 4 * D + 2 * LANES),
        out_shape=jax.ShapeDtypeStruct((BLOCKS, 4 * D + 2 * LANES), BF),
        scratch_shapes=[pltpu.VMEM((8, 3 * LANES), F32), pltpu.VMEM((BLOCKS, LANES), F32)],
        cost_estimate=cost(2),
        name="prepare",
        near="all",
        far_in=range(1, 11),
        operands=(me, shard, second, *small),
    )


def table_of(lines, table):
    row = line = 0
    values = lines.astype(F32)
    table[...] = jnp.zeros_like(table)
    for count, length in zip(LINES, LENGTHS):
        spans = []
        for group in range(BLOCKS // 4):
            blocks = [(4 * group + member) * BLOCKS + line for member in range(4)]
            if length == LANES:
                spans += [values[block : block + 1, :] for block in blocks]
            else:
                for part in range(count):
                    spans.append(sum((values[block + part : block + part + 1, :] for block in blocks[1:]), values[blocks[0] + part : blocks[0] + part + 1, :]))
        for begin in range(0, len(spans), D // LANES):
            table[row : row + 1, :] = jnp.concatenate(spans[begin : begin + D // LANES], 1)
            row += 1
        line += count


def project_kernel(layout_of, me_ref, tokens, cosine, sine, *rest):
    refs = rest[: len(layout_of)]
    normed_kept, normed_sent, qkv_out, table, weight, lines, normed_out, turned, sem, lines_sem = rest[len(layout_of) :]
    step = pl.program_id(0)

    @pl.when(step == 0)
    def _():
        fetch(me_ref[0], layout_of, refs, (4 * D, 4 * D + LANES), lines, lines_sem)
        fetch(me_ref[0], layout_of, refs, (0, 3 * D), weight, sem)
        arrive(lines, lines_sem)
        table_of(lines[...], table)
        gain, shift = table[GAIN_ONE : GAIN_ONE + 1, :], table[SHIFT_ONE : SHIFT_ONE + 1, :]
        for begin in range(0, tokens.shape[0], ROWS):
            part = slice(begin, begin + ROWS)
            unit, _ = normed(tokens[part, :].astype(F32))
            normed_out[part, :] = (unit * gain + shift).astype(BF)
        turn_out(me_ref[0], normed_out[...], normed_kept, normed_sent, turned)
        arrive(weight, sem)

    column = pl.multiple_of(step * WIDE_TILE, WIDE_TILE)
    heads_tiles = D // WIDE_TILE
    bias = table[pl.ds(QKV_B + step // heads_tiles, 1), pl.ds(pl.multiple_of(step % heads_tiles * WIDE_TILE, WIDE_TILE), WIDE_TILE)]

    @pl.when(step < 2 * heads_tiles)
    def _():
        scale = jnp.where(step < heads_tiles, HEAD**-0.5, 1.0).astype(F32)
        for begin in range(0, tokens.shape[0], ROWS):
            part = slice(begin, begin + ROWS)
            product = nn(normed_out[part, :], weight[:, pl.ds(column, WIDE_TILE)]) + bias
            turned = product * wide(cosine[part, :], WIDE_TILE) + partner(product) * wide(sine[part, :], WIDE_TILE)
            qkv_out[part, :] = (turned * scale).astype(BF)

    @pl.when(step >= 2 * heads_tiles)
    def _():
        product = nn(normed_out[...], weight[:, pl.ds(column, WIDE_TILE)]) + bias
        qkv_out[...] = product.astype(BF)


def project(me, tokens, cosine, sine, pieces, after=()):
    count = tokens.shape[0]
    layout_of = describe(pieces)
    return pallas(
        functools.partial(project_kernel, layout_of),
        grid=(3 * D // WIDE_TILE,),
        in_specs=[SMEM, fixed(count, D), fixed(count, LANES), fixed(count, LANES)] + [ANY] * len(pieces),
        out_specs=[fixed(D // 2, count)] * 2 + [pl.BlockSpec((count, WIDE_TILE), lambda step: (0, step)), fixed(TABLE, D)],
        out_shape=[jax.ShapeDtypeStruct((D // 2, count), BF)] * 2
        + [jax.ShapeDtypeStruct((count, 3 * D), BF), jax.ShapeDtypeStruct((TABLE, D), F32)],
        scratch_shapes=[
            pltpu.VMEM((D, 3 * D), BF),
            pltpu.VMEM((D, LANES), BF),
            pltpu.VMEM((count, D), BF),
            pltpu.VMEM((D, count), BF),
            pltpu.SemaphoreType.DMA,
            pltpu.SemaphoreType.DMA,
        ],
        cost_estimate=cost(16 / 4),
        name="project",
        far_in=(1, *range(4, 4 + len(pieces))),
        near=(1, 3),
        operands=(me, tokens, cosine, sine, *[array for _, _, array in pieces]),
        after=after,
    )


def line_of(table, line):
    return table[line : line + 1, :]


def branch_kernel(layout_of, me_ref, mixed, tokens, table, *rest):
    refs = rest[: len(layout_of)]
    resid, normed_two, normed_kept, normed_sent, mixed_kept, mixed_sent, weight, turned, sem = rest[len(layout_of) :]

    @pl.when(pl.program_id(0) == 0)
    def _():
        fetch(me_ref[0], layout_of, refs, (3 * D, 4 * D), weight, sem)
        arrive(weight, sem)

    value = tokens[...].astype(F32) + (nn(mixed[...], weight[...]) + line_of(table, OUT_B))
    resid[...] = value
    unit, _ = normed(value)
    low = (unit * line_of(table, GAIN_TWO) + line_of(table, SHIFT_TWO)).astype(BF)
    normed_two[...] = low
    turn_out(me_ref[0], low, normed_kept, normed_sent, turned)
    turn_out(me_ref[0], mixed[...], mixed_kept, mixed_sent, turned)


def branch(me, mixed, tokens, table, pieces, after=()):
    count = tokens.shape[0]
    layout_of = describe(pieces)
    rows = pl.BlockSpec((ROWS, D), lambda step: (step, 0))
    return pallas(
        functools.partial(branch_kernel, layout_of),
        grid=(count // ROWS,),
        in_specs=[SMEM, rows, rows, fixed(TABLE, D)] + [ANY] * len(pieces),
        out_specs=[rows, rows] + [pl.BlockSpec((D // 2, ROWS), lambda step: (0, step))] * 4,
        out_shape=[jax.ShapeDtypeStruct((count, D), F32), jax.ShapeDtypeStruct((count, D), BF)]
        + [jax.ShapeDtypeStruct((D // 2, count), BF)] * 4,
        scratch_shapes=[pltpu.VMEM((D, D), BF), pltpu.VMEM((D, ROWS), BF), pltpu.SemaphoreType.DMA],
        cost_estimate=cost(12 / 4),
        name="branch",
        far_in=(1, 2, *range(4, 4 + len(pieces))),
        near=(1, 3, 5),
            operands=(me, mixed, tokens, table, *[array for _, _, array in pieces],),
        after=after,
    )


def gelu_parts(value):
    decay = jnp.exp(-0.5 * value * value)
    point = 1.0 / (1.0 + (0.3275911 * 2.0**-0.5) * jnp.abs(value))
    series = 0.5 * 1.061405429
    for factor in (-1.453152027, 1.421413741, -0.284496736, 0.254829592):
        series = series * point + 0.5 * factor
    tail = series * point * decay
    return jnp.where(value >= 0, 1.0 - tail, tail), decay * (2.0 * np.pi) ** -0.5


def up_kernel(layout_of, me_ref, normed_two, table, *rest):
    refs = rest[: len(layout_of)]
    activ, slope, activ_sent, weight, sem = rest[len(layout_of) :]
    step = pl.program_id(0)

    @pl.when(step == 0)
    def _():
        fetch(me_ref[0], layout_of, refs, (0, FF), weight, sem)
        arrive(weight, sem)

    column = pl.multiple_of(step * TILE, TILE)
    tiles = D // TILE
    bias = table[pl.ds(UP_B + step // tiles, 1), pl.ds(pl.multiple_of(step % tiles * TILE, TILE), TILE)]
    rows = FF // BLOCKS
    odd = (me_ref[0] & 1) == 1
    parts = [slice(begin, begin + UP_ROWS) for begin in range(0, normed_two.shape[0], UP_ROWS)]

    def product(part):
        return nn(normed_two[part, :], weight[:, pl.ds(column, TILE)])

    ahead = product(parts[0])
    for number, part in enumerate(parts):
        value = ahead + bias
        if number + 1 < len(parts):
            ahead = product(parts[number + 1])
        share, density = gelu_parts(value)
        low = (value * share).astype(BF)
        activ[part, :] = low
        slope[part, :] = (share + value * density).astype(BF)
        pairs = [low[:, begin : begin + 2 * rows] for begin in range(0, TILE, 2 * rows)]
        sent = [jnp.where(odd, pair[:, :rows], pair[:, rows:]) for pair in pairs]
        activ_sent[part, :] = jnp.concatenate(sent, 1)


def up(me, normed_two, table, pieces, after=()):
    count = normed_two.shape[0]
    layout_of = describe(pieces)
    tile = pl.BlockSpec((count, TILE), lambda step: (0, step))
    return pallas(
        functools.partial(up_kernel, layout_of),
        grid=(FF // TILE,),
        in_specs=[SMEM, fixed(count, D), fixed(TABLE, D)] + [ANY] * len(pieces),
        out_specs=[tile, tile, pl.BlockSpec((count, TILE // 2), lambda step: (0, step))],
        out_shape=[jax.ShapeDtypeStruct((count, FF), BF)] * 2 + [jax.ShapeDtypeStruct((count, FF // 2), BF)],
        scratch_shapes=[pltpu.VMEM((D, FF), BF), pltpu.SemaphoreType.DMA],
        cost_estimate=cost(35 / 4),
        name="up",
        far_in=range(3, 3 + len(pieces)),
            operands=(me, normed_two, table, *[array for _, _, array in pieces],),
        after=after,
    )


def pre_kernel(slope, cotangent, weight, grad_pre, grad_bias):
    sums = jnp.zeros((1, WIDE_TILE), F32)
    for begin in range(0, slope.shape[0], ROWS):
        part = slice(begin, begin + ROWS)
        back = (nt(cotangent[part, :], weight[...]) * slope[part, :].astype(F32)).astype(BF)
        grad_pre[part, :] = back
        sums += jnp.sum(back.astype(F32), axis=0, keepdims=True)
    grad_bias[...] = sums


def pre(slope, cotangent, weight, after=()):
    count = slope.shape[0]
    tile = pl.BlockSpec((count, WIDE_TILE), lambda step: (0, step))
    return pallas(
        pre_kernel,
        grid=(FF // WIDE_TILE,),
        in_specs=[tile, fixed(count, D), pl.BlockSpec((WIDE_TILE, D), lambda step: (step, 0))],
        out_specs=[tile, pl.BlockSpec((1, WIDE_TILE), lambda step: (0, step))],
        out_shape=[jax.ShapeDtypeStruct((count, FF), BF), jax.ShapeDtypeStruct((1, FF), F32)],
        cost_estimate=cost(15),
        name="pre",
        far_in=(0, 1, 2),
        operands=(slope, cotangent, weight),
        after=after,
    )


def output_kernel(activ, resid, table, weight, *rest):
    output, total = rest[-2:]
    step = pl.program_id(0)

    @pl.when(step == 0)
    def _():
        total[...] = resid[...] + line_of(table, DOWN_B)

    total[...] += nn(activ[...], weight[...])

    @pl.when(step == pl.num_programs(0) - 1)
    def _():
        output[...] = total[...].astype(BF)


def output_rows(activ, resid, table, weight, part, parts, before=(), after=()):
    count = activ.shape[0]
    rows = count // parts
    wide_tile = 2 * WIDE_TILE
    mine = pl.BlockSpec((rows, D), lambda step: (part, 0))
    return pallas(
        output_kernel,
        grid=(FF // wide_tile,),
        in_specs=[
            pl.BlockSpec((rows, wide_tile), lambda step: (part, step)),
            mine,
            fixed(TABLE, D),
            pl.BlockSpec((wide_tile, D), lambda step: (step, 0)),
        ]
        + [ANY] * len(before),
        out_specs=mine,
        out_shape=jax.ShapeDtypeStruct((count, D), BF),
        scratch_shapes=[pltpu.VMEM((rows, D), F32)],
        input_output_aliases={4 + place: place for place in range(len(before))},
        cost_estimate=cost(16 // parts),
        name="output",
        far_in=(0, 1, 3),
        operands=(activ, resid, table, weight, *before),
        after=after,
    )


def tn(left, right):
    return lax.dot_general(left, right, (((0,), (0,)), ((), ())), preferred_element_type=F32)


def outer_rows_kernel(me_ref, *refs):
    own, other, (right, right_other), sides, grad_bias = refs[:4], refs[4:8], refs[8:10], refs[10:14], refs[14]
    step = pl.program_id(0)
    half = right.shape[1] // 2

    def group(blocks):
        return jnp.concatenate([ref[...] for ref in blocks], 1)

    product = tn(group(own), right[...]) + tn(group(other), right_other[...])
    for side in range(2):
        bit = (step >> (1 - side)) & 1
        values = product[:, side * half : (side + 1) * half]

        @pl.when(bit == 0)
        def _():
            sides[2 * side][...] = values

        @pl.when(bit == 1)
        def _():
            sides[2 * side + 1][...] = values.astype(BF)

    @pl.when(step == 0)
    def _():
        grad_bias[...] = jnp.sum(right[...].astype(F32), axis=0, keepdims=True)


def outer_rows(me, left, left_other, right, right_other, after=()):
    count, size = left_other.shape
    width = right.shape[1]
    rows = FF // BLOCKS
    block = (4 * rows, width // 2)
    own = [
        pl.BlockSpec((count, rows), lambda step, me, z=z: (0, me[0] ^ (2 * (4 * step + z)))) for z in range(4)
    ]
    other = [
        pl.BlockSpec((count, rows), lambda step, me, z=z: (0, (me[0] >> 1) ^ (4 * step + z))) for z in range(4)
    ]
    return pallas(
        outer_rows_kernel,
        grid=(4,),
        prefetch=1,
        in_specs=own + other + [fixed(count, width)] * 2,
        out_specs=[
            pl.BlockSpec(block, lambda step, me: (jnp.minimum(step, 1), 0)),
            pl.BlockSpec(block, lambda step, me: (jnp.maximum(step - 2, 0), 0)),
            pl.BlockSpec(block, lambda step, me: (step // 2, 0)),
            pl.BlockSpec(block, lambda step, me: (step // 2, 0)),
            fixed(1, width),
        ],
        out_shape=[jax.ShapeDtypeStruct((size // 2, width // 2), kind) for kind in (F32, BF, F32, BF)]
        + [jax.ShapeDtypeStruct((1, width), F32)],
        cost_estimate=cost(16),
        name="outer_rows",
        far_in=range(1, 11),
        near=(0, 1, 2, 3),
        operands=(me, *[left] * 4, *[left_other] * 4, right, right_other),
        after=after,
    )


def outer_kernel(tiles, parts, *refs):
    sides, grad_bias = refs[-5:-1], refs[-1]
    step = pl.program_id(0)
    for begin, end, *places in parts:
        left, left_other, right, right_other = [refs[place] for place in places]
        rows = left.shape[0] // (BLOCKS // 2)

        @pl.when((step >= begin) & (step < end))
        def _():
            product = nn(left[...], right[...]) + nn(left_other[...], right_other[...])
            for side in range(2):

                @pl.when((step >= tiles // 2) == bool(side))
                def _():
                    for which, positions in enumerate(parted(list(range(BLOCKS // 2)), UPPER[side][0] >> 1)):
                        target = sides[2 * side + which]
                        for position, first, length in runs_of(positions):
                            part = product[first * rows : (first + length) * rows, :]
                            target[position * rows : (position + length) * rows, :] = part.astype(target.dtype)

            grad_bias[...] = jnp.sum(right[...].astype(F32), axis=0, keepdims=True)


def outer(sets, tile_width, after=(), free=()):
    size, count = sets[0][0].shape
    parts, tiles, operands, in_specs = [], 0, [], []

    def take(array, spec):
        for place, known in enumerate(operands):
            if known is array:
                return place
        operands.append(array)
        in_specs.append(spec)
        return len(operands) - 1

    for left, left_other, right, right_other in sets:
        begin, end = tiles, tiles + right.shape[1] // tile_width

        def tile_of(step, begin=begin, end=end):
            return 0, jnp.clip(step - begin, 0, end - begin - 1)

        spec = pl.BlockSpec((count, tile_width), tile_of)
        places = [take(each, fixed(size, count)) for each in (left, left_other)]
        places += [take(each, spec) for each in (right, right_other)]
        parts.append((begin, end, *places))
        tiles = end

    width = tiles * tile_width
    block = (size // 2, tile_width)
    firsts = pl.BlockSpec(block, lambda step: (0, jnp.minimum(step, tiles // 2 - 1)))
    seconds = pl.BlockSpec(block, lambda step: (0, jnp.maximum(step - tiles // 2, 0)))
    return pallas(
        functools.partial(outer_kernel, tiles, parts),
        grid=(tiles,),
        in_specs=in_specs,
        out_specs=[firsts, firsts, seconds, seconds, pl.BlockSpec((1, tile_width), lambda step: (0, step))],
        out_shape=[jax.ShapeDtypeStruct((size // 2, width // 2), kind) for kind in (F32, BF, F32, BF)]
        + [jax.ShapeDtypeStruct((1, width), F32)],
        cost_estimate=cost(4 * count * size * width / 0.55e9),
        name="outer",
        far_in=[place for place, array in enumerate(operands) if not any(array is each for each in free)],
        near=(0, 1, 2, 3),
        operands=tuple(operands),
        after=after,
    )


def branch_back_kernel(layout_of, out_layout, me_ref, grad_pre, resid, cotangent, table, *rest):
    refs, rest = rest[: len(layout_of)], rest[len(layout_of) :]
    out_refs, rest = rest[: len(out_layout)], rest[len(out_layout) :]
    grad_resid, grad_branch, grad_mixed, grad_gain, grad_shift, grad_bias, up_weight, out_weight, up_sem, out_sem = rest

    @pl.when(pl.program_id(0) == 0)
    def _():
        fetch(me_ref[0], layout_of, refs, (0, FF), up_weight, up_sem)
        fetch(me_ref[0], out_layout, out_refs, (3 * D, 4 * D), out_weight, out_sem)
        grad_gain[...] = jnp.zeros_like(grad_gain)
        grad_shift[...] = jnp.zeros_like(grad_shift)
        grad_bias[...] = jnp.zeros_like(grad_bias)
        arrive(up_weight, up_sem)

    upstream = nt(grad_pre[...], up_weight[...])
    back, gain_part, shift_part = norm_back(resid[...], line_of(table, GAIN_TWO), upstream)
    total = cotangent[...].astype(F32) + back
    low = total.astype(BF)
    grad_resid[...] = total
    grad_branch[...] = low
    grad_gain[...] += gain_part
    grad_shift[...] += shift_part
    grad_bias[...] += jnp.sum(low.astype(F32), axis=0, keepdims=True)

    @pl.when(pl.program_id(0) == 0)
    def _():
        arrive(out_weight, out_sem)

    grad_mixed[...] = nt(low, out_weight[...]).astype(BF)


def branch_back(me, grad_pre, resid, cotangent, table, pieces, out_pieces, after=()):
    count = resid.shape[0]
    layout_of, out_layout = describe(pieces), describe(out_pieces)
    rows = pl.BlockSpec((ROWS, D), lambda step: (step, 0))
    vector = jax.ShapeDtypeStruct((1, D), F32)
    return pallas(
        functools.partial(branch_back_kernel, layout_of, out_layout),
        grid=(count // ROWS,),
        in_specs=[SMEM, pl.BlockSpec((ROWS, FF), lambda step: (step, 0)), rows, rows, fixed(TABLE, D)]
        + [ANY] * (len(pieces) + len(out_pieces)),
        out_specs=[rows, rows, rows] + [fixed(1, D)] * 3,
        out_shape=[
            jax.ShapeDtypeStruct((count, D), F32),
            jax.ShapeDtypeStruct((count, D), BF),
            jax.ShapeDtypeStruct((count, D), BF),
            vector,
            vector,
            vector,
        ],
        scratch_shapes=[
            pltpu.VMEM((D, FF), BF),
            pltpu.VMEM((D, D), BF),
            pltpu.SemaphoreType.DMA,
            pltpu.SemaphoreType.DMA,
        ],
        cost_estimate=cost(21),
        name="branch_back",
        far_in=(1, 2, 3, *range(5, 5 + len(pieces) + len(out_pieces))),
        near=(1, 2),
            operands=(me, grad_pre, resid, cotangent, table, *[array for _, _, array in (*pieces, *out_pieces)],),
        after=after,
    )


def tokens_back_kernel(layout_of, chunks, me_ref, *rest):
    grads, rest = rest[:chunks], rest[chunks:]
    tokens, grad_resid, table, out_bias, up_bias, down_bias, gain_two, shift_two = rest[:8]
    refs = rest[8 : 8 + len(layout_of)]
    grad_tokens, grad_table, weight, sem = rest[8 + len(layout_of) :]

    @pl.when(pl.program_id(0) == 0)
    def _():
        fetch(me_ref[0], layout_of, refs, (0, 3 * D), weight, sem)
        grad_table[...] = jnp.zeros_like(grad_table)
        for ref, row in ((out_bias, OUT_B), (down_bias, DOWN_B), (gain_two, GAIN_TWO), (shift_two, SHIFT_TWO)):
            grad_table[row : row + 1, :] = ref[...]
        for part in range(FF // D):
            grad_table[UP_B + part : UP_B + part + 1, :] = up_bias[:, part * D : (part + 1) * D]
        arrive(weight, sem)

    quads = [(ref, begin) for ref in grads for begin in range(0, ref.shape[1], 3 * QUAD)]
    ordered = jnp.concatenate(
        [ref[:, begin + part * QUAD : begin + (part + 1) * QUAD] for part in range(3) for ref, begin in quads], 1
    )
    for part in range(3):
        sums = jnp.sum(ordered[:, part * D : (part + 1) * D].astype(F32), axis=0, keepdims=True)
        grad_table[QKV_B + part : QKV_B + part + 1, :] += sums
    back, gain_part, shift_part = norm_back(
        tokens[...].astype(F32), line_of(table, GAIN_ONE), nt(ordered, weight[...])
    )
    grad_tokens[...] = (grad_resid[...] + back).astype(BF)
    grad_table[GAIN_ONE : GAIN_ONE + 1, :] += gain_part
    grad_table[SHIFT_ONE : SHIFT_ONE + 1, :] += shift_part


def tokens_back(me, grads, tokens, grad_resid, table, biases, pieces, after=()):
    count = tokens.shape[0]
    layout_of = describe(pieces)
    rows = pl.BlockSpec((ROWS, D), lambda step: (step, 0))
    return pallas(
        functools.partial(tokens_back_kernel, layout_of, len(grads)),
        grid=(count // ROWS,),
        in_specs=[SMEM]
        + [pl.BlockSpec((ROWS, part.shape[1]), lambda step: (step, 0)) for part in grads]
        + [rows, rows, fixed(TABLE, D)]
        + [fixed(*part.shape) for part in biases]
        + [ANY] * len(pieces),
        out_specs=[rows, fixed(TABLE, D)],
        out_shape=[jax.ShapeDtypeStruct((count, D), BF), jax.ShapeDtypeStruct((TABLE, D), F32)],
        scratch_shapes=[pltpu.VMEM((D, 3 * D), BF), pltpu.SemaphoreType.DMA],
        cost_estimate=cost(15),
        name="tokens_back",
        far_in=range(len(grads) + 1, len(grads) + 3),
        operands=(me, *grads, tokens, grad_resid, table, *biases, *[array for _, _, array in pieces]),
        after=after,
    )


def finish_kernel(lengths, terms, number, *refs):
    weights, sums, outs = refs[:8], refs[8 : 8 + terms], refs[8 + terms :]
    for chunk in range(2):
        arrived = weights[4 * chunk : 4 * chunk + 4]
        for half in range(2):
            for part in range(3):
                source = slice((3 * half + part) * QUAD, (3 * half + part + 1) * QUAD)
                target = part * D + (2 * chunk + half) * QUAD
                total = arrived[0][:, source]
                for ref in arrived[1:]:
                    total = total + ref[:, source].astype(F32)
                outs[0][:, target : target + QUAD] = total
    row = 0
    for place, (length, lines) in enumerate(lengths):
        place_in = number[0] * length
        wide_row = jnp.concatenate(
            [sum(line_of(ref, row + line) for ref in sums) for line in range(lines)], 1
        )
        wide_row = jnp.broadcast_to(wide_row, (8, lines * D))
        turned = pltpu.roll(wide_row, lines * D - place_in, 1)
        outs[1 + place][...] = turned[0:1, :length]
        row += lines


def finish(number, weights, total, sizes, count, after):
    lengths = [(size // count, size // D) for size in sizes]
    rows = weights[0].shape[0]
    return pallas(
        functools.partial(finish_kernel, lengths, len(total)),
        in_specs=[SMEM] + [fixed(*array.shape) for array in (*weights, *total)],
        out_specs=[fixed(rows, 3 * D)] + [fixed(1, length) for length, _ in lengths],
        out_shape=[jax.ShapeDtypeStruct((rows, 3 * D), F32)]
        + [jax.ShapeDtypeStruct((1, length), F32) for length, _ in lengths],
        cost_estimate=cost(3),
        name="finish",
        near="all",
        operands=(number, *weights, *total),
        after=after,
    )


def key_runs(positions, frames, patches):
    first, last = positions, positions + 1
    start = jnp.int32(0)
    for slot in range(frames.shape[1]):
        width = patches[0, slot] + 2
        size = frames[0, slot] * width
        offset = positions - start
        inside = (offset >= 0) & (offset < size)
        end = start + width + jnp.where(offset >= width, width, 0) + jnp.where(offset >= 2 * width, width, 0)
        first = jnp.where(inside, start, first)
        last = jnp.where(inside, end, last)
        start = start + size
    return first, last


def fill_mask(frames, patches, mask, runs):
    count = mask.shape[0]
    first, last = key_runs(lax.broadcasted_iota(jnp.int32, (1, count), 1), frames, patches)
    keys = lax.broadcasted_iota(jnp.int32, (count, count), 0)
    mask[...] = jnp.where((keys >= first) & (keys < last), 0.0, MASKED)
    for block in range(count // BQ):
        part = slice(block * BQ, (block + 1) * BQ)
        begin = jnp.min(first[:, part]) // BK
        needed = (jnp.max(last[:, part]) + (BK - 1)) // BK - begin
        length = jnp.int32(LENGTHS_OF_RUNS[-1])
        for size in LENGTHS_OF_RUNS[-2::-1]:
            length = jnp.where(needed <= size, size, length)
        runs[0, block] = jnp.minimum(begin, count // BK - length)
        runs[1, block] = length


def each_block(count, runs, work):
    @pl.loop(0, count // BQ)
    def _(block):
        for size in LENGTHS_OF_RUNS:

            @pl.when(runs[1, block] == size)
            def _():
                work(pl.multiple_of(block * BQ, BQ), pl.multiple_of(runs[0, block] * BK, BK), size * BK)


def pair_of(head):
    return slice(head // 2 * LANES, (head // 2 + 1) * LANES)


def one_head(pair_values, head):
    lane = lax.broadcasted_iota(jnp.int32, pair_values.shape, 1)
    return jnp.where(lane // HEAD == head, pair_values, jnp.zeros_like(pair_values))


def attend_kernel(frames, patches, queries, keys, values, *rest):
    mixed, log_totals, mask, turned, runs = rest[-5:]
    count = queries.shape[0]

    @pl.when(pl.program_id(0) == 0)
    def _():
        fill_mask(frames, patches, mask, runs)

    turned[...] = values[...].T

    heads = queries.shape[1] // HEAD

    def work(row, key, size):
        block, span = pl.ds(row, BQ), pl.ds(key, size)
        bias = mask[span, block]
        scores = [
            nt(keys[span, pair_of(head)], one_head(queries[block, pair_of(head)], head % 2)) + bias
            for head in range(heads)
        ]
        results = []
        for head in range(heads):
            highest = jnp.max(scores[head], axis=0, keepdims=True)
            expo = jnp.exp(scores[head] - highest)
            totals = jnp.sum(expo, axis=0, keepdims=True)
            result = nn(turned[head * HEAD : (head + 1) * HEAD, span], expo.astype(BF))
            results.append(result * (1.0 / totals))
            log_totals[head : head + 1, block] = highest + jnp.log(totals)
        mixed[block, :] = jnp.concatenate(results, 0).T.astype(BF)

    each_block(count, runs, work)


QUAD = 4 * HEAD
QUADS = HEADS // 4


def attend(frames, patches, qkv, after=()):
    count = qkv.shape[0]
    groups, wide_block = QUADS // 2, 2 * QUAD

    def columns(part):
        return pl.BlockSpec((count, wide_block), lambda step: (0, part * groups + step))

    (mixed, log_totals), token = pallas(
        attend_kernel,
        grid=(groups,),
        in_specs=[SMEM, SMEM, columns(0), columns(1), columns(2)],
        out_specs=[columns(0), pl.BlockSpec((None, 8, count), lambda step: (step, 0, 0))],
        out_shape=[jax.ShapeDtypeStruct((count, D), BF), jax.ShapeDtypeStruct((groups, 8, count), F32)],
        scratch_shapes=[
            pltpu.VMEM((count, count), F32),
            pltpu.VMEM((wide_block, count), BF),
            pltpu.SMEM((2, count // BQ), jnp.int32),
        ],
        cost_estimate=cost(26 / 4),
        name="attend",
        far_in=(2, 3, 4),
        vmem=ATTEND_BYTES,
        operands=(frames, patches, qkv, qkv, qkv),
        after=after,
    )
    return (mixed, log_totals.reshape(QUADS, 4, count)), token


def attend_back_kernel(
    frames,
    patches,
    queries,
    keys,
    values,
    mixed,
    grads,
    log_totals,
    cosine,
    sine,
    grad_projected,
    mask,
    turned,
    grad_keys,
    grad_values,
    inner,
    runs,
):
    count = queries.shape[0]

    @pl.when(pl.program_id(0) == 0)
    def _():
        fill_mask(frames, patches, mask, runs)

    turned[...] = keys[...].T
    grad_keys[...] = jnp.zeros_like(grad_keys)
    grad_values[...] = jnp.zeros_like(grad_values)
    product = mixed[...].astype(F32) * grads[...].astype(F32)
    own = (
        lax.broadcasted_iota(jnp.int32, (8, QUAD), 1) // HEAD == lax.broadcasted_iota(jnp.int32, (8, QUAD), 0)
    ).astype(F32)
    inner[...] = lax.dot_general(
        own, product, (((1,), (1,)), ((), ())), precision=lax.Precision.HIGHEST, preferred_element_type=F32
    )

    def work(row, key, size):
        block, span = pl.ds(row, BQ), pl.ds(key, size)
        bias = mask[span, block]
        heads = range(QUAD // HEAD)
        rows = [one_head(queries[block, pair_of(head)], head % 2) for head in heads]
        rows_grads = [one_head(grads[block, pair_of(head)], head % 2) for head in heads]
        shares = [nt(keys[span, pair_of(head)], rows[head]) + bias for head in heads]
        changes = [nt(values[span, pair_of(head)], rows_grads[head]) for head in heads]
        probs, grad_scores, grad_rows = [], [], []
        for head in heads:
            share = jnp.exp(shares[head] - log_totals[head : head + 1, block])
            change = (share * (changes[head] - inner[head : head + 1, block])).astype(BF)
            grad_rows.append(nn(turned[head * HEAD : (head + 1) * HEAD, span], change))
            probs.append(share.astype(BF))
            grad_scores.append(change)
        for pair in range(QUAD // LANES):
            lanes, two = slice(pair * LANES, (pair + 1) * LANES), slice(2 * pair, 2 * pair + 2)
            grad_values[span, lanes] += nn(jnp.concatenate(probs[two], 1), jnp.concatenate(rows_grads[two], 0))
            grad_keys[span, lanes] += nn(jnp.concatenate(grad_scores[two], 1), jnp.concatenate(rows[two], 0))
        back = jnp.concatenate(grad_rows, 0).T * HEAD**-0.5
        back = back * wide(cosine[block, :], QUAD) - partner(back) * wide(sine[block, :], QUAD)
        grad_projected[block, :QUAD] = back.astype(BF)

    each_block(count, runs, work)
    back = grad_keys[...] * wide(cosine[...], QUAD) - partner(grad_keys[...]) * wide(sine[...], QUAD)
    grad_projected[:, QUAD : 2 * QUAD] = back.astype(BF)
    grad_projected[:, 2 * QUAD :] = grad_values[...].astype(BF)


def attend_back(frames, patches, qkv, mixed, grads, log_totals, cosine, sine, begin, quads, after=()):
    count = qkv.shape[0]

    def columns(part):
        return pl.BlockSpec((count, QUAD), lambda step: (0, part * QUADS + begin + step))

    return pallas(
        attend_back_kernel,
        grid=(quads,),
        in_specs=[
            SMEM,
            SMEM,
            columns(0),
            columns(1),
            columns(2),
            columns(0),
            columns(0),
            pl.BlockSpec((None, 4, count), lambda step: (begin + step, 0, 0)),
            fixed(count, LANES),
            fixed(count, LANES),
        ],
        out_specs=pl.BlockSpec((count, 3 * QUAD), lambda step: (0, step)),
        out_shape=jax.ShapeDtypeStruct((count, 3 * QUAD * quads), BF),
        scratch_shapes=[
            pltpu.VMEM((count, count), F32),
            pltpu.VMEM((QUAD, count), BF),
            pltpu.VMEM((count, QUAD), F32),
            pltpu.VMEM((count, QUAD), F32),
            pltpu.VMEM((8, count), F32),
            pltpu.SMEM((2, count // BQ), jnp.int32),
        ],
        cost_estimate=cost(15 * quads),
        name="attend_back",
        far_in=(2, 3, 4, 5),
        near=(0,),
            operands=(frames, patches, qkv, qkv, qkv, mixed, grads, log_totals, cosine, sine,),
        after=after,
    )


def positions_of(frames, patches):
    frame_tokens = patches + 2
    clip_tokens = frames * frame_tokens
    clip_starts = jnp.cumsum(clip_tokens) - clip_tokens
    positions = jnp.arange(TOK_DEV, dtype=jnp.int32)
    inside = (
        (positions[None, :] >= clip_starts[:, None])
        & (positions[None, :] < (clip_starts + clip_tokens)[:, None])
    ).astype(jnp.int32)
    begins = jnp.sum(inside * clip_starts[:, None], axis=0)
    widths = jnp.maximum(jnp.sum(inside * frame_tokens[:, None], axis=0), 1)
    clip_sides = jnp.where(patches == SIDE_SMALL * SIDE_SMALL, SIDE_SMALL, SIDE_LARGE).astype(jnp.int32)
    sides_rows = jnp.maximum(jnp.sum(inside * clip_sides[:, None], axis=0), 1)
    offsets = positions - begins
    frame_index = offsets // widths
    within = offsets % widths
    patch_index = jnp.maximum(within - 2, 0)
    row_index = jnp.where(within >= 2, patch_index // sides_rows, 0)
    col_index = jnp.where(within >= 2, patch_index % sides_rows, 0)
    return frame_index, row_index, col_index


def rotary_tables(places):
    pair_count = HEAD // 2
    time_pairs = pair_count // 3
    row_pairs = (pair_count - time_pairs) // 2
    pair_ranks = np.arange(pair_count)
    group_ids = np.where(pair_ranks < time_pairs, 0, np.where(pair_ranks < time_pairs + row_pairs, 1, 2))
    group_first = np.array([0, time_pairs, time_pairs + row_pairs])[group_ids]
    group_sizes = np.array([time_pairs, row_pairs, pair_count - time_pairs - row_pairs])[group_ids]
    rate_table = 10000.0 ** (-(pair_ranks - group_first) / group_sizes)
    angles = jnp.zeros((TOK_DEV, pair_count), F32)
    for group_id, place in enumerate(places):
        table = jnp.asarray(np.where(group_ids == group_id, rate_table, 0.0), F32)
        angles = angles + place.astype(F32)[:, None] * table[None, :]
    cosine, sine = jnp.cos(angles), jnp.sin(angles)
    return jnp.concatenate([cosine] * 4, 1), jnp.concatenate([-sine, sine] * 2, 1)


def by_side(made):
    return (made[0], made[1]), (made[2], made[3])


def local(
    count,
    tokens,
    clip_frames,
    clip_patches,
    qkv_weight,
    qkv_bias,
    out_weight,
    out_bias,
    up_weight,
    up_bias,
    down_weight,
    down_bias,
    norm1_gain,
    norm1_shift,
    norm2_gain,
    norm2_shift,
    cotangent,
):
    net = Net(count)
    me_ref = net.me.reshape(1)
    small = (qkv_bias, out_bias, up_bias, down_bias, norm1_gain, norm1_shift, norm2_gain, norm2_shift)
    sizes = [item.shape[0] * count for item in small]
    clips = (clip_frames, clip_patches)

    joined, _ = prepare(me_ref, net.widen(qkv_weight), net.widen(out_weight), [net.widen(values) for values in small])
    first = Gather(net, joined)
    middle_shard = net.widen(up_weight)
    cosine, sine = rotary_tables(positions_of(clip_frames[0], clip_patches[0]))

    def copy_of(shard):
        def put(relay):
            relay.put(relay.make(*shard.shape, BF), 0, 0, *shard.shape, [(shard, 0, 0)])

        return put

    made, _ = advance([first], extra=copy_of(middle_shard))
    middle = Gather(net, made[0])
    advance([first], after=[middle.held[0][1]])
    first.finish()
    made, token = advance([middle], after=first.arrivals(), extra=copy_of(down_weight))
    final = lax.all_gather(made[0], AXES, axis=0, tiled=True)
    (normed_kept, normed_sent, qkv, table), token = project(
        me_ref, tokens, cosine, sine, first.pieces, after=[token]
    )
    normed_other = net.swap(normed_sent, 1)
    _, token = advance([middle], after=[token])
    (mixed, log_totals), token = attend(*clips, qkv, after=[token])
    cotangent_other = net.swap(cotangent, 1)
    (resid, normed_two, two_kept, two_sent, mixed_kept, mixed_sent), token = branch(
        me_ref, mixed, tokens, table, [piece for piece in first.pieces if piece[0] == 1], after=[token]
    )
    token = middle.finish([token])
    two_other, mixed_other = net.swap(two_sent, 1), net.swap(mixed_sent, 1)
    (activ, slope, activ_sent), token = up(me_ref, normed_two, table, middle.pieces, after=[token])
    activ_other = net.swap(activ_sent, 1)
    (grad_pre, grad_up_bias), token = pre(slope, cotangent, final, after=[token])
    grad_pre_other = net.swap(grad_pre, 1)
    (*sides, grad_down_bias), token = outer_rows(
        me_ref, activ, activ_other, cotangent, cotangent_other, after=[token]
    )
    moving_down = Scatter(net, by_side(sides))
    (grad_resid, grad_branch, grad_mixed, grad_gain_two, grad_shift_two, grad_out_bias), token = branch_back(
        me_ref, grad_pre, resid, cotangent, table, middle.pieces, first.pieces[4:], after=[token]
    )
    grad_branch_other = net.swap(grad_branch, 1)
    _, token = advance([moving_down], after=[token])
    (*sides, _), token = outer(
        [(mixed_kept, mixed_other, grad_branch, grad_branch_other), (two_kept, two_other, grad_pre, grad_pre_other)],
        TILE,
        after=[token],
        free=(grad_branch, grad_branch_other),
    )
    moving_up = Scatter(net, by_side(sides), (D, FF))
    parts, others, moving_qkv = [], [], []

    def back(quad, token):
        part, token = attend_back(
            *clips, qkv, mixed, grad_mixed, log_totals, cosine, sine, quad, 1, after=[token]
        )
        parts.append(part)
        others.append(net.swap(part, 1))
        return token

    def weigh(quads, token):
        sets = [(normed_kept, normed_other, parts[quad], others[quad]) for quad in quads]
        (*sides, _), token = outer(sets, 3 * QUAD, after=[token], free=(*parts, *others))
        moving_qkv.append(Scatter(net, by_side(sides)))
        return token

    token = back(0, token)
    _, token = advance([moving_down], after=[token])
    token = back(1, token)
    _, token = advance([moving_up], after=[token])
    token = back(2, token)
    _, token = advance([moving_up, moving_down], after=[token])
    token = weigh([0, 1], token)
    token = back(3, token)
    _, token = advance([moving_qkv[0]], after=[token])
    (grad_tokens, grad_table), token = tokens_back(
        me_ref,
        parts,
        tokens,
        grad_resid,
        table,
        (grad_out_bias, grad_up_bias, grad_down_bias, grad_gain_two, grad_shift_two),
        first.pieces,
        after=[token],
    )
    total = Sum(net, grad_table)
    _, token = advance([moving_qkv[0], moving_up], after=[token])
    token = weigh([2, 3], token)
    _, token = advance([total], after=[token, *moving_qkv[0].held[1:]])
    output, token = output_rows(activ, resid, table, final, 0, 2, after=[token])
    _, token = advance([moving_qkv[1], total], after=[token])
    output, token = output_rows(activ, resid, table, final, 2, 4, [output], after=[token])
    _, token = advance([moving_qkv[1], total], after=[token])
    output, token = output_rows(activ, resid, table, final, 3, 4, [output], after=[token])
    (grad_qkv_weight, *own), _ = finish(
        net.number.reshape(1), (*moving_qkv[0].held, *moving_qkv[1].held), total.finish(), sizes, count, [token]
    )
    own = [values.reshape(-1) for values in own]
    return (
        output,
        grad_tokens,
        net.narrow(grad_qkv_weight),
        own[0],
        moving_up.result[0],
        own[1],
        moving_up.result[1],
        own[2],
        moving_down.result[0],
        own[3],
        own[4],
        own[5],
        own[6],
        own[7],
    )


def solution(mesh):
    count = mesh.shape["fsdp"] * mesh.shape["dp"]
    rows, vector = P(AXES, None), P(AXES)
    placed = (rows, rows, rows, rows, vector, rows, vector, rows, vector, rows, vector) + (vector,) * 4 + (rows,)
    given = (rows, rows, rows, vector, rows, vector, rows, vector, rows) + (vector,) * 5
    return jax.shard_map(
        functools.partial(local, count), mesh=mesh, in_specs=placed, out_specs=given, check_vma=False
    )
```
